128 devices in a mesh: gx: 16 (over y, x), gy: 8 (over z, core).
Axes of the slice: x: 4, y: 4, z: 4, core: 2. Of those that a mesh axis runs over, the one named last changes fastest.
Arguments:
- coarse_source: float32 [512, 8192], P('gx', 'gy'), may hold values from -6 to 6
- coarse_coefficient: float32 [512, 8192], P('gx', 'gy'), may hold values from 0.25 to 4
- coarse_start: float32 [512, 8192], P('gx', 'gy'), may hold values from -6 to 6
- fine_source: float32 [128, 32, 1024], P(('gx', 'gy')), may hold values from -6 to 6
- fine_coefficient: float32 [128, 32, 1024], P(('gx', 'gy')), may hold values from 0.25 to 4
- fine_start: float32 [128, 32, 1024], P(('gx', 'gy')), may hold values from -6 to 6
- fine_position: int32 [128], replicated, may hold values from 0 to 1023, as said below
- first_colour: int32 [3], replicated, may hold values from 0 to 1
Outputs:
- coarse_solution: float32 [512, 8192], P('gx', 'gy')
- fine_solution: float32 [128, 32, 1024], P(('gx', 'gy'))
The draws below stay inside these ranges and needn't reach their ends.
Inputs may be any that keep to these rules, and one draw needn't show every extreme that they name: `fine_position`: entry r is the box held by device r = gx index * 8 + gy index; its coarse device p // 8 has the same gy index as device r; only octants whose three bits sum to an even number occur, so no two boxes share a face; positions are distinct; in every gy index some coarse device lies under four boxes, and some box lies 16 // 2 gx indices away from its coarse device.
All inputs are finite; a program needn't handle non-finite values.
Results may differ from the reference program's by a relative error of at most 0.0003.
Values sent between devices are 32-bit elements; how exact they have to be, the bound alone decides.
A program may use at most 64 MiB of HBM per device.

```python
import math
import jax
import jax.numpy as jnp
from jax import lax

B = 32
SWEEPS = 4
NCX = 512
NCY = 256
FBOXES = 128
N_GX = 16
N_GY = 8


def draw_fine_position(key, part):
    octant_kinds = jnp.array([0, 3, 5, 6], dtype=jnp.int32)

    def one_row(row_number):
        row_key = jax.random.fold_in(jax.random.fold_in(key, 7), row_number)
        crowded_x = jax.random.randint(jax.random.fold_in(row_key, 1), (), 0, N_GX)
        labels = jnp.arange(4 * (N_GX - 1), dtype=jnp.int32)
        shuffled = jax.random.permutation(jax.random.fold_in(row_key, 2), labels)
        chosen = shuffled[:N_GX - 4]
        column = chosen // 4
        column = column + (column >= crowded_x).astype(jnp.int32)
        octant = octant_kinds[chosen % 4]
        others = (column * N_GY + row_number) * 8 + octant
        crowded = (crowded_x * N_GY + row_number) * 8 + octant_kinds
        positions = jnp.concatenate([others, crowded]).astype(jnp.int32)
        columns = positions // 8 // N_GY
        holders = jax.random.permutation(jax.random.fold_in(row_key, 3), jnp.arange(N_GX, dtype=jnp.int32)).astype(jnp.int32)
        pick = jax.random.randint(jax.random.fold_in(row_key, 4), (), 0, N_GX).astype(jnp.int32)
        wanted = ((columns[pick] + N_GX // 2) % N_GX).astype(jnp.int32)
        indices = jnp.arange(N_GX, dtype=jnp.int32)
        spot = jnp.sum(jnp.where(holders == wanted, indices, 0)).astype(jnp.int32)
        previous = holders[pick]
        holders = holders.at[spot].set(previous)
        holders = holders.at[pick].set(wanted)
        return jnp.zeros((N_GX,), jnp.int32).at[holders].set(positions)
    table_rows = jax.vmap(one_row)(jnp.arange(N_GY, dtype=jnp.int32))
    return table_rows.T.reshape(N_GX * N_GY).astype(jnp.int32)


def level_of(key, extent, cuts, low, high):
    loudness = 1.0
    for dim, shards_of in cuts:
        heights = jax.random.uniform(jax.random.fold_in(jax.random.fold_in(key, 6), dim), (shards_of,), jnp.float32, low / len(cuts), high / len(cuts))
        loudness = loudness * jnp.repeat(jnp.exp(heights), extent[dim] // shards_of).reshape((-1,) + (1,) * (len(extent) - 1 - dim))
    return loudness


def noise(rng, shape, width, most, pieces=(), kind=jnp.bfloat16):
    result = jax.random.normal(rng, shape, jnp.float32) * width
    if len(pieces) > 0:
        result = level_of(rng, shape, pieces, -0.22, 0.18) * result
    return jnp.clip(result, min=-most, max=most).astype(kind)


def setup_inputs(seed: int = 0) -> dict:
    arg_keys = jax.random.split(jax.random.key(seed), 9)
    coarse_source = noise(arg_keys[0], (NCX, NCY * B), 1.0, 6.0, ((0, 16), (1, 8)), jnp.float32)
    coarse_coefficient = jnp.clip(jnp.exp(math.log(4.0) - 2.7725887 * jax.random.uniform(arg_keys[1], (NCX, NCY * B), jnp.float32) ** level_of(arg_keys[1], (NCX, NCY * B), ((0, 16), (1, 8)), -0.2, 0.2)), 0.25, 4.0)
    coarse_start = noise(arg_keys[2], (NCX, NCY * B), 1.0, 6.0, ((0, 16), (1, 8)), jnp.float32)
    fine_source = noise(arg_keys[3], (FBOXES, B, B * B), 1.0, 6.0, ((0, 128),), jnp.float32)
    fine_coefficient = jnp.clip(jnp.exp(math.log(4.0) - 2.7725887 * jax.random.uniform(arg_keys[4], (FBOXES, B, B * B), jnp.float32) ** level_of(arg_keys[4], (FBOXES, B, B * B), ((0, 128),), -0.2, 0.2)), 0.25, 4.0)
    fine_start = noise(arg_keys[5], (FBOXES, B, B * B), 1.0, 6.0, ((0, 128),), jnp.float32)
    fine_position = draw_fine_position(jax.random.fold_in(arg_keys[8], 71), 0)
    first_colour = jax.random.randint(arg_keys[7], (3,), 0, 2).astype(jnp.int32)
    return {"coarse_source": coarse_source, "coarse_coefficient": coarse_coefficient, "coarse_start": coarse_start, "fine_source": fine_source, "fine_coefficient": fine_coefficient, "fine_start": fine_start, "fine_position": fine_position, "first_colour": first_colour}


def shifted(values, stride, before, beyond):
    column = lax.broadcasted_iota(jnp.int32, values.shape, 1) % stride
    blanks = jnp.zeros_like(values[:, :1])
    toward = jnp.concatenate([blanks, values[:, :-1]], axis=1)
    backward = jnp.concatenate([values[:, 1:], blanks], axis=1)
    behind = jnp.where(column == 0, before, toward)
    forward = jnp.where(column == stride - 1, beyond, backward)
    return behind, forward


def neighbours(values, borders, stride, before, beyond):
    x_before, x_beyond, y_before, y_beyond = borders
    x_minus = jnp.concatenate([x_before, values[:-1]], axis=0)
    x_plus = jnp.concatenate([values[1:], x_beyond], axis=0)
    y_minus = jnp.concatenate([y_before, values[:, :-stride]], axis=1)
    y_plus = jnp.concatenate([values[:, stride:], y_beyond], axis=1)
    z_minus, z_plus = shifted(values, stride, before, beyond)
    return (x_minus, x_plus, y_minus, y_plus, z_minus, z_plus)


def face_terms(coefficient, around):
    weights = tuple(0.5 * (coefficient + neighbour) for neighbour in around)
    diagonal = weights[0] + weights[1] + weights[2] + weights[3] + weights[4] + weights[5]
    return weights, diagonal


def coupling(weights, around):
    total = weights[0] * around[0]
    for number in range(1, 6):
        total = total + weights[number] * around[number]
    return total


def relaxed(values, source, coupled, diagonal, factor, parity, colour):
    fresh = (source + factor * coupled) / (factor * diagonal)
    return jnp.where(parity == colour, fresh, values)


def residual_of(values, source, weights, diagonal, around, factor):
    return source - factor * (diagonal * values - coupling(weights, around))


def parity_of(rows_count, breadth, stride):
    along_x = lax.broadcasted_iota(jnp.int32, (rows_count, breadth), 0)
    flattened = lax.broadcasted_iota(jnp.int32, (rows_count, breadth), 1)
    return (along_x + flattened // stride + flattened % stride) % 2


def coarsen(values, stride):
    rows_count = values.shape[0]
    planes = values.shape[1] // stride
    volume = values.reshape(rows_count // 2, 2, planes // 2, 2, stride // 2, 2)
    summed = volume[:, 0] + volume[:, 1]
    summed = summed[:, :, 0] + summed[:, :, 1]
    summed = summed[..., 0] + summed[..., 1]
    return (0.125 * summed).reshape(rows_count // 2, (planes // 2) * (stride // 2))


def refine(values, stride):
    rows_count = values.shape[0]
    planes = values.shape[1] // stride
    volume = values.reshape(rows_count, planes, stride)
    volume = jnp.repeat(jnp.repeat(jnp.repeat(volume, 2, axis=0), 2, axis=1), 2, axis=2)
    return volume.reshape(2 * rows_count, 4 * planes * stride)


def enlarge(surface):
    return jnp.repeat(jnp.repeat(surface, 2, axis=0), 2, axis=1)


def zero_borders(values, stride):
    blank_row = jnp.zeros_like(values[:1])
    blank_side = jnp.zeros_like(values[:, :stride])
    return (blank_row, blank_row, blank_side, blank_side)


def fine_sweep(surfaces, source, coefficient, start, leading, parity, box_edge):
    widened = [enlarge(surface) for surface in surfaces]
    ghosts = (widened[0].reshape(1, box_edge * box_edge), widened[1].reshape(1, box_edge * box_edge), widened[2], widened[3])
    ghost_before = jnp.repeat(widened[4], box_edge, axis=1)
    ghost_beyond = jnp.repeat(widened[5], box_edge, axis=1)
    inside = (coefficient[:1], coefficient[-1:], coefficient[:, :box_edge], coefficient[:, -box_edge:])
    weights, diagonal = face_terms(coefficient, neighbours(coefficient, inside, box_edge, coefficient, coefficient))
    values = start
    for colour in (leading, 1 - leading):
        coupled = coupling(weights, neighbours(values, ghosts, box_edge, ghost_before, ghost_beyond))
        values = relaxed(values, source, coupled, diagonal, 4.0, parity, colour)
    remainder = residual_of(values, source, weights, diagonal, neighbours(values, ghosts, box_edge, ghost_before, ghost_beyond), 4.0)
    return values, coarsen(remainder, box_edge)


def bottom_sweeps(source, weights, diagonal, parity, leading, borders_of, half_edge):
    values = jnp.zeros_like(source)
    started = False
    for passage in range(SWEEPS):
        for colour in (leading, 1 - leading):
            if started:
                coupled = coupling(weights, neighbours(values, borders_of(values), half_edge, 0.0, 0.0))
            else:
                coupled = jnp.zeros_like(values)
            started = True
            values = relaxed(values, source, coupled, diagonal, 0.25, parity, colour)
    return values


def reference(coarse_source, coarse_coefficient, coarse_start, fine_source, fine_coefficient, fine_start, fine_position, first_colour):
    box_edge = B
    half_edge = B // 2
    outside = zero_borders(coarse_start, box_edge)
    parity_coarse = parity_of(NCX, NCY * box_edge, box_edge)
    weights_c, diagonal_c = face_terms(coarse_coefficient, neighbours(coarse_coefficient, outside, box_edge, 0.0, 0.0))
    resid_c = residual_of(coarse_start, coarse_source, weights_c, diagonal_c, neighbours(coarse_start, outside, box_edge, 0.0, 0.0), 1.0)
    padded_start = jnp.pad(coarse_start.reshape(NCX, NCY, box_edge), 1)
    parity_fine = parity_of(box_edge, box_edge * box_edge, box_edge)

    def box_anchor(position):
        holder = position // 8
        octant = position % 8
        corner_x = (holder // N_GY) * box_edge + (octant // 4) * half_edge
        corner_y = (holder % N_GY) * box_edge + ((octant // 2) % 2) * half_edge
        corner_z = (octant % 2) * half_edge
        return (corner_x.astype(jnp.int32), corner_y.astype(jnp.int32), corner_z.astype(jnp.int32))

    def smooth_box(operands):
        position, source, coefficient, start = operands
        region = lax.dynamic_slice(padded_start, box_anchor(position), (half_edge + 2, half_edge + 2, half_edge + 2))
        surfaces = [region[0, 1:-1, 1:-1], region[half_edge + 1, 1:-1, 1:-1], region[1:-1, 0, 1:-1], region[1:-1, half_edge + 1, 1:-1], region[1:-1, 1:-1, 0], region[1:-1, 1:-1, half_edge + 1]]
        return fine_sweep(surfaces, source, coefficient, start, first_colour[0], parity_fine, box_edge)

    smoothed, restricted = lax.map(smooth_box, (fine_position, fine_source, fine_coefficient, fine_start))
    resid_volume = resid_c.reshape(NCX, NCY, box_edge)

    def insert(number, volume):
        portion = restricted[number].reshape(half_edge, half_edge, half_edge)
        return lax.dynamic_update_slice(volume, portion, box_anchor(fine_position[number]))

    resid_volume = lax.fori_loop(0, FBOXES, insert, resid_volume)
    composite = resid_volume.reshape(NCX, NCY * box_edge)
    leading = first_colour[1]
    blanks = jnp.zeros_like(composite)
    correction = relaxed(blanks, composite, blanks, diagonal_c, 1.0, parity_coarse, leading)
    coupled = coupling(weights_c, neighbours(correction, outside, box_edge, 0.0, 0.0))
    correction = relaxed(correction, composite, coupled, diagonal_c, 1.0, parity_coarse, 1 - leading)
    leftover = residual_of(correction, composite, weights_c, diagonal_c, neighbours(correction, outside, box_edge, 0.0, 0.0), 1.0)
    bottom_source = coarsen(leftover, box_edge)
    bottom_coefficient = coarsen(coarse_coefficient, box_edge)
    bottom_outside = zero_borders(bottom_source, half_edge)

    def borders_of(values):
        return bottom_outside

    weights_b, diagonal_b = face_terms(bottom_coefficient, neighbours(bottom_coefficient, bottom_outside, half_edge, 0.0, 0.0))
    parity_bottom = parity_of(bottom_source.shape[0], bottom_source.shape[1], half_edge)
    bottom_values = bottom_sweeps(bottom_source, weights_b, diagonal_b, parity_bottom, first_colour[2], borders_of, half_edge)
    correction = correction + refine(bottom_values, half_edge)
    coarse_solution = coarse_start + correction
    correction_volume = correction.reshape(NCX, NCY, box_edge)

    def finish_box(operands):
        position, values = operands
        portion = lax.dynamic_slice(correction_volume, box_anchor(position), (half_edge, half_edge, half_edge))
        return values + refine(portion.reshape(half_edge, half_edge * half_edge), half_edge)

    fine_solution = lax.map(finish_box, (fine_position, smoothed))
    return coarse_solution, fine_solution
```

```python
import functools

import jax
import jax.numpy as jnp
from jax import lax
from jax.experimental import pallas as pl
from jax.experimental.pallas import tpu as pltpu
from jax.sharding import PartitionSpec as P


MESH = pl.DeviceIdType.MESH
F32 = jnp.float32
BF16 = jnp.bfloat16
SWEEPS = 4
N_X = 16
N_Y = 8


def iota(shape, dim):
    return lax.broadcasted_iota(jnp.int32, shape, dim)


def halves(values):
    high = values.astype(BF16)
    low = (values - high.astype(F32)).astype(BF16)
    return jnp.concatenate([high, low], axis=0)


def mapped(values, matrix):
    rows = values.shape[0]
    both = jnp.dot(halves(values), matrix, preferred_element_type=F32)
    return both[:rows] + both[rows:]


def roll(values, amount):
    return pltpu.roll(values, amount, axis=1)


def y_before(ref, j, rows, lanes, step):
    return roll(jnp.where(lanes >= 128 - step, ref[j - 1, rows], ref[j, rows]), step)


def y_beyond(ref, j, rows, lanes, step):
    return roll(jnp.where(lanes < step, ref[j + 1, rows], ref[j, rows]), 128 - step)


def coupled(value, weights, j, low, count, lanes, step):
    wx, wy, wz = weights
    here = pl.ds(low, count)
    before = pl.ds(low - 1, count)
    beyond = pl.ds(low + 1, count)
    mid = value[j, here]
    w_y = wy[j, here]
    w_z = wz[j, here]
    total = wx[j, here] * value[j, before] + wx[j, beyond] * value[j, beyond]
    total = total + w_y * y_before(value, j, here, lanes, step)
    ahead = jnp.where(lanes < step, wy[j + 1, here] * value[j + 1, here], w_y * mid)
    total = total + roll(ahead, 128 - step)
    return total + w_z * roll(mid, 1) + roll(w_z * mid, 127)


def zero_pads(ref, low, high):
    blocks, rows, _ = ref.shape
    ref[0] = jnp.zeros((rows, 128), F32)
    ref[blocks - 1] = jnp.zeros((rows, 128), F32)
    ref[1 : blocks - 1, :low] = jnp.zeros((blocks - 2, low, 128), F32)
    ref[1 : blocks - 1, high:] = jnp.zeros((blocks - 2, rows - high, 128), F32)


def put(ref, mask):
    ref[...] = jnp.where(mask, 1.0, 0.0).astype(BF16)


def kernel(
    pos,
    colours,
    c_source,
    c_coeff,
    c_start,
    f_source,
    f_coeff,
    f_start,
    out_c,
    out_f,
    s_fr,
    kq_fr,
    src_c,
    f_src,
    f_k,
    f_v,
    f_wx,
    f_wy,
    f_wz,
    f_inv,
    f_base,
    f_a,
    f_sm,
    f_d,
    f_res,
    f_gx,
    k_fr,
    r_fr,
    wx,
    wy,
    wz,
    inv_a,
    inv_b,
    e_a,
    e_b,
    left,
    b_k,
    b_wx,
    b_wy,
    b_wz,
    b_ia,
    b_ib,
    b_fa,
    b_fb,
    b_ua,
    b_ub,
    x_rows,
    faces,
    ghost_out,
    ghost_in,
    box_out,
    box_in,
    boxes,
    e_oct,
    e_out,
    e_in,
    u_oct,
    u_out,
    u_in,
    dup,
    dup2,
    m_face,
    m_ghost,
    m_down,
    m_up,
    m_exp,
    m_com,
    m_four,
    sem_l,
    sem_s0,
    sem_r0,
    sem_sk,
    sem_rk,
    sem_sr,
    sem_rr,
    sem_s1,
    sem_r1,
    sem_s2,
    sem_r2,
    sem_s3,
    sem_r3,
    sem_s4,
    sem_r4,
    sem_s5,
    sem_r5,
):
    mx = lax.axis_index("gx")
    my = lax.axis_index("gy")
    x_up, x_dn = lax.rem(mx + 1, N_X), lax.rem(mx + N_X - 1, N_X)
    y_up, y_dn = lax.rem(my + 1, N_Y), lax.rem(my + N_Y - 1, N_Y)
    around = [
        (x_dn, my),
        (x_up, my),
        (mx, y_dn),
        (mx, y_up),
        (x_dn, y_dn),
        (x_dn, y_up),
        (x_up, y_dn),
        (x_up, y_up),
    ]
    mates = [(lax.rem(mx + d, N_X), my) for d in range(1, N_X)]

    barrier = pltpu.get_barrier_semaphore()
    greeted = mates + around[2:]
    for device in greeted:
        pl.semaphore_signal(barrier, inc=1, device_id=device, device_id_type=MESH)

    loads = []

    def load(number, source, target):
        group = []
        for j in range(8):
            copy = pltpu.make_async_copy(source(j), target(j), sem_l.at[number, j])
            copy.start()
            group.append(copy)
        loads.append(group)

    def chunk(j):
        return pl.ds(128 * j, 128)

    load(0, lambda j: c_start.at[:, chunk(j)], lambda j: s_fr.at[1 + j, pl.ds(8, 32)])
    load(1, lambda j: c_coeff.at[:, chunk(j)], lambda j: kq_fr.at[1 + j, pl.ds(8, 32)])
    load(2, lambda j: f_coeff.at[0, :, chunk(j)], lambda j: f_k.at[1 + j, pl.ds(8, 32)])
    load(3, lambda j: f_start.at[0, :, chunk(j)], lambda j: f_v.at[1 + j, pl.ds(8, 32)])
    load(4, lambda j: f_source.at[0, :, chunk(j)], lambda j: f_src.at[j])
    load(5, lambda j: c_source.at[:, chunk(j)], lambda j: src_c.at[j])
    load(6, lambda j: c_coeff.at[:, chunk(j)], lambda j: k_fr.at[5 + j, pl.ds(24, 32)])

    own_pos = pos[mx * N_Y + my]
    owner_x = own_pos >> 6
    own_oz = own_pos & 1

    slots = []
    for ye in range(4):
        row = (my, y_dn, y_up)[1 if ye == 0 else (2 if ye == 3 else 0)]
        for sx in range(4):
            ox, oy = (sx + 1) % 2, (ye + 1) % 2
            octant = 4 * ox + 2 * oy + (ox + oy) % 2
            column = mx + (-1, 0, 0, 1)[sx]
            slots.append((row, (column * N_Y + row) * 8 + octant))

    def look(h, found):
        held = [pos[h * N_Y + row] for row in (my, y_dn, y_up)]
        result = []
        for number, (row, wanted) in enumerate(slots):
            ye = number // 4
            at = held[1 if ye == 0 else (2 if ye == 3 else 0)]
            result.append(jnp.where(at == wanted, h, found[number]))
        return tuple(result)

    found = lax.fori_loop(0, N_X, look, tuple(jnp.int32(-1) for _ in slots))
    octs = [(pos[h * N_Y + my] >> 1) & 3 for h in range(N_X)]

    lanes = iota((1, 128), 1)
    z_first = lanes % 32 == 0
    z_last = lanes % 32 == 31
    parity = (iota((8, 128), 0) + iota((8, 128), 1) // 32 + iota((8, 128), 1)) % 2
    parity_b = (iota((8, 128), 0) + iota((8, 128), 1) // 16 + iota((8, 128), 1)) % 2

    def painted(base, colour, rows):
        flags = jnp.where(base == colour, 1.0, 0.0)
        return jnp.concatenate([flags] * (rows // 8), axis=0) > 0.5

    first_f = painted(parity, colours[0], 32)
    first_c = painted(parity, colours[1], 64)
    first_b = painted(parity_b, colours[2], 32)

    zero_pads(f_v, 8, 40)
    zero_pads(f_wx, 8, 40)
    zero_pads(f_wy, 8, 40)
    zero_pads(f_a, 8, 40)
    zero_pads(f_d, 8, 40)
    x_rows[...] = jnp.zeros(x_rows.shape, F32)
    f_gx[...] = jnp.zeros(f_gx.shape, F32)

    for oz in range(2):
        k = iota((896, 128), 0)
        c = iota((896, 128), 1)
        block, lane = k // 128, k % 128
        z, yy = lane % 32, lane // 32
        mask = (block == 0) & (c < 16) & (lane == 96 + 16 * oz + c)
        mask = mask | ((block == 1) & (c >= 16) & (c < 32) & (lane == 16 * oz + c - 16))
        own = (block >= 2) & (block < 6) & (z == (16, 15)[oz])
        mask = mask | (own & (c == (48, 32)[oz] + 4 * (block - 2) + yy))
        mask = mask | (
            (block == 6) & (z >= 16 * oz) & (z < 16 * oz + 16) & (c == 64 + yy * 16 + z - 16 * oz)
        )
        m_face[oz] = jnp.where(mask, 1.0, 0.0).astype(BF16)

    for group in loads[:2]:
        for copy in group:
            copy.wait()
    pl.semaphore_wait(barrier, len(greeted))

    sends = []

    def remote(source, target, send_sem, recv_sem, device):
        copy = pltpu.make_async_remote_copy(
            src_ref=source,
            dst_ref=target,
            send_sem=send_sem,
            recv_sem=recv_sem,
            device_id=device,
            device_id_type=MESH,
        )
        copy.start()
        sends.append(copy)
        return copy

    layer = []
    for number, ref in enumerate((s_fr, kq_fr)):
        rows, blocks = pl.ds(8, 32), pl.ds(1, 8)
        for side, (source, target, device) in enumerate(
            (
                (ref.at[8, rows], ref.at[0, rows], around[3]),
                (ref.at[1, rows], ref.at[9, rows], around[2]),
                (ref.at[blocks, pl.ds(39, 1)], ref.at[blocks, pl.ds(7, 1)], around[1]),
                (ref.at[blocks, pl.ds(8, 1)], ref.at[blocks, pl.ds(40, 1)], around[0]),
            )
        ):
            at = 4 * number + side
            layer.append(remote(source, target, sem_s0.at[at], sem_r0.at[at], device))

    for group in loads[2:5]:
        for copy in group:
            copy.wait()
    rows_f = iota((32, 128), 0)
    own_f = pl.ds(8, 32)

    def fine_weights(i, carry):
        j = i + 1
        k = f_k[j, own_f]
        y_first = (lanes < 32) & (j == 1)
        y_last = (lanes >= 96) & (j == 8)
        kxm = jnp.where(rows_f == 0, k, f_k[j, pl.ds(7, 32)])
        kxp = jnp.where(rows_f == 31, k, f_k[j, pl.ds(9, 32)])
        kym = jnp.where(y_first, k, y_before(f_k, j, own_f, lanes, 32))
        kyp = jnp.where(y_last, k, y_beyond(f_k, j, own_f, lanes, 32))
        kzm = jnp.where(z_first, k, roll(k, 1))
        kzp = jnp.where(z_last, k, roll(k, 127))
        f_wx[j, own_f] = jnp.where(rows_f == 0, 0.0, 0.5 * (k + kxm))
        f_wy[j, own_f] = jnp.where(y_first, 0.0, 0.5 * (k + kym))
        f_wz[j, own_f] = jnp.where(z_first, 0.0, 0.5 * (k + kzm))
        f_inv[j, own_f] = 1.0 / (3.0 * k + 0.5 * (kxm + kxp + kym + kyp + kzm + kzp))
        return carry

    lax.fori_loop(0, 8, fine_weights, 0)
    w_f = (f_wx, f_wy, f_wz)

    def fine_base(i, carry):
        f_base[i + 1, own_f] = 0.25 * f_src[i] + coupled(f_v, w_f, i + 1, 8, 32, lanes, 32)
        return carry

    lax.fori_loop(0, 8, fine_base, 0)

    for copy in layer:
        copy.wait_recv()
    for ref in (s_fr, kq_fr):

        @pl.when(mx == 0)
        def _():
            ref[1:9, 7:8] = jnp.zeros((8, 1, 128), F32)

        @pl.when(mx == N_X - 1)
        def _():
            ref[1:9, 40:41] = jnp.zeros((8, 1, 128), F32)

        @pl.when(my == 0)
        def _():
            ref[0, 8:40] = jnp.zeros((32, 128), F32)

        @pl.when(my == N_Y - 1)
        def _():
            ref[9, 8:40] = jnp.zeros((32, 128), F32)

    for ox in range(2):
        for oy in range(2):
            for q in range(4):
                for at, row in ((q, 7 + 16 * ox), (4 + q, 24 + 16 * ox)):
                    x_rows[2 * ox + oy, at : at + 1] = s_fr[1 + 4 * oy + q, row : row + 1]
    for oz in range(2):
        pair = [(0, oz), (1, 1 - oz)]
        stacked = []
        for ox, oy in pair:
            rows = pl.ds(8 + 16 * ox, 16)
            parts = [s_fr[4 * oy, rows], s_fr[5 + 4 * oy, rows]]
            parts += [s_fr[1 + 4 * oy + q, rows] for q in range(4)]
            parts.append(x_rows[2 * ox + oy])
            stacked.append(jnp.concatenate(parts, axis=1))
        packed = mapped(jnp.concatenate(stacked, axis=0), m_face[oz])
        for number, (ox, oy) in enumerate(pair):
            faces[2 * ox + oy] = packed[16 * number : 16 * number + 16]

    def to_mates(source, target, send_sem, recv_sem):
        started = []
        for d in range(1, N_X):
            other = lax.rem(mx + d, N_X)
            started.append(
                remote(source(other), target.at[mx], send_sem.at[d], recv_sem.at[d], (other, my))
            )
        return started

    for h in range(N_X):
        ghost_out[h] = faces[octs[h]]
    ghosts = to_mates(lambda other: ghost_out.at[other], ghost_in, sem_s1, sem_r1)
    ghost_in[mx] = ghost_out[mx]

    for copy in loads[6]:
        copy.wait()

    def deep(ref, base, width, blocks, send_sem, recv_sem):
        full_r, full_b = (base, base, 32), (5, 5, 8)
        r_low = (base, base + 32, width)
        r_high = (base + 32 - width, base - width, width)
        b_low = (5, 13, blocks)
        b_high = (13 - blocks, 5 - blocks, blocks)
        started = []
        for number, (r, b) in enumerate(
            (
                (r_low, full_b),
                (r_high, full_b),
                (full_r, b_low),
                (full_r, b_high),
                (r_low, b_low),
                (r_low, b_high),
                (r_high, b_low),
                (r_high, b_high),
            )
        ):
            started.append(
                remote(
                    ref.at[pl.ds(b[0], b[2]), pl.ds(r[0], r[2])],
                    ref.at[pl.ds(b[1], b[2]), pl.ds(r[1], r[2])],
                    send_sem.at[number],
                    recv_sem.at[number],
                    around[number],
                )
            )
        return started

    deep_k = deep(k_fr, 24, 24, 5, sem_sk, sem_rk)

    for copy in loads[5]:
        copy.wait()

    def coarse_residual(i, carry):
        j = i + 1
        s = s_fr[j, own_f]
        k = kq_fr[j, own_f]

        def flux(k_there, s_there):
            return (k + k_there) * (s - s_there)

        before, beyond = pl.ds(7, 32), pl.ds(9, 32)
        total = flux(kq_fr[j, before], s_fr[j, before]) + flux(kq_fr[j, beyond], s_fr[j, beyond])
        total = total + flux(
            y_before(kq_fr, j, own_f, lanes, 32), y_before(s_fr, j, own_f, lanes, 32)
        )
        total = total + flux(
            y_beyond(kq_fr, j, own_f, lanes, 32), y_beyond(s_fr, j, own_f, lanes, 32)
        )
        total = total + flux(
            jnp.where(z_first, 0.0, roll(k, 1)), jnp.where(z_first, 0.0, roll(s, 1))
        )
        total = total + flux(
            jnp.where(z_last, 0.0, roll(k, 127)), jnp.where(z_last, 0.0, roll(s, 127))
        )
        r_fr[i + 5, pl.ds(24, 32)] = src_c[i] - 0.5 * total
        return carry

    lax.fori_loop(0, 8, coarse_residual, 0)
    deep_r = deep(r_fr, 24, 16, 4, sem_sr, sem_rr)

    k = iota((128, 1280), 0)
    c = iota((128, 1280), 1)
    y, z = c // 32, c % 32
    inner = c < 1024
    mask = inner & (y == 0) & (k == z // 2)
    mask = mask | (inner & (y == 31) & (k == 16 + z // 2))
    mask = mask | (inner & (z == 0) & (k == 32 + y // 2))
    mask = mask | (inner & (z == 31) & (k == 48 + y // 2))
    mask = mask | ((c >= 1024) & (k == 64 + (y - 32) // 2 * 16 + z // 2))
    put(m_ghost, mask)
    k, c = iota((512, 128), 0), iota((512, 128), 1)
    put(m_down, c == k // 64 * 16 + k % 32 // 2)

    for copy in ghosts:
        copy.wait_recv()
    mine = ghost_in[owner_x]
    dup[0, pl.ds(0, 16, stride=2)] = mine
    dup[0, pl.ds(1, 16, stride=2)] = mine
    widened = mapped(dup[0], m_ghost[...])
    for q in range(4):
        for t in range(2):
            piece = widened[:, 1024 + 128 * t : 1152 + 128 * t]
            f_gx[2 * q + t, 0:1] = piece[2 * q : 2 * q + 1]
            f_gx[2 * q + t, 31:32] = piece[8 + 2 * q : 9 + 2 * q]
    for i in range(8):
        j = i + 1
        ghost = f_k[j, own_f] * (widened[:, 128 * i : 128 * i + 128] + f_gx[i])
        f_gx[i] = ghost
        f_a[j, own_f] = jnp.where(first_f, (f_base[j, own_f] + ghost) * f_inv[j, own_f], 0.0)
    for i in range(8):
        j = i + 1
        around_a = coupled(f_a, w_f, j, 8, 32, lanes, 32)
        fresh = (0.25 * f_src[i] + f_gx[i] + around_a) * f_inv[j, own_f]
        f_sm[i] = jnp.where(first_f, f_a[j, own_f], fresh)
        f_d[j, own_f] = jnp.where(first_f, 0.0, fresh - f_v[j, own_f])
    for i in range(8):
        f_res[i] = jnp.where(first_f, coupled(f_d, w_f, i + 1, 8, 32, lanes, 32), 0.0)
    stacked = []
    for b in range(2):
        parts = [
            f_res[4 * b + q, pl.ds(0, 16, stride=2)] + f_res[4 * b + q, pl.ds(1, 16, stride=2)]
            for q in range(4)
        ]
        stacked.append(jnp.concatenate(parts, axis=1))
    packed = 0.5 * mapped(jnp.concatenate(stacked, axis=0), m_down[...])
    box_out[0] = packed[:16]
    box_out[1] = packed[16:]
    gathered = to_mates(lambda other: box_out, box_in, sem_s2, sem_r2)
    box_in[mx] = box_out[...]

    zero_pads(wx, 8, 72)
    zero_pads(wy, 8, 72)
    zero_pads(e_a, 8, 72)
    zero_pads(e_b, 8, 72)
    for ref in (b_k, b_wx, b_wy, b_ua, b_ub):
        zero_pads(ref, 8, 40)
    for oz in range(2):
        k, c = iota((128, 256), 0), iota((128, 256), 1)
        m_exp[oz] = jnp.where((k // 16 == c // 32) & (c % 32 == 16 * oz + k % 16), 1.0, 0.0).astype(BF16)
        k, c = iota((256, 128), 1), iota((256, 128), 0)
        m_com[oz] = jnp.where((k // 16 == c // 32) & (c % 32 == 16 * oz + k % 16), 1.0, 0.0).astype(BF16)
    k, c = iota((128, 512), 0), iota((128, 512), 1)
    put(m_up, k == c // 64 * 16 + c % 32 // 2)
    k, c = iota((128, 1024), 0), iota((128, 1024), 1)
    put(m_four, k == c // 128 * 16 + c % 32 // 4)

    for copy in deep_k:
        copy.wait_recv()
    for copy in deep_k:
        copy.wait_send()

    @pl.when(mx == 0)
    def _():
        k_fr[:, 0:24] = jnp.zeros((18, 24, 128), F32)

    @pl.when(mx == N_X - 1)
    def _():
        k_fr[:, 56:80] = jnp.zeros((18, 24, 128), F32)

    @pl.when(my == 0)
    def _():
        k_fr[0:5] = jnp.zeros((5, 80, 128), F32)

    @pl.when(my == N_Y - 1)
    def _():
        k_fr[13:18] = jnp.zeros((5, 80, 128), F32)

    window = pl.ds(8, 64)

    def coarse_weights(i, carry):
        j = i + 1
        k = k_fr[j, window]
        kxm = k_fr[j, pl.ds(7, 64)]
        kxp = k_fr[j, pl.ds(9, 64)]
        kym = y_before(k_fr, j, window, lanes, 32)
        kyp = y_beyond(k_fr, j, window, lanes, 32)
        kzm = jnp.where(z_first, 0.0, roll(k, 1))
        kzp = jnp.where(z_last, 0.0, roll(k, 127))
        wx[j, window] = 0.5 * (k + kxm)
        wy[j, window] = 0.5 * (k + kym)
        wz[j, window] = jnp.where(z_first, 0.0, 0.5 * (k + kzm))
        inverse = 1.0 / (3.0 * k + 0.5 * (kxm + kxp + kym + kyp + kzm + kzp))
        inverse = jnp.where(k > 0.0, inverse, 0.0)
        inv_a[j, window] = jnp.where(first_c, inverse, 0.0)
        inv_b[j, window] = jnp.where(first_c, 0.0, inverse)
        return carry

    lax.fori_loop(0, 16, coarse_weights, 0)
    w_c = (wx, wy, wz)

    def coarsened(ref):
        stacked = []
        for b in range(4):
            parts = [
                ref[1 + 4 * b + q, pl.ds(8, 32, stride=2)]
                + ref[1 + 4 * b + q, pl.ds(9, 32, stride=2)]
                for q in range(4)
            ]
            stacked.append(jnp.concatenate(parts, axis=1))
        return mapped(jnp.concatenate(stacked, axis=0), m_down[...])

    summed = coarsened(k_fr)
    own_b = pl.ds(8, 32)
    for b in range(4):
        b_k[1 + b, own_b] = 0.125 * summed[32 * b : 32 * b + 32]
    zb_first = lanes % 16 == 0
    zb_last = lanes % 16 == 15
    for b in range(4):
        j = b + 1
        k = b_k[j, own_b]
        kxm = b_k[j, pl.ds(7, 32)]
        kxp = b_k[j, pl.ds(9, 32)]
        kym = y_before(b_k, j, own_b, lanes, 16)
        kyp = y_beyond(b_k, j, own_b, lanes, 16)
        kzm = jnp.where(zb_first, 0.0, roll(k, 1))
        kzp = jnp.where(zb_last, 0.0, roll(k, 127))
        b_wx[j, own_b] = 0.5 * (k + kxm)
        b_wy[j, own_b] = 0.5 * (k + kym)
        b_wz[j, own_b] = jnp.where(zb_first, 0.0, 0.5 * (k + kzm))
        inverse = 1.0 / (3.0 * k + 0.5 * (kxm + kxp + kym + kyp + kzm + kzp))
        inverse = jnp.where(k > 0.0, inverse, 0.0)
        b_ia[b] = jnp.where(first_b, inverse, 0.0)
        b_ib[b] = jnp.where(first_b, 0.0, inverse)

    for copy in deep_r:
        copy.wait_recv()
    for copy in deep_r:
        copy.wait_send()

    for copy in gathered:
        copy.wait_recv()
    for ye in (1, 2):
        for sx in range(4):
            boxes[ye, sx] = box_in[jnp.maximum(found[4 * ye + sx], 0)]
    beside = [
        remote(boxes.at[1], boxes.at[3], sem_s3.at[0], sem_r3.at[0], around[2]),
        remote(boxes.at[2], boxes.at[0], sem_s3.at[1], sem_r3.at[1], around[3]),
    ]

    def compose(ye):
        for oz in range(2):
            pair = [sx for sx in range(4) if (sx + ye) % 2 == oz]
            stacked = [boxes[ye, sx, b] for sx in pair for b in range(2)]
            wide = mapped(jnp.concatenate(stacked, axis=0), m_exp[oz])
            for number, sx in enumerate(pair):
                here = jnp.where(found[4 * ye + sx] >= 0, 1.0, 0.0)
                covered = jnp.where(lanes % 32 // 16 == oz, here, 0.0) > 0.5
                rows = pl.ds(8 + 16 * sx, 16)
                for q in range(4):
                    b, t = q // 2, q % 2
                    j = 1 + 4 * ye + q
                    at = 32 * number + 16 * b
                    part = wide[at : at + 16, 128 * t : 128 * t + 128]
                    mixed = jnp.where(covered, part, r_fr[j, rows])
                    r_fr[j, rows] = mixed
                    e_a[j, rows] = mixed * inv_a[j, rows]

    compose(1)
    compose(2)
    for copy in beside:
        copy.wait_recv()
    compose(0)
    compose(3)

    def second(i, carry):
        j = i + 1
        fresh = r_fr[j, window] + coupled(e_a, w_c, j, 8, 64, lanes, 32)
        e_b[j, window] = fresh * inv_b[j, window]
        return carry

    lax.fori_loop(0, 16, second, 0, unroll=2)

    own_c = pl.ds(24, 32)
    for oz in range(2):
        pair = [(0, oz), (1, 1 - oz)]
        stacked = []
        for ox, oy in pair:
            rows = pl.ds(24 + 16 * ox, 16)
            for b in range(2):
                parts = [
                    e_a[5 + 4 * oy + 2 * b + t, rows] + e_b[5 + 4 * oy + 2 * b + t, rows]
                    for t in range(2)
                ]
                stacked.append(jnp.concatenate(parts, axis=1))
        packed = mapped(jnp.concatenate(stacked, axis=0), m_com[oz])
        for number, (ox, oy) in enumerate(pair):
            for b in range(2):
                at = 32 * number + 16 * b
                e_oct[2 * ox + oy, b] = packed[at : at + 16]
    for h in range(N_X):
        e_out[h] = e_oct[octs[h]]
    returned = to_mates(lambda other: e_out.at[other], e_in, sem_s4, sem_r4)
    e_in[mx] = e_out[mx]

    def remaining(i, carry):
        j = i + 1
        left[j, window] = jnp.where(first_c, coupled(e_b, w_c, j, 8, 64, lanes, 32), 0.0)
        return carry

    lax.fori_loop(0, 16, remaining, 0, unroll=2)
    summed = 0.5 * coarsened(left)
    for b in range(4):
        source = summed[32 * b : 32 * b + 32]
        b_fa[b] = source * b_ia[b]
        b_fb[b] = source * b_ib[b]
        b_ua[1 + b, own_b] = source * b_ia[b]
    w_b = (b_wx, b_wy, b_wz)
    for half in range(2 * SWEEPS - 1):
        into, out_of = ((b_ub, b_ua), (b_ua, b_ub))[half % 2]
        fixed, inverse = ((b_fb, b_ib), (b_fa, b_ia))[half % 2]
        for b in range(4):
            into[1 + b, own_b] = fixed[b] + inverse[b] * coupled(
                out_of, w_b, 1 + b, 8, 32, lanes, 16
            )

    for ox in range(2):
        for oy in range(2):
            rows = pl.ds(16 + 8 * ox, 8)
            u_oct[2 * ox + oy] = b_ua[2 + oy, rows] + b_ub[2 + oy, rows]
    for h in range(N_X):
        u_out[h] = u_oct[octs[h]]
    settled = to_mates(lambda other: u_out.at[other], u_in, sem_s5, sem_r5)
    u_in[mx] = u_out[mx]

    def doubled(ref, pieces):
        for b, piece in enumerate(pieces):
            ref[b, pl.ds(0, 16, stride=2)] = piece
            ref[b, pl.ds(1, 16, stride=2)] = piece
        return mapped(jnp.concatenate([ref[0], ref[1]], axis=0), m_up[...])

    wide = doubled(dup, [b_ua[2 + b, pl.ds(16, 16)] + b_ub[2 + b, pl.ds(16, 16)] for b in range(2)])
    for j in range(8):
        b, q = j // 4, j % 4
        part = wide[32 * b : 32 * b + 32, 128 * q : 128 * q + 128]
        total = e_a[5 + j, own_c] + e_b[5 + j, own_c] + part
        out_c[:, 128 * j : 128 * j + 128] = s_fr[1 + j, own_f] + total

    for copy in returned:
        copy.wait_recv()
    got = e_in.at[owner_x]
    wide = doubled(dup2, [got[0], got[1]])
    for j in range(8):
        b, q = j // 4, j % 4
        f_sm[j] = f_sm[j] + wide[32 * b : 32 * b + 32, 128 * q : 128 * q + 128]
    for copy in settled:
        copy.wait_recv()
    tile = u_in[owner_x]
    side = jnp.where(own_oz == 1, 1.0, 0.0)
    tile = jnp.where(jnp.zeros((8, 128), F32) + side > 0.5, roll(tile, 120), tile)
    for t in range(4):
        dup[0, pl.ds(t, 8, stride=4)] = tile
    wide = mapped(dup[0], m_four[...])
    for j in range(8):
        out_f[0, :, 128 * j : 128 * j + 128] = f_sm[j] + wide[:, 128 * j : 128 * j + 128]

    done = [id(copy) for copy in deep_k + deep_r]
    for copy in sends:
        if id(copy) not in done:
            copy.wait_send()


def scratch():
    v = pltpu.VMEM
    shapes = [(10, 48, 128)] * 2 + [(8, 32, 128)]
    shapes += [(8, 32, 128)] + [(10, 48, 128)] * 8 + [(8, 32, 128), (10, 48, 128)]
    shapes += [(8, 32, 128)] * 2
    shapes += [(18, 80, 128)] * 10
    shapes += [(6, 48, 128)] * 4 + [(4, 32, 128)] * 4 + [(6, 48, 128)] * 2
    shapes += [(4, 16, 128), (4, 16, 128), (N_X, 16, 128), (N_X, 16, 128)]
    shapes += [(2, 16, 128), (N_X, 2, 16, 128), (4, 4, 2, 16, 128)]
    shapes += [(4, 2, 16, 128), (N_X, 2, 16, 128), (N_X, 2, 16, 128)]
    shapes += [(4, 8, 128), (N_X, 8, 128), (N_X, 8, 128)]
    shapes += [(2, 32, 128)] * 2
    result = [v(shape, F32) for shape in shapes]
    maps = [(2, 896, 128), (128, 1280), (512, 128), (128, 512), (2, 128, 256), (2, 256, 128)]
    result += [v(shape, BF16) for shape in maps + [(128, 1024)]]
    dma = pltpu.SemaphoreType.DMA
    result += [dma((7, 8))] + [dma((8,))] * 6 + [dma((N_X,))] * 4 + [dma((2,))] * 2
    return result + [dma((N_X,))] * 4


def on_device(
    coarse_source,
    coarse_coefficient,
    coarse_start,
    fine_source,
    fine_coefficient,
    fine_start,
    fine_position,
    first_colour,
):
    smem = pl.BlockSpec(memory_space=pltpu.SMEM)
    vmem = pl.BlockSpec(memory_space=pltpu.VMEM)
    hbm = pl.BlockSpec(memory_space=pl.ANY)
    return pl.pallas_call(
        kernel,
        out_shape=(
            jax.ShapeDtypeStruct(coarse_start.shape, F32),
            jax.ShapeDtypeStruct(fine_start.shape, F32),
        ),
        in_specs=[smem, smem] + [hbm] * 6,
        out_specs=(vmem, vmem),
        scratch_shapes=scratch(),
        compiler_params=pltpu.CompilerParams(
            collective_id=0, has_side_effects=True, vmem_limit_bytes=48 << 20
        ),
    )(
        fine_position,
        first_colour,
        coarse_source,
        coarse_coefficient,
        coarse_start,
        fine_source,
        fine_coefficient,
        fine_start,
    )


def solution(mesh):
    placed = (
        P("gx", "gy"),
        P("gx", "gy"),
        P("gx", "gy"),
        P(("gx", "gy"), None, None),
        P(("gx", "gy"), None, None),
        P(("gx", "gy"), None, None),
        P(),
        P(),
    )
    return jax.shard_map(
        on_device,
        mesh=mesh,
        in_specs=placed,
        out_specs=(P("gx", "gy"), P(("gx", "gy"), None, None)),
        check_vma=False,
    )
```

```python
import functools

import jax
import jax.numpy as jnp
from jax import lax
from jax.experimental import pallas as pl
from jax.experimental.pallas import tpu as pltpu
from jax.sharding import PartitionSpec as P


MESH = pl.DeviceIdType.MESH
F32 = jnp.float32
BF16 = jnp.bfloat16
SWEEPS = 4
N_X = 16
N_Y = 8


def iota(shape, dim):
    return lax.broadcasted_iota(jnp.int32, shape, dim)


def halves(values):
    high = values.astype(BF16)
    low = (values - high.astype(F32)).astype(BF16)
    return jnp.concatenate([high, low], axis=0)


def mapped(values, matrix):
    rows = values.shape[0]
    both = jnp.dot(halves(values), matrix, preferred_element_type=F32)
    return both[:rows] + both[rows:]


def roll(values, amount):
    return pltpu.roll(values, amount, axis=1)


def y_before(ref, j, rows, lanes, step):
    return roll(jnp.where(lanes >= 128 - step, ref[j - 1, rows], ref[j, rows]), step)


def y_beyond(ref, j, rows, lanes, step):
    return roll(jnp.where(lanes < step, ref[j + 1, rows], ref[j, rows]), 128 - step)


def coupled(value, weights, j, low, count, lanes, step):
    wx, wy, wz = weights
    here = pl.ds(low, count)
    before = pl.ds(low - 1, count)
    beyond = pl.ds(low + 1, count)
    mid = value[j, here]
    w_y = wy[j, here]
    w_z = wz[j, here]
    total = wx[j, here] * value[j, before] + wx[j, beyond] * value[j, beyond]
    total = total + w_y * y_before(value, j, here, lanes, step)
    ahead = jnp.where(lanes < step, wy[j + 1, here] * value[j + 1, here], w_y * mid)
    total = total + roll(ahead, 128 - step)
    return total + w_z * roll(mid, 1) + roll(w_z * mid, 127)


def zero_pads(ref, low, high):
    blocks, rows, _ = ref.shape
    ref[0] = jnp.zeros((rows, 128), F32)
    ref[blocks - 1] = jnp.zeros((rows, 128), F32)
    ref[1 : blocks - 1, :low] = jnp.zeros((blocks - 2, low, 128), F32)
    ref[1 : blocks - 1, high:] = jnp.zeros((blocks - 2, rows - high, 128), F32)


class Remote:
    def __init__(self, copy):
        self.copy = copy
        self.landed = False
        self.left = False
        copy.start()

    def wait_recv(self):
        if not self.landed:
            self.copy.wait_recv()
        self.landed = True

    def wait_send(self):
        if not self.left:
            self.copy.wait_send()
        self.left = True


def put(ref, mask):
    ref[...] = jnp.where(mask, 1.0, 0.0).astype(BF16)


def kernel(
    pos,
    colours,
    c_source,
    c_coeff,
    c_start,
    f_source,
    f_coeff,
    f_start,
    out_c,
    out_f,
    s_fr,
    kq_fr,
    src_c,
    f_src,
    f_k,
    f_v,
    f_wx,
    f_wy,
    f_wz,
    f_inv,
    f_base,
    f_a,
    f_sm,
    f_d,
    f_res,
    f_gx,
    k_fr,
    r_fr,
    wx,
    wy,
    wz,
    inv_a,
    inv_b,
    e_a,
    e_b,
    left,
    b_k,
    b_wx,
    b_wy,
    b_wz,
    b_ia,
    b_ib,
    b_fa,
    b_fb,
    b_ua,
    b_ub,
    x_rows,
    faces,
    ghost_out,
    ghost_in,
    box_out,
    box_in,
    boxes,
    e_oct,
    e_out,
    e_in,
    u_oct,
    u_out,
    u_in,
    dup,
    dup2,
    m_face,
    m_ghost,
    m_down,
    m_up,
    m_exp,
    m_com,
    m_four,
    sem_l,
    sem_s0,
    sem_r0,
    sem_sk,
    sem_rk,
    sem_sr,
    sem_rr,
    sem_s1,
    sem_r1,
    sem_s2,
    sem_r2,
    sem_s3,
    sem_r3,
    sem_s4,
    sem_r4,
    sem_s5,
    sem_r5,
):
    mx = lax.axis_index("gx")
    my = lax.axis_index("gy")
    x_up, x_dn = lax.rem(mx + 1, N_X), lax.rem(mx + N_X - 1, N_X)
    y_up, y_dn = lax.rem(my + 1, N_Y), lax.rem(my + N_Y - 1, N_Y)
    around = [
        (x_dn, my),
        (x_up, my),
        (mx, y_dn),
        (mx, y_up),
    ]
    mates = [(lax.rem(mx + d, N_X), my) for d in range(1, N_X)]

    for blocks in (pl.ds(0, 5), pl.ds(13, 5)):
        for rows in (pl.ds(0, 24), pl.ds(56, 24)):
            k_fr[blocks, rows] = jnp.zeros((5, 24, 128), F32)
            r_fr[blocks, rows] = jnp.zeros((5, 24, 128), F32)

    barrier = pltpu.get_barrier_semaphore()
    greeted = mates + around[2:]
    for device in greeted:
        pl.semaphore_signal(barrier, inc=1, device_id=device, device_id_type=MESH)

    loads = []

    def load(number, source, target):
        group = []
        for j in range(8):
            copy = pltpu.make_async_copy(source(j), target(j), sem_l.at[number, j])
            copy.start()
            group.append(copy)
        loads.append(group)

    def chunk(j):
        return pl.ds(128 * j, 128)

    load(0, lambda j: c_start.at[:, chunk(j)], lambda j: s_fr.at[1 + j, pl.ds(8, 32)])
    load(1, lambda j: c_coeff.at[:, chunk(j)], lambda j: kq_fr.at[1 + j, pl.ds(8, 32)])
    load(2, lambda j: f_coeff.at[0, :, chunk(j)], lambda j: f_k.at[1 + j, pl.ds(8, 32)])
    load(3, lambda j: f_start.at[0, :, chunk(j)], lambda j: f_v.at[1 + j, pl.ds(8, 32)])
    load(4, lambda j: f_source.at[0, :, chunk(j)], lambda j: f_src.at[j])
    load(5, lambda j: c_source.at[:, chunk(j)], lambda j: src_c.at[j])
    load(6, lambda j: c_coeff.at[:, chunk(j)], lambda j: k_fr.at[5 + j, pl.ds(24, 32)])

    own_pos = pos[mx * N_Y + my]
    owner_x = own_pos >> 6
    own_oz = own_pos & 1

    slots = []
    for ye in range(4):
        row = (my, y_dn, y_up)[1 if ye == 0 else (2 if ye == 3 else 0)]
        for sx in range(4):
            ox, oy = (sx + 1) % 2, (ye + 1) % 2
            octant = 4 * ox + 2 * oy + (ox + oy) % 2
            column = mx + (-1, 0, 0, 1)[sx]
            slots.append((row, (column * N_Y + row) * 8 + octant))

    def look(h, found):
        held = [pos[h * N_Y + row] for row in (my, y_dn, y_up)]
        result = []
        for number, (row, wanted) in enumerate(slots):
            ye = number // 4
            at = held[1 if ye == 0 else (2 if ye == 3 else 0)]
            result.append(jnp.where(at == wanted, h, found[number]))
        return tuple(result)

    found = lax.fori_loop(0, N_X, look, tuple(jnp.int32(-1) for _ in slots))
    octs = [(pos[h * N_Y + my] >> 1) & 3 for h in range(N_X)]

    lanes = iota((1, 128), 1)
    z_first = lanes % 32 == 0
    z_last = lanes % 32 == 31
    parity = (iota((8, 128), 0) + iota((8, 128), 1) // 32 + iota((8, 128), 1)) % 2
    parity_b = (iota((8, 128), 0) + iota((8, 128), 1) // 16 + iota((8, 128), 1)) % 2

    def painted(base, colour, rows):
        flags = jnp.where(base == colour, 1.0, 0.0)
        return jnp.concatenate([flags] * (rows // 8), axis=0) > 0.5

    first_f = painted(parity, colours[0], 32)
    first_c = painted(parity, colours[1], 64)
    first_b = painted(parity_b, colours[2], 32)

    zero_pads(f_v, 8, 40)
    zero_pads(f_wx, 8, 40)
    zero_pads(f_wy, 8, 40)
    zero_pads(f_a, 8, 40)
    zero_pads(f_d, 8, 40)
    x_rows[...] = jnp.zeros(x_rows.shape, F32)
    f_gx[...] = jnp.zeros(f_gx.shape, F32)

    for oz in range(2):
        k = iota((896, 128), 0)
        c = iota((896, 128), 1)
        block, lane = k // 128, k % 128
        z, yy = lane % 32, lane // 32
        mask = (block == 0) & (c < 16) & (lane == 96 + 16 * oz + c)
        mask = mask | ((block == 1) & (c >= 16) & (c < 32) & (lane == 16 * oz + c - 16))
        own = (block >= 2) & (block < 6) & (z == (16, 15)[oz])
        mask = mask | (own & (c == (48, 32)[oz] + 4 * (block - 2) + yy))
        mask = mask | (
            (block == 6) & (z >= 16 * oz) & (z < 16 * oz + 16) & (c == 64 + yy * 16 + z - 16 * oz)
        )
        m_face[oz] = jnp.where(mask, 1.0, 0.0).astype(BF16)

    for group in loads[:2]:
        for copy in group:
            copy.wait()
    pl.semaphore_wait(barrier, len(greeted))

    sends = []

    def remote(source, target, send_sem, recv_sem, device):
        copy = Remote(
            pltpu.make_async_remote_copy(
                src_ref=source,
                dst_ref=target,
                send_sem=send_sem,
                recv_sem=recv_sem,
                device_id=device,
                device_id_type=MESH,
            )
        )
        sends.append(copy)
        return copy

    layer = []
    for number, ref in enumerate((s_fr, kq_fr)):
        rows, blocks = pl.ds(8, 32), pl.ds(1, 8)
        for side, (source, target, device) in enumerate(
            (
                (ref.at[8, rows], ref.at[0, rows], around[3]),
                (ref.at[1, rows], ref.at[9, rows], around[2]),
                (ref.at[blocks, pl.ds(39, 1)], ref.at[blocks, pl.ds(7, 1)], around[1]),
                (ref.at[blocks, pl.ds(8, 1)], ref.at[blocks, pl.ds(40, 1)], around[0]),
            )
        ):
            at = 4 * number + side
            layer.append(remote(source, target, sem_s0.at[at], sem_r0.at[at], device))

    for copy in loads[6]:
        copy.wait()

    def deep_x(ref, width, send_sem, recv_sem):
        blocks = pl.ds(5, 8)
        started = []
        for side, (source, target) in enumerate(((24, 56), (56 - width, 24 - width))):
            started.append(
                remote(
                    ref.at[blocks, pl.ds(source, width)],
                    ref.at[blocks, pl.ds(target, width)],
                    send_sem.at[side],
                    recv_sem.at[side],
                    around[side],
                )
            )
        return started

    def deep_y(ref, depth, send_sem, recv_sem):
        started = []
        for q in range(depth):
            rows = pl.ds(8 + 4 * q, 64 - 8 * q)
            for side, (source, target) in enumerate(((5 + q, 13 + q), (12 - q, 4 - q))):
                at = 2 + 2 * q + side
                started.append(
                    remote(
                        ref.at[source, rows],
                        ref.at[target, rows],
                        send_sem.at[at],
                        recv_sem.at[at],
                        around[2 + side],
                    )
                )
        return started

    deep_k = deep_x(k_fr, 17, sem_sk, sem_rk)

    for group in loads[2:5]:
        for copy in group:
            copy.wait()
    rows_f = iota((32, 128), 0)
    own_f = pl.ds(8, 32)

    def fine_weights(i, carry):
        j = i + 1
        k = f_k[j, own_f]
        y_first = (lanes < 32) & (j == 1)
        y_last = (lanes >= 96) & (j == 8)
        kxm = jnp.where(rows_f == 0, k, f_k[j, pl.ds(7, 32)])
        kxp = jnp.where(rows_f == 31, k, f_k[j, pl.ds(9, 32)])
        kym = jnp.where(y_first, k, y_before(f_k, j, own_f, lanes, 32))
        kyp = jnp.where(y_last, k, y_beyond(f_k, j, own_f, lanes, 32))
        kzm = jnp.where(z_first, k, roll(k, 1))
        kzp = jnp.where(z_last, k, roll(k, 127))
        f_wx[j, own_f] = jnp.where(rows_f == 0, 0.0, 0.5 * (k + kxm))
        f_wy[j, own_f] = jnp.where(y_first, 0.0, 0.5 * (k + kym))
        f_wz[j, own_f] = jnp.where(z_first, 0.0, 0.5 * (k + kzm))
        f_inv[j, own_f] = 1.0 / (3.0 * k + 0.5 * (kxm + kxp + kym + kyp + kzm + kzp))
        return carry

    lax.fori_loop(0, 8, fine_weights, 0)
    w_f = (f_wx, f_wy, f_wz)

    def fine_base(i, carry):
        f_base[i + 1, own_f] = 0.25 * f_src[i] + coupled(f_v, w_f, i + 1, 8, 32, lanes, 32)
        return carry

    lax.fori_loop(0, 8, fine_base, 0)

    for copy in layer:
        copy.wait_recv()
    for ref in (s_fr, kq_fr):

        @pl.when(mx == 0)
        def _():
            ref[1:9, 7:8] = jnp.zeros((8, 1, 128), F32)

        @pl.when(mx == N_X - 1)
        def _():
            ref[1:9, 40:41] = jnp.zeros((8, 1, 128), F32)

        @pl.when(my == 0)
        def _():
            ref[0, 8:40] = jnp.zeros((32, 128), F32)

        @pl.when(my == N_Y - 1)
        def _():
            ref[9, 8:40] = jnp.zeros((32, 128), F32)

    for ox in range(2):
        for oy in range(2):
            for q in range(4):
                for at, row in ((q, 7 + 16 * ox), (4 + q, 24 + 16 * ox)):
                    x_rows[2 * ox + oy, at : at + 1] = s_fr[1 + 4 * oy + q, row : row + 1]
    for oz in range(2):
        pair = [(0, oz), (1, 1 - oz)]
        stacked = []
        for ox, oy in pair:
            rows = pl.ds(8 + 16 * ox, 16)
            parts = [s_fr[4 * oy, rows], s_fr[5 + 4 * oy, rows]]
            parts += [s_fr[1 + 4 * oy + q, rows] for q in range(4)]
            parts.append(x_rows[2 * ox + oy])
            stacked.append(jnp.concatenate(parts, axis=1))
        packed = mapped(jnp.concatenate(stacked, axis=0), m_face[oz])
        for number, (ox, oy) in enumerate(pair):
            faces[2 * ox + oy] = packed[16 * number : 16 * number + 16]

    def to_mates(source, target, send_sem, recv_sem):
        started = []
        for d in range(1, N_X):
            other = lax.rem(mx + d, N_X)
            started.append(
                remote(source(other), target.at[mx], send_sem.at[d], recv_sem.at[d], (other, my))
            )
        return started

    for h in range(N_X):
        ghost_out[h] = faces[octs[h]]
    ghosts = to_mates(lambda other: ghost_out.at[other], ghost_in, sem_s1, sem_r1)
    ghost_in[mx] = ghost_out[mx]

    for copy in loads[5]:
        copy.wait()

    def coarse_residual(i, carry):
        j = i + 1
        s = s_fr[j, own_f]
        k = kq_fr[j, own_f]

        def flux(k_there, s_there):
            return (k + k_there) * (s - s_there)

        before, beyond = pl.ds(7, 32), pl.ds(9, 32)
        total = flux(kq_fr[j, before], s_fr[j, before]) + flux(kq_fr[j, beyond], s_fr[j, beyond])
        total = total + flux(
            y_before(kq_fr, j, own_f, lanes, 32), y_before(s_fr, j, own_f, lanes, 32)
        )
        total = total + flux(
            y_beyond(kq_fr, j, own_f, lanes, 32), y_beyond(s_fr, j, own_f, lanes, 32)
        )
        total = total + flux(
            jnp.where(z_first, 0.0, roll(k, 1)), jnp.where(z_first, 0.0, roll(s, 1))
        )
        total = total + flux(
            jnp.where(z_last, 0.0, roll(k, 127)), jnp.where(z_last, 0.0, roll(s, 127))
        )
        r_fr[i + 5, pl.ds(24, 32)] = src_c[i] - 0.5 * total
        return carry

    lax.fori_loop(0, 8, coarse_residual, 0)
    deep_r = deep_x(r_fr, 16, sem_sr, sem_rr)

    for copy in deep_k:
        copy.wait_recv()

    @pl.when(mx == 0)
    def _():
        k_fr[5:13, 7:24] = jnp.zeros((8, 17, 128), F32)

    @pl.when(mx == N_X - 1)
    def _():
        k_fr[5:13, 56:73] = jnp.zeros((8, 17, 128), F32)

    deep_k += deep_y(k_fr, 5, sem_sk, sem_rk)

    k = iota((128, 1280), 0)
    c = iota((128, 1280), 1)
    y, z = c // 32, c % 32
    inner = c < 1024
    mask = inner & (y == 0) & (k == z // 2)
    mask = mask | (inner & (y == 31) & (k == 16 + z // 2))
    mask = mask | (inner & (z == 0) & (k == 32 + y // 2))
    mask = mask | (inner & (z == 31) & (k == 48 + y // 2))
    mask = mask | ((c >= 1024) & (k == 64 + (y - 32) // 2 * 16 + z // 2))
    put(m_ghost, mask)
    k, c = iota((512, 128), 0), iota((512, 128), 1)
    put(m_down, c == k // 64 * 16 + k % 32 // 2)

    for copy in ghosts:
        copy.wait_recv()
    mine = ghost_in[owner_x]
    dup[0, pl.ds(0, 16, stride=2)] = mine
    dup[0, pl.ds(1, 16, stride=2)] = mine
    widened = mapped(dup[0], m_ghost[...])
    for q in range(4):
        for t in range(2):
            piece = widened[:, 1024 + 128 * t : 1152 + 128 * t]
            f_gx[2 * q + t, 0:1] = piece[2 * q : 2 * q + 1]
            f_gx[2 * q + t, 31:32] = piece[8 + 2 * q : 9 + 2 * q]
    for i in range(8):
        j = i + 1
        ghost = f_k[j, own_f] * (widened[:, 128 * i : 128 * i + 128] + f_gx[i])
        f_gx[i] = ghost
        f_a[j, own_f] = jnp.where(first_f, (f_base[j, own_f] + ghost) * f_inv[j, own_f], 0.0)
    for i in range(8):
        j = i + 1
        around_a = coupled(f_a, w_f, j, 8, 32, lanes, 32)
        fresh = (0.25 * f_src[i] + f_gx[i] + around_a) * f_inv[j, own_f]
        f_sm[i] = jnp.where(first_f, f_a[j, own_f], fresh)
        f_d[j, own_f] = jnp.where(first_f, 0.0, fresh - f_v[j, own_f])
    for i in range(8):
        f_res[i] = jnp.where(first_f, coupled(f_d, w_f, i + 1, 8, 32, lanes, 32), 0.0)
    stacked = []
    for b in range(2):
        parts = [
            f_res[4 * b + q, pl.ds(0, 16, stride=2)] + f_res[4 * b + q, pl.ds(1, 16, stride=2)]
            for q in range(4)
        ]
        stacked.append(jnp.concatenate(parts, axis=1))
    packed = 0.5 * mapped(jnp.concatenate(stacked, axis=0), m_down[...])
    box_out[0] = packed[:16]
    box_out[1] = packed[16:]
    gathered = to_mates(lambda other: box_out, box_in, sem_s2, sem_r2)
    box_in[mx] = box_out[...]
    for copy in deep_r:
        copy.wait_recv()
    deep_r += deep_y(r_fr, 4, sem_sr, sem_rr)

    zero_pads(wx, 8, 72)
    zero_pads(wy, 8, 72)
    zero_pads(e_a, 8, 72)
    zero_pads(e_b, 8, 72)
    for ref in (b_k, b_wx, b_wy, b_ua, b_ub):
        zero_pads(ref, 8, 40)
    for oz in range(2):
        k, c = iota((128, 256), 0), iota((128, 256), 1)
        m_exp[oz] = jnp.where((k // 16 == c // 32) & (c % 32 == 16 * oz + k % 16), 1.0, 0.0).astype(BF16)
        k, c = iota((256, 128), 1), iota((256, 128), 0)
        m_com[oz] = jnp.where((k // 16 == c // 32) & (c % 32 == 16 * oz + k % 16), 1.0, 0.0).astype(BF16)
    k, c = iota((128, 512), 0), iota((128, 512), 1)
    put(m_up, k == c // 64 * 16 + c % 32 // 2)
    k, c = iota((128, 1024), 0), iota((128, 1024), 1)
    put(m_four, k == c // 128 * 16 + c % 32 // 4)

    for copy in deep_k:
        copy.wait_recv()
    @pl.when(my == 0)
    def _():
        k_fr[0:5] = jnp.zeros((5, 80, 128), F32)

    @pl.when(my == N_Y - 1)
    def _():
        k_fr[13:18] = jnp.zeros((5, 80, 128), F32)

    window = pl.ds(8, 64)

    def coarse_weights(i, carry):
        j = i + 1
        k = k_fr[j, window]
        kxm = k_fr[j, pl.ds(7, 64)]
        kxp = k_fr[j, pl.ds(9, 64)]
        kym = y_before(k_fr, j, window, lanes, 32)
        kyp = y_beyond(k_fr, j, window, lanes, 32)
        kzm = jnp.where(z_first, 0.0, roll(k, 1))
        kzp = jnp.where(z_last, 0.0, roll(k, 127))
        wx[j, window] = 0.5 * (k + kxm)
        wy[j, window] = 0.5 * (k + kym)
        wz[j, window] = jnp.where(z_first, 0.0, 0.5 * (k + kzm))
        inverse = 1.0 / (3.0 * k + 0.5 * (kxm + kxp + kym + kyp + kzm + kzp))
        inverse = jnp.where(k > 0.0, inverse, 0.0)
        inv_a[j, window] = jnp.where(first_c, inverse, 0.0)
        inv_b[j, window] = jnp.where(first_c, 0.0, inverse)
        return carry

    lax.fori_loop(0, 16, coarse_weights, 0)
    w_c = (wx, wy, wz)

    def coarsened(ref):
        stacked = []
        for b in range(4):
            parts = [
                ref[1 + 4 * b + q, pl.ds(8, 32, stride=2)]
                + ref[1 + 4 * b + q, pl.ds(9, 32, stride=2)]
                for q in range(4)
            ]
            stacked.append(jnp.concatenate(parts, axis=1))
        return mapped(jnp.concatenate(stacked, axis=0), m_down[...])

    summed = coarsened(k_fr)
    own_b = pl.ds(8, 32)
    for b in range(4):
        b_k[1 + b, own_b] = 0.125 * summed[32 * b : 32 * b + 32]
    zb_first = lanes % 16 == 0
    zb_last = lanes % 16 == 15
    for b in range(4):
        j = b + 1
        k = b_k[j, own_b]
        kxm = b_k[j, pl.ds(7, 32)]
        kxp = b_k[j, pl.ds(9, 32)]
        kym = y_before(b_k, j, own_b, lanes, 16)
        kyp = y_beyond(b_k, j, own_b, lanes, 16)
        kzm = jnp.where(zb_first, 0.0, roll(k, 1))
        kzp = jnp.where(zb_last, 0.0, roll(k, 127))
        b_wx[j, own_b] = 0.5 * (k + kxm)
        b_wy[j, own_b] = 0.5 * (k + kym)
        b_wz[j, own_b] = jnp.where(zb_first, 0.0, 0.5 * (k + kzm))
        inverse = 1.0 / (3.0 * k + 0.5 * (kxm + kxp + kym + kyp + kzm + kzp))
        inverse = jnp.where(k > 0.0, inverse, 0.0)
        b_ia[b] = jnp.where(first_b, inverse, 0.0)
        b_ib[b] = jnp.where(first_b, 0.0, inverse)

    for copy in deep_r:
        copy.wait_recv()
    for copy in deep_r:
        copy.wait_send()

    for copy in gathered:
        copy.wait_recv()
    for ye in (1, 2):
        for sx in range(4):
            boxes[ye, sx] = box_in[jnp.maximum(found[4 * ye + sx], 0)]
    beside = [
        remote(boxes.at[1], boxes.at[3], sem_s3.at[0], sem_r3.at[0], around[2]),
        remote(boxes.at[2], boxes.at[0], sem_s3.at[1], sem_r3.at[1], around[3]),
    ]

    def compose(ye):
        for oz in range(2):
            pair = [sx for sx in range(4) if (sx + ye) % 2 == oz]
            stacked = [boxes[ye, sx, b] for sx in pair for b in range(2)]
            wide = mapped(jnp.concatenate(stacked, axis=0), m_exp[oz])
            for number, sx in enumerate(pair):
                here = jnp.where(found[4 * ye + sx] >= 0, 1.0, 0.0)
                covered = jnp.where(lanes % 32 // 16 == oz, here, 0.0) > 0.5
                rows = pl.ds(8 + 16 * sx, 16)
                for q in range(4):
                    b, t = q // 2, q % 2
                    j = 1 + 4 * ye + q
                    at = 32 * number + 16 * b
                    part = wide[at : at + 16, 128 * t : 128 * t + 128]
                    mixed = jnp.where(covered, part, r_fr[j, rows])
                    r_fr[j, rows] = mixed
                    e_a[j, rows] = mixed * inv_a[j, rows]

    compose(1)
    compose(2)
    for copy in beside:
        copy.wait_recv()
    compose(0)
    compose(3)

    def second(i, carry):
        j = i + 1
        fresh = r_fr[j, window] + coupled(e_a, w_c, j, 8, 64, lanes, 32)
        e_b[j, window] = fresh * inv_b[j, window]
        return carry

    lax.fori_loop(0, 16, second, 0, unroll=2)

    own_c = pl.ds(24, 32)
    for oz in range(2):
        pair = [(0, oz), (1, 1 - oz)]
        stacked = []
        for ox, oy in pair:
            rows = pl.ds(24 + 16 * ox, 16)
            for b in range(2):
                parts = [
                    e_a[5 + 4 * oy + 2 * b + t, rows] + e_b[5 + 4 * oy + 2 * b + t, rows]
                    for t in range(2)
                ]
                stacked.append(jnp.concatenate(parts, axis=1))
        packed = mapped(jnp.concatenate(stacked, axis=0), m_com[oz])
        for number, (ox, oy) in enumerate(pair):
            for b in range(2):
                at = 32 * number + 16 * b
                e_oct[2 * ox + oy, b] = packed[at : at + 16]
    for h in range(N_X):
        e_out[h] = e_oct[octs[h]]
    returned = to_mates(lambda other: e_out.at[other], e_in, sem_s4, sem_r4)
    e_in[mx] = e_out[mx]

    def remaining(i, carry):
        j = i + 1
        left[j, window] = jnp.where(first_c, coupled(e_b, w_c, j, 8, 64, lanes, 32), 0.0)
        return carry

    lax.fori_loop(0, 16, remaining, 0, unroll=2)
    summed = 0.5 * coarsened(left)
    for b in range(4):
        source = summed[32 * b : 32 * b + 32]
        b_fa[b] = source * b_ia[b]
        b_fb[b] = source * b_ib[b]
        b_ua[1 + b, own_b] = source * b_ia[b]
    w_b = (b_wx, b_wy, b_wz)
    for half in range(2 * SWEEPS - 1):
        into, out_of = ((b_ub, b_ua), (b_ua, b_ub))[half % 2]
        fixed, inverse = ((b_fb, b_ib), (b_fa, b_ia))[half % 2]
        for b in range(4):
            into[1 + b, own_b] = fixed[b] + inverse[b] * coupled(
                out_of, w_b, 1 + b, 8, 32, lanes, 16
            )

    for ox in range(2):
        for oy in range(2):
            rows = pl.ds(16 + 8 * ox, 8)
            u_oct[2 * ox + oy] = b_ua[2 + oy, rows] + b_ub[2 + oy, rows]
    for h in range(N_X):
        u_out[h] = u_oct[octs[h]]
    settled = to_mates(lambda other: u_out.at[other], u_in, sem_s5, sem_r5)
    u_in[mx] = u_out[mx]

    def doubled(ref, pieces):
        for b, piece in enumerate(pieces):
            ref[b, pl.ds(0, 16, stride=2)] = piece
            ref[b, pl.ds(1, 16, stride=2)] = piece
        return mapped(jnp.concatenate([ref[0], ref[1]], axis=0), m_up[...])

    wide = doubled(dup, [b_ua[2 + b, pl.ds(16, 16)] + b_ub[2 + b, pl.ds(16, 16)] for b in range(2)])
    for j in range(8):
        b, q = j // 4, j % 4
        part = wide[32 * b : 32 * b + 32, 128 * q : 128 * q + 128]
        total = e_a[5 + j, own_c] + e_b[5 + j, own_c] + part
        out_c[:, 128 * j : 128 * j + 128] = s_fr[1 + j, own_f] + total

    for copy in returned:
        copy.wait_recv()
    got = e_in.at[owner_x]
    wide = doubled(dup2, [got[0], got[1]])
    for j in range(8):
        b, q = j // 4, j % 4
        f_sm[j] = f_sm[j] + wide[32 * b : 32 * b + 32, 128 * q : 128 * q + 128]
    for copy in settled:
        copy.wait_recv()
    tile = u_in[owner_x]
    side = jnp.where(own_oz == 1, 1.0, 0.0)
    tile = jnp.where(jnp.zeros((8, 128), F32) + side > 0.5, roll(tile, 120), tile)
    for t in range(4):
        dup[0, pl.ds(t, 8, stride=4)] = tile
    wide = mapped(dup[0], m_four[...])
    for j in range(8):
        out_f[0, :, 128 * j : 128 * j + 128] = f_sm[j] + wide[:, 128 * j : 128 * j + 128]

    for copy in sends:
        copy.wait_send()


def scratch():
    v = pltpu.VMEM
    shapes = [(10, 48, 128)] * 2 + [(8, 32, 128)]
    shapes += [(8, 32, 128)] + [(10, 48, 128)] * 8 + [(8, 32, 128), (10, 48, 128)]
    shapes += [(8, 32, 128)] * 2
    shapes += [(18, 80, 128)] * 10
    shapes += [(6, 48, 128)] * 4 + [(4, 32, 128)] * 4 + [(6, 48, 128)] * 2
    shapes += [(4, 16, 128), (4, 16, 128), (N_X, 16, 128), (N_X, 16, 128)]
    shapes += [(2, 16, 128), (N_X, 2, 16, 128), (4, 4, 2, 16, 128)]
    shapes += [(4, 2, 16, 128), (N_X, 2, 16, 128), (N_X, 2, 16, 128)]
    shapes += [(4, 8, 128), (N_X, 8, 128), (N_X, 8, 128)]
    shapes += [(2, 32, 128)] * 2
    result = [v(shape, F32) for shape in shapes]
    maps = [(2, 896, 128), (128, 1280), (512, 128), (128, 512), (2, 128, 256), (2, 256, 128)]
    result += [v(shape, BF16) for shape in maps + [(128, 1024)]]
    dma = pltpu.SemaphoreType.DMA
    result += [dma((7, 8))] + [dma((8,))] * 2 + [dma((12,))] * 4 + [dma((N_X,))] * 4 + [dma((2,))] * 2
    return result + [dma((N_X,))] * 4


def on_device(
    coarse_source,
    coarse_coefficient,
    coarse_start,
    fine_source,
    fine_coefficient,
    fine_start,
    fine_position,
    first_colour,
):
    smem = pl.BlockSpec(memory_space=pltpu.SMEM)
    vmem = pl.BlockSpec(memory_space=pltpu.VMEM)
    hbm = pl.BlockSpec(memory_space=pltpu.HBM)
    return pl.pallas_call(
        kernel,
        out_shape=(
            jax.ShapeDtypeStruct(coarse_start.shape, F32),
            jax.ShapeDtypeStruct(fine_start.shape, F32),
        ),
        in_specs=[smem, smem] + [hbm] * 6,
        out_specs=(vmem, vmem),
        scratch_shapes=scratch(),
        compiler_params=pltpu.CompilerParams(
            collective_id=0, has_side_effects=True, vmem_limit_bytes=48 << 20
        ),
    )(
        *[
            pltpu.with_memory_space_constraint(array, pltpu.HBM)
            for array in (
                fine_position,
                first_colour,
                coarse_source,
                coarse_coefficient,
                coarse_start,
                fine_source,
                fine_coefficient,
                fine_start,
            )
        ],
    )


def solution(mesh):
    placed = (
        P("gx", "gy"),
        P("gx", "gy"),
        P("gx", "gy"),
        P(("gx", "gy"), None, None),
        P(("gx", "gy"), None, None),
        P(("gx", "gy"), None, None),
        P(),
        P(),
    )
    return jax.shard_map(
        on_device,
        mesh=mesh,
        in_specs=placed,
        out_specs=(P("gx", "gy"), P(("gx", "gy"), None, None)),
        check_vma=False,
    )
```

```python
import functools

import jax
import jax.numpy as jnp
from jax import lax
from jax.experimental import pallas as pl
from jax.experimental.pallas import tpu as pltpu
from jax.sharding import PartitionSpec as P


MESH = pl.DeviceIdType.MESH
F32 = jnp.float32
BF16 = jnp.bfloat16
SWEEPS = 4
N_X = 16
N_Y = 8


def iota(shape, dim):
    return lax.broadcasted_iota(jnp.int32, shape, dim)


def halves(values):
    high = values.astype(BF16)
    low = (values - high.astype(F32)).astype(BF16)
    return jnp.concatenate([high, low], axis=0)


def mapped(values, matrix):
    rows = values.shape[0]
    both = jnp.dot(halves(values), matrix, preferred_element_type=F32)
    return both[:rows] + both[rows:]


def roll(values, amount):
    return pltpu.roll(values, amount, axis=1)


def y_before(ref, j, rows, lanes, step):
    return roll(jnp.where(lanes >= 128 - step, ref[j - 1, rows], ref[j, rows]), step)


def y_beyond(ref, j, rows, lanes, step):
    return roll(jnp.where(lanes < step, ref[j + 1, rows], ref[j, rows]), 128 - step)


def coupled(value, weights, j, low, count, lanes, step):
    wx, wy, wz = weights
    here = pl.ds(low, count)
    before = pl.ds(low - 1, count)
    beyond = pl.ds(low + 1, count)
    mid = value[j, here]
    w_y = wy[j, here]
    w_z = wz[j, here]
    total = wx[j, here] * value[j, before] + wx[j, beyond] * value[j, beyond]
    total = total + w_y * y_before(value, j, here, lanes, step)
    ahead = jnp.where(lanes < step, wy[j + 1, here] * value[j + 1, here], w_y * mid)
    total = total + roll(ahead, 128 - step)
    return total + w_z * roll(mid, 1) + roll(w_z * mid, 127)


def zero_pads(ref, low, high):
    blocks, rows, _ = ref.shape
    ref[0] = jnp.zeros((rows, 128), F32)
    ref[blocks - 1] = jnp.zeros((rows, 128), F32)
    ref[1 : blocks - 1, :low] = jnp.zeros((blocks - 2, low, 128), F32)
    ref[1 : blocks - 1, high:] = jnp.zeros((blocks - 2, rows - high, 128), F32)


class Remote:
    def __init__(self, copy):
        self.copy = copy
        self.landed = False
        self.left = False
        copy.start()

    def wait_recv(self):
        if not self.landed:
            self.copy.wait_recv()
        self.landed = True

    def wait_send(self):
        if not self.left:
            self.copy.wait_send()
        self.left = True


def put(ref, mask):
    ref[...] = jnp.where(mask, 1.0, 0.0).astype(BF16)


def kernel(
    pos_hbm,
    colours_hbm,
    c_source,
    c_coeff,
    c_start,
    f_source,
    f_coeff,
    f_start,
    out_c,
    out_f,
    pos,
    colours,
    s_fr,
    kq_fr,
    src_c,
    f_src,
    f_k,
    f_v,
    f_wx,
    f_wy,
    f_wz,
    f_inv,
    f_base,
    f_a,
    f_sm,
    f_d,
    f_res,
    f_gx,
    k_fr,
    r_fr,
    wx,
    wy,
    wz,
    inv_a,
    inv_b,
    e_a,
    e_b,
    left,
    b_k,
    b_wx,
    b_wy,
    b_wz,
    b_ia,
    b_ib,
    b_fa,
    b_fb,
    b_ua,
    b_ub,
    x_rows,
    faces,
    ghost_out,
    ghost_in,
    box_out,
    box_in,
    boxes,
    e_oct,
    e_out,
    e_in,
    u_oct,
    u_out,
    u_in,
    dup,
    dup2,
    m_face,
    m_ghost,
    m_down,
    m_up,
    m_exp,
    m_com,
    m_four,
    sem_l,
    sem_s0,
    sem_r0,
    sem_sk,
    sem_rk,
    sem_sr,
    sem_rr,
    sem_s1,
    sem_r1,
    sem_s2,
    sem_r2,
    sem_s3,
    sem_r3,
    sem_s4,
    sem_r4,
    sem_s5,
    sem_r5,
):
    mx = lax.axis_index("gx")
    my = lax.axis_index("gy")
    x_up, x_dn = lax.rem(mx + 1, N_X), lax.rem(mx + N_X - 1, N_X)
    y_up, y_dn = lax.rem(my + 1, N_Y), lax.rem(my + N_Y - 1, N_Y)
    around = [
        (x_dn, my),
        (x_up, my),
        (mx, y_dn),
        (mx, y_up),
    ]
    mates = [(lax.rem(mx + d, N_X), my) for d in range(1, N_X)]

    barrier = pltpu.get_barrier_semaphore()
    greeted = mates + around[2:]
    for device in greeted:
        pl.semaphore_signal(barrier, inc=1, device_id=device, device_id_type=MESH)

    loads = [
        [
            pltpu.make_async_copy(pos_hbm, pos, sem_l.at[7, 0]),
            pltpu.make_async_copy(colours_hbm, colours, sem_l.at[7, 1]),
        ]
    ]
    for copy in loads[0]:
        copy.start()

    def load(number, source, target):
        group = []
        for j in range(8):
            copy = pltpu.make_async_copy(source(j), target(j), sem_l.at[number, j])
            copy.start()
            group.append(copy)
        loads.append(group)

    def chunk(j):
        return pl.ds(128 * j, 128)

    load(0, lambda j: c_start.at[:, chunk(j)], lambda j: s_fr.at[1 + j, pl.ds(8, 32)])
    load(1, lambda j: c_coeff.at[:, chunk(j)], lambda j: kq_fr.at[1 + j, pl.ds(8, 32)])
    load(2, lambda j: f_coeff.at[0, :, chunk(j)], lambda j: f_k.at[1 + j, pl.ds(8, 32)])
    load(3, lambda j: f_start.at[0, :, chunk(j)], lambda j: f_v.at[1 + j, pl.ds(8, 32)])
    load(4, lambda j: f_source.at[0, :, chunk(j)], lambda j: f_src.at[j])
    load(5, lambda j: c_source.at[:, chunk(j)], lambda j: src_c.at[j])
    load(6, lambda j: c_coeff.at[:, chunk(j)], lambda j: k_fr.at[5 + j, pl.ds(24, 32)])

    for q in range(5):
        for j in (4 - q, 13 + q):
            for low, high in ((0, 8 + 4 * q), (72 - 4 * q, 80)):
                k_fr[j, low:high] = jnp.zeros((high - low, 128), F32)
                r_fr[j, low:high] = jnp.zeros((high - low, 128), F32)
    for copy in loads[0]:
        copy.wait()
    own_pos = pos[mx * N_Y + my]
    owner_x = own_pos >> 6
    own_oz = own_pos & 1

    slots = []
    for ye in range(4):
        row = (my, y_dn, y_up)[1 if ye == 0 else (2 if ye == 3 else 0)]
        for sx in range(4):
            ox, oy = (sx + 1) % 2, (ye + 1) % 2
            octant = 4 * ox + 2 * oy + (ox + oy) % 2
            column = mx + (-1, 0, 0, 1)[sx]
            slots.append((row, (column * N_Y + row) * 8 + octant))

    def look(h, found):
        held = [pos[h * N_Y + row] for row in (my, y_dn, y_up)]
        result = []
        for number, (row, wanted) in enumerate(slots):
            ye = number // 4
            at = held[1 if ye == 0 else (2 if ye == 3 else 0)]
            result.append(jnp.where(at == wanted, h, found[number]))
        return tuple(result)

    found = lax.fori_loop(0, N_X, look, tuple(jnp.int32(-1) for _ in slots))
    octs, picks = [], []
    for h in range(N_X):
        at = pos[h * N_Y + my]
        octant, away = (at >> 1) & 3, (at >> 6) - mx
        pick = jnp.where((away == 1) & (octant < 2), 4 + octant, 0)
        pick = jnp.where((away == -1) & (octant >= 2), 4 + octant, pick)
        octs.append(octant)
        picks.append(jnp.where(away == 0, octant, pick))

    lanes = iota((1, 128), 1)
    z_first = lanes % 32 == 0
    z_last = lanes % 32 == 31
    parity = (iota((8, 128), 0) + iota((8, 128), 1) // 32 + iota((8, 128), 1)) % 2
    parity_b = (iota((8, 128), 0) + iota((8, 128), 1) // 16 + iota((8, 128), 1)) % 2

    def painted(base, colour, rows):
        flags = jnp.where(base == colour, 1.0, 0.0)
        return jnp.concatenate([flags] * (rows // 8), axis=0) > 0.5

    first_f = painted(parity, colours[0], 32)
    first_c = painted(parity, colours[1], 64)
    first_b = painted(parity_b, colours[2], 32)

    zero_pads(f_v, 8, 40)
    zero_pads(f_wx, 8, 40)
    zero_pads(f_wy, 8, 40)
    zero_pads(f_a, 8, 40)
    zero_pads(f_d, 8, 40)
    x_rows[...] = jnp.zeros(x_rows.shape, F32)
    f_gx[...] = jnp.zeros(f_gx.shape, F32)

    for oz in range(2):
        k = iota((896, 128), 0)
        c = iota((896, 128), 1)
        block, lane = k // 128, k % 128
        z, yy = lane % 32, lane // 32
        mask = (block == 0) & (c < 16) & (lane == 96 + 16 * oz + c)
        mask = mask | ((block == 1) & (c >= 16) & (c < 32) & (lane == 16 * oz + c - 16))
        own = (block >= 2) & (block < 6) & (z == (16, 15)[oz])
        mask = mask | (own & (c == (48, 32)[oz] + 4 * (block - 2) + yy))
        mask = mask | (
            (block == 6) & (z >= 16 * oz) & (z < 16 * oz + 16) & (c == 64 + yy * 16 + z - 16 * oz)
        )
        m_face[oz] = jnp.where(mask, 1.0, 0.0).astype(BF16)

    for group in loads[1:3]:
        for copy in group:
            copy.wait()

    for ox in range(2):
        for oy in range(2):
            own, at = (24, 4) if ox == 0 else (23, 0)
            far, at_far = (39, 0) if ox == 0 else (8, 4)
            for q in range(4):
                j = 1 + 4 * oy + q
                x_rows[2 * ox + oy, at + q : at + q + 1] = s_fr[j, own : own + 1]
                x_rows[4 + 2 * ox + oy, at_far + q : at_far + q + 1] = s_fr[j, far : far + 1]
    blank = jnp.zeros((16, 128), F32)
    for oz in range(2):
        pair = [(0, oz), (1, 1 - oz)]
        stacked = []
        for ox, oy in pair:
            rows = pl.ds(8 + 16 * ox, 16)
            parts = [s_fr[4, rows], blank] if oy else [blank, s_fr[5, rows]]
            parts += [s_fr[1 + 4 * oy + q, rows] for q in range(4)]
            parts.append(x_rows[2 * ox + oy])
            stacked.append(jnp.concatenate(parts, axis=1))
        for ox, oy in pair:
            stacked.append(jnp.concatenate([blank] * 6 + [x_rows[4 + 2 * ox + oy]], axis=1))
        packed = mapped(jnp.concatenate(stacked, axis=0), m_face[oz])
        for number, (ox, oy) in enumerate(pair):
            faces[2 * ox + oy] = packed[16 * number : 16 * number + 16]
            faces[4 + 2 * ox + oy] = packed[32 + 16 * number : 48 + 16 * number]
    pl.semaphore_wait(barrier, len(greeted))

    sends = []

    def remote(source, target, send_sem, recv_sem, device):
        copy = Remote(
            pltpu.make_async_remote_copy(
                src_ref=source,
                dst_ref=target,
                send_sem=send_sem,
                recv_sem=recv_sem,
                device_id=device,
                device_id_type=MESH,
            )
        )
        sends.append(copy)
        return copy

    layer = []
    for number, ref in enumerate((s_fr, kq_fr)):
        rows, blocks = pl.ds(8, 32), pl.ds(1, 8)
        for side, (source, target, device) in enumerate(
            (
                (ref.at[8, rows], ref.at[0, rows], around[3]),
                (ref.at[1, rows], ref.at[9, rows], around[2]),
                (ref.at[blocks, pl.ds(39, 1)], ref.at[blocks, pl.ds(7, 1)], around[1]),
                (ref.at[blocks, pl.ds(8, 1)], ref.at[blocks, pl.ds(40, 1)], around[0]),
            )
        ):
            at = 4 * number + side
            layer.append(remote(source, target, sem_s0.at[at], sem_r0.at[at], device))

    for copy in loads[7]:
        copy.wait()

    def deep_x(ref, width, send_sem, recv_sem):
        blocks = pl.ds(5, 8)
        started = []
        for side, (source, target) in enumerate(((24, 56), (56 - width, 24 - width))):
            started.append(
                remote(
                    ref.at[blocks, pl.ds(source, width)],
                    ref.at[blocks, pl.ds(target, width)],
                    send_sem.at[side],
                    recv_sem.at[side],
                    around[side],
                )
            )
        return started

    def deep_y(ref, depth, send_sem, recv_sem):
        started = []
        for q in range(depth):
            rows = pl.ds(8 + 4 * q, 64 - 8 * q)
            for side, (source, target) in enumerate(((5 + q, 13 + q), (12 - q, 4 - q))):
                at = 2 + 2 * q + side
                started.append(
                    remote(
                        ref.at[source, rows],
                        ref.at[target, rows],
                        send_sem.at[at],
                        recv_sem.at[at],
                        around[2 + side],
                    )
                )
        return started

    deep_k = deep_x(k_fr, 17, sem_sk, sem_rk)

    for group in loads[3:6]:
        for copy in group:
            copy.wait()
    rows_f = iota((32, 128), 0)
    own_f = pl.ds(8, 32)

    def fine_weights(i, carry):
        j = i + 1
        k = f_k[j, own_f]
        y_first = (lanes < 32) & (j == 1)
        y_last = (lanes >= 96) & (j == 8)
        kxm = jnp.where(rows_f == 0, k, f_k[j, pl.ds(7, 32)])
        kxp = jnp.where(rows_f == 31, k, f_k[j, pl.ds(9, 32)])
        kym = jnp.where(y_first, k, y_before(f_k, j, own_f, lanes, 32))
        kyp = jnp.where(y_last, k, y_beyond(f_k, j, own_f, lanes, 32))
        kzm = jnp.where(z_first, k, roll(k, 1))
        kzp = jnp.where(z_last, k, roll(k, 127))
        f_wx[j, own_f] = jnp.where(rows_f == 0, 0.0, 0.5 * (k + kxm))
        f_wy[j, own_f] = jnp.where(y_first, 0.0, 0.5 * (k + kym))
        f_wz[j, own_f] = jnp.where(z_first, 0.0, 0.5 * (k + kzm))
        f_inv[j, own_f] = 1.0 / (3.0 * k + 0.5 * (kxm + kxp + kym + kyp + kzm + kzp))
        return carry

    lax.fori_loop(0, 8, fine_weights, 0)
    w_f = (f_wx, f_wy, f_wz)

    def fine_base(i, carry):
        f_base[i + 1, own_f] = 0.25 * f_src[i] + coupled(f_v, w_f, i + 1, 8, 32, lanes, 32)
        return carry

    lax.fori_loop(0, 8, fine_base, 0)

    for copy in layer[:2]:
        copy.wait_recv()

    def blank_sides(ref):
        @pl.when(my == 0)
        def _():
            ref[0, 8:40] = jnp.zeros((32, 128), F32)

        @pl.when(my == N_Y - 1)
        def _():
            ref[9, 8:40] = jnp.zeros((32, 128), F32)

    blank_sides(s_fr)

    for ox in range(2):
        for oy in range(2):
            rows = pl.ds(8 + 16 * ox, 16)
            oz = (ox + oy) % 2
            shift = (128 - 96 - 16 * oz, 16 - 16 * oz)[oy] % 128
            beside = s_fr[9 * oy, rows]
            if shift:
                beside = roll(beside, shift)
            wanted = (lanes >= 16 * oy) & (lanes < 16 * oy + 16)
            faces[2 * ox + oy] = faces[2 * ox + oy] + jnp.where(wanted, beside, 0.0)

    def to_mates(source, target, send_sem, recv_sem):
        started = []
        for d in range(1, N_X):
            other = lax.rem(mx + d, N_X)
            started.append(
                remote(source(other), target.at[mx], send_sem.at[d], recv_sem.at[d], (other, my))
            )
        return started

    for h in range(N_X):
        ghost_out[h] = faces[picks[h]]
    ghosts = to_mates(lambda other: ghost_out.at[other], ghost_in, sem_s1, sem_r1)
    ghost_in[mx] = ghost_out[mx]

    for copy in layer:
        copy.wait_recv()
    blank_sides(kq_fr)
    for ref in (s_fr, kq_fr):

        @pl.when(mx == 0)
        def _():
            ref[1:9, 7:8] = jnp.zeros((8, 1, 128), F32)

        @pl.when(mx == N_X - 1)
        def _():
            ref[1:9, 40:41] = jnp.zeros((8, 1, 128), F32)

    for copy in loads[6]:
        copy.wait()

    def coarse_residual(i, carry):
        j = i + 1
        s = s_fr[j, own_f]
        k = kq_fr[j, own_f]

        def flux(k_there, s_there):
            return (k + k_there) * (s - s_there)

        before, beyond = pl.ds(7, 32), pl.ds(9, 32)
        total = flux(kq_fr[j, before], s_fr[j, before]) + flux(kq_fr[j, beyond], s_fr[j, beyond])
        total = total + flux(
            y_before(kq_fr, j, own_f, lanes, 32), y_before(s_fr, j, own_f, lanes, 32)
        )
        total = total + flux(
            y_beyond(kq_fr, j, own_f, lanes, 32), y_beyond(s_fr, j, own_f, lanes, 32)
        )
        total = total + flux(
            jnp.where(z_first, 0.0, roll(k, 1)), jnp.where(z_first, 0.0, roll(s, 1))
        )
        total = total + flux(
            jnp.where(z_last, 0.0, roll(k, 127)), jnp.where(z_last, 0.0, roll(s, 127))
        )
        r_fr[i + 5, pl.ds(24, 32)] = src_c[i] - 0.5 * total
        return carry

    lax.fori_loop(0, 8, coarse_residual, 0)
    deep_r = deep_x(r_fr, 16, sem_sr, sem_rr)

    for copy in deep_k:
        copy.wait_recv()

    @pl.when(mx == 0)
    def _():
        k_fr[5:13, 7:24] = jnp.zeros((8, 17, 128), F32)

    @pl.when(mx == N_X - 1)
    def _():
        k_fr[5:13, 56:73] = jnp.zeros((8, 17, 128), F32)

    deep_k += deep_y(k_fr, 5, sem_sk, sem_rk)

    k = iota((128, 1280), 0)
    c = iota((128, 1280), 1)
    y, z = c // 32, c % 32
    inner = c < 1024
    mask = inner & (y == 0) & (k == z // 2)
    mask = mask | (inner & (y == 31) & (k == 16 + z // 2))
    mask = mask | (inner & (z == 0) & (k == 32 + y // 2))
    mask = mask | (inner & (z == 31) & (k == 48 + y // 2))
    mask = mask | ((c >= 1024) & (k == 64 + (y - 32) // 2 * 16 + z // 2))
    put(m_ghost, mask)
    k, c = iota((512, 128), 0), iota((512, 128), 1)
    put(m_down, c == k // 64 * 16 + k % 32 // 2)

    for copy in ghosts:
        copy.wait_recv()
    high_x = (own_pos >> 2) & 1
    other_x = owner_x + 2 * high_x - 1
    beyond_x = ghost_in[jnp.clip(other_x, 0, N_X - 1)]
    inside = jnp.where((other_x >= 0) & (other_x < N_X), 1.0, 0.0)
    mine = ghost_in[owner_x] + inside * beyond_x
    dup[0, pl.ds(0, 16, stride=2)] = mine
    dup[0, pl.ds(1, 16, stride=2)] = mine
    widened = mapped(dup[0], m_ghost[...])
    for q in range(4):
        for t in range(2):
            piece = widened[:, 1024 + 128 * t : 1152 + 128 * t]
            f_gx[2 * q + t, 0:1] = piece[2 * q : 2 * q + 1]
            f_gx[2 * q + t, 31:32] = piece[8 + 2 * q : 9 + 2 * q]
    for i in range(8):
        j = i + 1
        ghost = f_k[j, own_f] * (widened[:, 128 * i : 128 * i + 128] + f_gx[i])
        f_gx[i] = ghost
        f_a[j, own_f] = jnp.where(first_f, (f_base[j, own_f] + ghost) * f_inv[j, own_f], 0.0)
    for i in range(8):
        j = i + 1
        around_a = coupled(f_a, w_f, j, 8, 32, lanes, 32)
        fresh = (0.25 * f_src[i] + f_gx[i] + around_a) * f_inv[j, own_f]
        f_sm[i] = jnp.where(first_f, f_a[j, own_f], fresh)
        f_d[j, own_f] = jnp.where(first_f, 0.0, fresh - f_v[j, own_f])
    for i in range(8):
        f_res[i] = jnp.where(first_f, coupled(f_d, w_f, i + 1, 8, 32, lanes, 32), 0.0)
    stacked = []
    for b in range(2):
        parts = [
            f_res[4 * b + q, pl.ds(0, 16, stride=2)] + f_res[4 * b + q, pl.ds(1, 16, stride=2)]
            for q in range(4)
        ]
        stacked.append(jnp.concatenate(parts, axis=1))
    packed = 0.5 * mapped(jnp.concatenate(stacked, axis=0), m_down[...])
    box_out[0] = packed[:16]
    box_out[1] = packed[16:]
    gathered = to_mates(lambda other: box_out, box_in, sem_s2, sem_r2)
    box_in[mx] = box_out[...]
    for copy in deep_r:
        copy.wait_recv()
    deep_r += deep_y(r_fr, 4, sem_sr, sem_rr)

    zero_pads(wx, 8, 72)
    zero_pads(wy, 8, 72)
    zero_pads(e_a, 8, 72)
    zero_pads(e_b, 8, 72)
    for ref in (b_k, b_wx, b_wy, b_ua, b_ub):
        zero_pads(ref, 8, 40)
    for oz in range(2):
        k, c = iota((128, 256), 0), iota((128, 256), 1)
        m_exp[oz] = jnp.where((k // 16 == c // 32) & (c % 32 == 16 * oz + k % 16), 1.0, 0.0).astype(BF16)
        k, c = iota((256, 128), 1), iota((256, 128), 0)
        m_com[oz] = jnp.where((k // 16 == c // 32) & (c % 32 == 16 * oz + k % 16), 1.0, 0.0).astype(BF16)
    k, c = iota((128, 512), 0), iota((128, 512), 1)
    put(m_up, k == c // 64 * 16 + c % 32 // 2)
    k, c = iota((128, 1024), 0), iota((128, 1024), 1)
    put(m_four, k == c // 128 * 16 + c % 32 // 4)

    for copy in deep_k:
        copy.wait_recv()
    @pl.when(my == 0)
    def _():
        k_fr[0:5] = jnp.zeros((5, 80, 128), F32)

    @pl.when(my == N_Y - 1)
    def _():
        k_fr[13:18] = jnp.zeros((5, 80, 128), F32)

    window = pl.ds(8, 64)

    def coarse_weights(i, carry):
        j = i + 1
        k = k_fr[j, window]
        kxm = k_fr[j, pl.ds(7, 64)]
        kxp = k_fr[j, pl.ds(9, 64)]
        kym = y_before(k_fr, j, window, lanes, 32)
        kyp = y_beyond(k_fr, j, window, lanes, 32)
        kzm = jnp.where(z_first, 0.0, roll(k, 1))
        kzp = jnp.where(z_last, 0.0, roll(k, 127))
        wx[j, window] = 0.5 * (k + kxm)
        wy[j, window] = 0.5 * (k + kym)
        wz[j, window] = jnp.where(z_first, 0.0, 0.5 * (k + kzm))
        inverse = 1.0 / (3.0 * k + 0.5 * (kxm + kxp + kym + kyp + kzm + kzp))
        inverse = jnp.where(k > 0.0, inverse, 0.0)
        inv_a[j, window] = jnp.where(first_c, inverse, 0.0)
        inv_b[j, window] = jnp.where(first_c, 0.0, inverse)
        return carry

    lax.fori_loop(0, 16, coarse_weights, 0)
    w_c = (wx, wy, wz)

    def coarsened(ref):
        stacked = []
        for b in range(4):
            parts = [
                ref[1 + 4 * b + q, pl.ds(8, 32, stride=2)]
                + ref[1 + 4 * b + q, pl.ds(9, 32, stride=2)]
                for q in range(4)
            ]
            stacked.append(jnp.concatenate(parts, axis=1))
        return mapped(jnp.concatenate(stacked, axis=0), m_down[...])

    summed = coarsened(k_fr)
    own_b = pl.ds(8, 32)
    for b in range(4):
        b_k[1 + b, own_b] = 0.125 * summed[32 * b : 32 * b + 32]
    zb_first = lanes % 16 == 0
    zb_last = lanes % 16 == 15
    for b in range(4):
        j = b + 1
        k = b_k[j, own_b]
        kxm = b_k[j, pl.ds(7, 32)]
        kxp = b_k[j, pl.ds(9, 32)]
        kym = y_before(b_k, j, own_b, lanes, 16)
        kyp = y_beyond(b_k, j, own_b, lanes, 16)
        kzm = jnp.where(zb_first, 0.0, roll(k, 1))
        kzp = jnp.where(zb_last, 0.0, roll(k, 127))
        b_wx[j, own_b] = 0.5 * (k + kxm)
        b_wy[j, own_b] = 0.5 * (k + kym)
        b_wz[j, own_b] = jnp.where(zb_first, 0.0, 0.5 * (k + kzm))
        inverse = 1.0 / (3.0 * k + 0.5 * (kxm + kxp + kym + kyp + kzm + kzp))
        inverse = jnp.where(k > 0.0, inverse, 0.0)
        b_ia[b] = jnp.where(first_b, inverse, 0.0)
        b_ib[b] = jnp.where(first_b, 0.0, inverse)

    for copy in deep_r:
        copy.wait_recv()
    for copy in deep_r:
        copy.wait_send()

    for copy in gathered:
        copy.wait_recv()
    for ye in (1, 2):
        for sx in range(4):
            boxes[ye, sx] = box_in[jnp.maximum(found[4 * ye + sx], 0)]
    beside = [
        remote(boxes.at[1], boxes.at[3], sem_s3.at[0], sem_r3.at[0], around[2]),
        remote(boxes.at[2], boxes.at[0], sem_s3.at[1], sem_r3.at[1], around[3]),
    ]

    def compose(ye):
        for oz in range(2):
            pair = [sx for sx in range(4) if (sx + ye) % 2 == oz]
            stacked = [boxes[ye, sx, b] for sx in pair for b in range(2)]
            wide = mapped(jnp.concatenate(stacked, axis=0), m_exp[oz])
            for number, sx in enumerate(pair):
                here = jnp.where(found[4 * ye + sx] >= 0, 1.0, 0.0)
                covered = jnp.where(lanes % 32 // 16 == oz, here, 0.0) > 0.5
                rows = pl.ds(8 + 16 * sx, 16)
                for q in range(4):
                    b, t = q // 2, q % 2
                    j = 1 + 4 * ye + q
                    at = 32 * number + 16 * b
                    part = wide[at : at + 16, 128 * t : 128 * t + 128]
                    mixed = jnp.where(covered, part, r_fr[j, rows])
                    r_fr[j, rows] = mixed
                    e_a[j, rows] = mixed * inv_a[j, rows]

    compose(1)
    compose(2)
    for copy in beside:
        copy.wait_recv()
    compose(0)
    compose(3)

    def second(i, carry):
        j = i + 1
        fresh = r_fr[j, window] + coupled(e_a, w_c, j, 8, 64, lanes, 32)
        e_b[j, window] = fresh * inv_b[j, window]
        return carry

    lax.fori_loop(0, 16, second, 0, unroll=2)

    own_c = pl.ds(24, 32)
    for oz in range(2):
        pair = [(0, oz), (1, 1 - oz)]
        stacked = []
        for ox, oy in pair:
            rows = pl.ds(24 + 16 * ox, 16)
            for b in range(2):
                parts = [
                    e_a[5 + 4 * oy + 2 * b + t, rows] + e_b[5 + 4 * oy + 2 * b + t, rows]
                    for t in range(2)
                ]
                stacked.append(jnp.concatenate(parts, axis=1))
        packed = mapped(jnp.concatenate(stacked, axis=0), m_com[oz])
        for number, (ox, oy) in enumerate(pair):
            for b in range(2):
                at = 32 * number + 16 * b
                e_oct[2 * ox + oy, b] = packed[at : at + 16]
    for h in range(N_X):
        e_out[h] = e_oct[octs[h]]
    returned = to_mates(lambda other: e_out.at[other], e_in, sem_s4, sem_r4)
    e_in[mx] = e_out[mx]

    def remaining(i, carry):
        j = i + 1
        left[j, window] = jnp.where(first_c, coupled(e_b, w_c, j, 8, 64, lanes, 32), 0.0)
        return carry

    lax.fori_loop(0, 16, remaining, 0, unroll=2)
    summed = 0.5 * coarsened(left)
    for b in range(4):
        source = summed[32 * b : 32 * b + 32]
        b_fa[b] = source * b_ia[b]
        b_fb[b] = source * b_ib[b]
        b_ua[1 + b, own_b] = source * b_ia[b]
    w_b = (b_wx, b_wy, b_wz)
    for half in range(2 * SWEEPS - 1):
        into, out_of = ((b_ub, b_ua), (b_ua, b_ub))[half % 2]
        fixed, inverse = ((b_fb, b_ib), (b_fa, b_ia))[half % 2]
        for b in range(4):
            into[1 + b, own_b] = fixed[b] + inverse[b] * coupled(
                out_of, w_b, 1 + b, 8, 32, lanes, 16
            )

    for ox in range(2):
        for oy in range(2):
            rows = pl.ds(16 + 8 * ox, 8)
            u_oct[2 * ox + oy] = b_ua[2 + oy, rows] + b_ub[2 + oy, rows]
    for h in range(N_X):
        u_out[h] = u_oct[octs[h]]
    settled = to_mates(lambda other: u_out.at[other], u_in, sem_s5, sem_r5)
    u_in[mx] = u_out[mx]

    def doubled(ref, pieces):
        for b, piece in enumerate(pieces):
            ref[b, pl.ds(0, 16, stride=2)] = piece
            ref[b, pl.ds(1, 16, stride=2)] = piece
        return mapped(jnp.concatenate([ref[0], ref[1]], axis=0), m_up[...])

    wide = doubled(dup, [b_ua[2 + b, pl.ds(16, 16)] + b_ub[2 + b, pl.ds(16, 16)] for b in range(2)])
    for j in range(8):
        b, q = j // 4, j % 4
        part = wide[32 * b : 32 * b + 32, 128 * q : 128 * q + 128]
        total = e_a[5 + j, own_c] + e_b[5 + j, own_c] + part
        out_c[:, 128 * j : 128 * j + 128] = s_fr[1 + j, own_f] + total

    for copy in returned:
        copy.wait_recv()
    got = e_in.at[owner_x]
    wide = doubled(dup2, [got[0], got[1]])
    for j in range(8):
        b, q = j // 4, j % 4
        f_sm[j] = f_sm[j] + wide[32 * b : 32 * b + 32, 128 * q : 128 * q + 128]
    for copy in settled:
        copy.wait_recv()
    tile = u_in[owner_x]
    side = jnp.where(own_oz == 1, 1.0, 0.0)
    tile = jnp.where(jnp.zeros((8, 128), F32) + side > 0.5, roll(tile, 120), tile)
    for t in range(4):
        dup[0, pl.ds(t, 8, stride=4)] = tile
    wide = mapped(dup[0], m_four[...])
    for j in range(8):
        out_f[0, :, 128 * j : 128 * j + 128] = f_sm[j] + wide[:, 128 * j : 128 * j + 128]

    for copy in sends:
        copy.wait_send()


def scratch():
    v = pltpu.VMEM
    lists = [pltpu.SMEM((N_X * N_Y,), jnp.int32), pltpu.SMEM((3,), jnp.int32)]
    shapes = [(10, 48, 128)] * 2 + [(8, 32, 128)]
    shapes += [(8, 32, 128)] + [(10, 48, 128)] * 8 + [(8, 32, 128), (10, 48, 128)]
    shapes += [(8, 32, 128)] * 2
    shapes += [(18, 80, 128)] * 10
    shapes += [(6, 48, 128)] * 4 + [(4, 32, 128)] * 4 + [(6, 48, 128)] * 2
    shapes += [(8, 16, 128), (8, 16, 128), (N_X, 16, 128), (N_X, 16, 128)]
    shapes += [(2, 16, 128), (N_X, 2, 16, 128), (4, 4, 2, 16, 128)]
    shapes += [(4, 2, 16, 128), (N_X, 2, 16, 128), (N_X, 2, 16, 128)]
    shapes += [(4, 8, 128), (N_X, 8, 128), (N_X, 8, 128)]
    shapes += [(2, 32, 128)] * 2
    result = lists + [v(shape, F32) for shape in shapes]
    maps = [(2, 896, 128), (128, 1280), (512, 128), (128, 512), (2, 128, 256), (2, 256, 128)]
    result += [v(shape, BF16) for shape in maps + [(128, 1024)]]
    dma = pltpu.SemaphoreType.DMA
    result += [dma((8, 8))] + [dma((8,))] * 2 + [dma((12,))] * 4 + [dma((N_X,))] * 4 + [dma((2,))] * 2
    return result + [dma((N_X,))] * 4


def on_device(
    coarse_source,
    coarse_coefficient,
    coarse_start,
    fine_source,
    fine_coefficient,
    fine_start,
    fine_position,
    first_colour,
):
    vmem = pl.BlockSpec(memory_space=pltpu.VMEM)
    hbm = pl.BlockSpec(memory_space=pltpu.HBM)
    return pl.pallas_call(
        kernel,
        out_shape=(
            jax.ShapeDtypeStruct(coarse_start.shape, F32),
            jax.ShapeDtypeStruct(fine_start.shape, F32),
        ),
        in_specs=[hbm] * 8,
        out_specs=(vmem, vmem),
        scratch_shapes=scratch(),
        compiler_params=pltpu.CompilerParams(
            collective_id=0, has_side_effects=True, vmem_limit_bytes=48 << 20
        ),
    )(
        *[
            pltpu.with_memory_space_constraint(array, pltpu.HBM)
            for array in (
                fine_position,
                first_colour,
                coarse_source,
                coarse_coefficient,
                coarse_start,
                fine_source,
                fine_coefficient,
                fine_start,
            )
        ],
    )


def solution(mesh):
    placed = (
        P("gx", "gy"),
        P("gx", "gy"),
        P("gx", "gy"),
        P(("gx", "gy"), None, None),
        P(("gx", "gy"), None, None),
        P(("gx", "gy"), None, None),
        P(),
        P(),
    )
    return jax.shard_map(
        on_device,
        mesh=mesh,
        in_specs=placed,
        out_specs=(P("gx", "gy"), P(("gx", "gy"), None, None)),
        check_vma=False,
    )
```

```python
import functools

import jax
import jax.numpy as jnp
from jax import lax
from jax.experimental import pallas as pl
from jax.experimental.pallas import tpu as pltpu
from jax.sharding import PartitionSpec as P


MESH = pl.DeviceIdType.MESH
F32 = jnp.float32
BF16 = jnp.bfloat16
SWEEPS = 4
N_X = 16
N_Y = 8
FAR_FIRST = (10, 6, 9, 11, 7, 5, 14, 2, 8, 13, 15, 3, 1, 12, 4)
UNROLL = 16


def iota(shape, dim):
    return lax.broadcasted_iota(jnp.int32, shape, dim)


def halves(values):
    high = values.astype(BF16)
    low = (values - high.astype(F32)).astype(BF16)
    return jnp.concatenate([high, low], axis=0)


def mapped(values, matrix):
    rows = values.shape[0]
    both = jnp.dot(halves(values), matrix, preferred_element_type=F32)
    return both[:rows] + both[rows:]


def roll(values, amount):
    return pltpu.roll(values, amount, axis=1)


def y_before(ref, j, rows, lanes, step):
    return roll(jnp.where(lanes >= 128 - step, ref[j - 1, rows], ref[j, rows]), step)


def y_beyond(ref, j, rows, lanes, step):
    return roll(jnp.where(lanes < step, ref[j + 1, rows], ref[j, rows]), 128 - step)


def coupled(value, weights, j, low, count, lanes, step):
    wx, wy, wz = weights
    here = pl.ds(low, count)
    before = pl.ds(low - 1, count)
    beyond = pl.ds(low + 1, count)
    mid = value[j, here]
    w_y = wy[j, here]
    w_z = wz[j, here]
    total = wx[j, here] * value[j, before] + wx[j, beyond] * value[j, beyond]
    total = total + w_y * y_before(value, j, here, lanes, step)
    ahead = jnp.where(lanes < step, wy[j + 1, here] * value[j + 1, here], w_y * mid)
    total = total + roll(ahead, 128 - step)
    return total + w_z * roll(mid, 1) + roll(w_z * mid, 127)


def zero_pads(ref, low, high):
    blocks, rows, _ = ref.shape
    ref[0] = jnp.zeros((rows, 128), F32)
    ref[blocks - 1] = jnp.zeros((rows, 128), F32)
    ref[1 : blocks - 1, :low] = jnp.zeros((blocks - 2, low, 128), F32)
    ref[1 : blocks - 1, high:] = jnp.zeros((blocks - 2, rows - high, 128), F32)


class Remote:
    def __init__(self, copy):
        self.copy = copy
        self.landed = False
        self.left = False
        copy.start()

    def wait_recv(self):
        if not self.landed:
            self.copy.wait_recv()
        self.landed = True

    def wait_send(self):
        if not self.left:
            self.copy.wait_send()
        self.left = True


def put(ref, mask):
    ref[...] = jnp.where(mask, 1.0, 0.0).astype(BF16)


def kernel(
    pos_hbm,
    colours_hbm,
    c_source,
    c_coeff,
    c_start,
    f_source,
    f_coeff,
    f_start,
    out,
    pos,
    colours,
    s_fr,
    kq_fr,
    src_c,
    f_src,
    f_k,
    f_v,
    f_wx,
    f_wy,
    f_wz,
    f_inv,
    f_base,
    f_a,
    f_sm,
    f_d,
    f_res,
    f_gx,
    k_fr,
    r_fr,
    wx,
    wy,
    wz,
    inv_a,
    inv_b,
    e_a,
    e_b,
    left,
    b_k,
    b_wx,
    b_wy,
    b_wz,
    b_ia,
    b_ib,
    b_fa,
    b_fb,
    b_ua,
    b_ub,
    x_rows,
    faces,
    ghost_out,
    ghost_in,
    box_out,
    box_in,
    boxes,
    e_oct,
    e_out,
    e_in,
    u_oct,
    u_out,
    u_in,
    dup,
    dup2,
    m_face,
    m_ghost,
    m_down,
    m_up,
    m_exp,
    m_com,
    m_four,
    sem_l,
    sem_s0,
    sem_r0,
    sem_sk,
    sem_rk,
    sem_sr,
    sem_rr,
    sem_s1,
    sem_r1,
    sem_s2,
    sem_r2,
    sem_s3,
    sem_r3,
    sem_s4,
    sem_r4,
    sem_s5,
    sem_r5,
):
    mx = lax.axis_index("gx")
    my = lax.axis_index("gy")
    x_up, x_dn = lax.rem(mx + 1, N_X), lax.rem(mx + N_X - 1, N_X)
    y_up, y_dn = lax.rem(my + 1, N_Y), lax.rem(my + N_Y - 1, N_Y)
    around = [
        (x_dn, my),
        (x_up, my),
        (mx, y_dn),
        (mx, y_up),
    ]
    mates = [(lax.rem(mx + d, N_X), my) for d in FAR_FIRST]

    barrier = pltpu.get_barrier_semaphore()
    greeted = mates + around[2:]
    for device in greeted:
        pl.semaphore_signal(barrier, inc=1, device_id=device, device_id_type=MESH)

    loads = [
        [
            pltpu.make_async_copy(pos_hbm, pos, sem_l.at[7, 0]),
            pltpu.make_async_copy(colours_hbm, colours, sem_l.at[7, 1]),
        ]
    ]
    for copy in loads[0]:
        copy.start()

    def load(number, source, target):
        group = []
        for j in range(8):
            copy = pltpu.make_async_copy(source(j), target(j), sem_l.at[number, j])
            copy.start()
            group.append(copy)
        loads.append(group)

    def chunk(j):
        return pl.ds(128 * j, 128)

    load(0, lambda j: c_start.at[:, chunk(j)], lambda j: s_fr.at[1 + j, pl.ds(8, 32)])
    load(1, lambda j: c_coeff.at[:, chunk(j)], lambda j: kq_fr.at[1 + j, pl.ds(8, 32)])
    load(2, lambda j: f_coeff.at[0, :, chunk(j)], lambda j: f_k.at[1 + j, pl.ds(8, 32)])
    load(3, lambda j: f_start.at[0, :, chunk(j)], lambda j: f_v.at[1 + j, pl.ds(8, 32)])
    load(4, lambda j: f_source.at[0, :, chunk(j)], lambda j: f_src.at[j])
    load(5, lambda j: c_source.at[:, chunk(j)], lambda j: src_c.at[j])
    load(6, lambda j: c_coeff.at[:, chunk(j)], lambda j: k_fr.at[5 + j, pl.ds(24, 32)])

    for q in range(5):
        for j in (4 - q, 13 + q):
            for low, high in ((0, 8 + 4 * q), (72 - 4 * q, 80)):
                k_fr[j, low:high] = jnp.zeros((high - low, 128), F32)
                r_fr[j, low:high] = jnp.zeros((high - low, 128), F32)
    for copy in loads[0]:
        copy.wait()
    own_pos = pos[mx * N_Y + my]
    owner_x = own_pos >> 6
    own_oz = own_pos & 1

    slots = []
    for ye in range(4):
        row = (my, y_dn, y_up)[1 if ye == 0 else (2 if ye == 3 else 0)]
        for sx in range(4):
            ox, oy = (sx + 1) % 2, (ye + 1) % 2
            octant = 4 * ox + 2 * oy + (ox + oy) % 2
            column = mx + (-1, 0, 0, 1)[sx]
            slots.append((row, (column * N_Y + row) * 8 + octant))

    def look(h, found):
        held = [pos[h * N_Y + row] for row in (my, y_dn, y_up)]
        result = []
        for number, (row, wanted) in enumerate(slots):
            ye = number // 4
            at = held[1 if ye == 0 else (2 if ye == 3 else 0)]
            result.append(jnp.where(at == wanted, h, found[number]))
        return tuple(result)

    found = lax.fori_loop(0, N_X, look, tuple(jnp.int32(-1) for _ in slots))
    octs, picks = [], []
    for h in range(N_X):
        at = pos[h * N_Y + my]
        octant, away = (at >> 1) & 3, (at >> 6) - mx
        pick = jnp.where((away == 1) & (octant < 2), 4 + octant, 0)
        pick = jnp.where((away == -1) & (octant >= 2), 4 + octant, pick)
        octs.append(octant)
        picks.append(jnp.where(away == 0, octant, pick))

    lanes = iota((1, 128), 1)
    z_first = lanes % 32 == 0
    z_last = lanes % 32 == 31
    parity = (iota((8, 128), 0) + iota((8, 128), 1) // 32 + iota((8, 128), 1)) % 2
    parity_b = (iota((8, 128), 0) + iota((8, 128), 1) // 16 + iota((8, 128), 1)) % 2

    def painted(base, colour, rows):
        flags = jnp.where(base == colour, 1.0, 0.0)
        return jnp.concatenate([flags] * (rows // 8), axis=0) > 0.5

    first_f = painted(parity, colours[0], 32)
    first_c = painted(parity, colours[1], 64)
    first_b = painted(parity_b, colours[2], 32)

    zero_pads(f_v, 8, 40)
    zero_pads(f_wx, 8, 40)
    zero_pads(f_wy, 8, 40)
    zero_pads(f_a, 8, 40)
    zero_pads(f_d, 8, 40)
    x_rows[...] = jnp.zeros(x_rows.shape, F32)
    f_gx[...] = jnp.zeros(f_gx.shape, F32)

    for oz in range(2):
        k = iota((896, 128), 0)
        c = iota((896, 128), 1)
        block, lane = k // 128, k % 128
        z, yy = lane % 32, lane // 32
        mask = (block == 0) & (c < 16) & (lane == 96 + 16 * oz + c)
        mask = mask | ((block == 1) & (c >= 16) & (c < 32) & (lane == 16 * oz + c - 16))
        own = (block >= 2) & (block < 6) & (z == (16, 15)[oz])
        mask = mask | (own & (c == (48, 32)[oz] + 4 * (block - 2) + yy))
        mask = mask | (
            (block == 6) & (z >= 16 * oz) & (z < 16 * oz + 16) & (c == 64 + yy * 16 + z - 16 * oz)
        )
        m_face[oz] = jnp.where(mask, 1.0, 0.0).astype(BF16)

    for group in loads[1:3]:
        for copy in group:
            copy.wait()

    for ox in range(2):
        for oy in range(2):
            own, at = (24, 4) if ox == 0 else (23, 0)
            far, at_far = (39, 0) if ox == 0 else (8, 4)
            for q in range(4):
                j = 1 + 4 * oy + q
                x_rows[2 * ox + oy, at + q : at + q + 1] = s_fr[j, own : own + 1]
                x_rows[4 + 2 * ox + oy, at_far + q : at_far + q + 1] = s_fr[j, far : far + 1]
    blank = jnp.zeros((16, 128), F32)
    for oz in range(2):
        pair = [(0, oz), (1, 1 - oz)]
        stacked = []
        for ox, oy in pair:
            rows = pl.ds(8 + 16 * ox, 16)
            parts = [s_fr[4, rows], blank] if oy else [blank, s_fr[5, rows]]
            parts += [s_fr[1 + 4 * oy + q, rows] for q in range(4)]
            parts.append(x_rows[2 * ox + oy])
            stacked.append(jnp.concatenate(parts, axis=1))
        for ox, oy in pair:
            stacked.append(jnp.concatenate([blank] * 6 + [x_rows[4 + 2 * ox + oy]], axis=1))
        packed = mapped(jnp.concatenate(stacked, axis=0), m_face[oz])
        for number, (ox, oy) in enumerate(pair):
            faces[2 * ox + oy] = packed[16 * number : 16 * number + 16]
            faces[4 + 2 * ox + oy] = packed[32 + 16 * number : 48 + 16 * number]
    pl.semaphore_wait(barrier, len(greeted))

    sends = []

    def remote(source, target, send_sem, recv_sem, device):
        copy = Remote(
            pltpu.make_async_remote_copy(
                src_ref=source,
                dst_ref=target,
                send_sem=send_sem,
                recv_sem=recv_sem,
                device_id=device,
                device_id_type=MESH,
            )
        )
        sends.append(copy)
        return copy

    layer = []
    for number, ref in enumerate((s_fr, kq_fr)):
        rows, blocks = pl.ds(8, 32), pl.ds(1, 8)
        for side, (source, target, device) in enumerate(
            (
                (ref.at[8, rows], ref.at[0, rows], around[3]),
                (ref.at[1, rows], ref.at[9, rows], around[2]),
                (ref.at[blocks, pl.ds(39, 1)], ref.at[blocks, pl.ds(7, 1)], around[1]),
                (ref.at[blocks, pl.ds(8, 1)], ref.at[blocks, pl.ds(40, 1)], around[0]),
            )
        ):
            at = 4 * number + side
            layer.append(remote(source, target, sem_s0.at[at], sem_r0.at[at], device))

    for copy in loads[7]:
        copy.wait()

    def deep_x(ref, width, send_sem, recv_sem):
        blocks = pl.ds(5, 8)
        started = []
        for side, (source, target) in enumerate(((24, 56), (56 - width, 24 - width))):
            started.append(
                remote(
                    ref.at[blocks, pl.ds(source, width)],
                    ref.at[blocks, pl.ds(target, width)],
                    send_sem.at[side],
                    recv_sem.at[side],
                    around[side],
                )
            )
        return started

    def deep_y(ref, depth, send_sem, recv_sem):
        started = []
        for q in range(depth):
            rows = pl.ds(8 + 4 * q, 64 - 8 * q)
            for side, (source, target) in enumerate(((5 + q, 13 + q), (12 - q, 4 - q))):
                at = 2 + 2 * q + side
                started.append(
                    remote(
                        ref.at[source, rows],
                        ref.at[target, rows],
                        send_sem.at[at],
                        recv_sem.at[at],
                        around[2 + side],
                    )
                )
        return started

    deep_k = deep_x(k_fr, 17, sem_sk, sem_rk)

    for group in loads[3:6]:
        for copy in group:
            copy.wait()
    rows_f = iota((32, 128), 0)
    own_f = pl.ds(8, 32)

    def fine_weights(i, carry):
        j = i + 1
        k = f_k[j, own_f]
        y_first = (lanes < 32) & (j == 1)
        y_last = (lanes >= 96) & (j == 8)
        kxm = jnp.where(rows_f == 0, k, f_k[j, pl.ds(7, 32)])
        kxp = jnp.where(rows_f == 31, k, f_k[j, pl.ds(9, 32)])
        kym = jnp.where(y_first, k, y_before(f_k, j, own_f, lanes, 32))
        kyp = jnp.where(y_last, k, y_beyond(f_k, j, own_f, lanes, 32))
        kzm = jnp.where(z_first, k, roll(k, 1))
        kzp = jnp.where(z_last, k, roll(k, 127))
        f_wx[j, own_f] = jnp.where(rows_f == 0, 0.0, 0.5 * (k + kxm))
        f_wy[j, own_f] = jnp.where(y_first, 0.0, 0.5 * (k + kym))
        f_wz[j, own_f] = jnp.where(z_first, 0.0, 0.5 * (k + kzm))
        f_inv[j, own_f] = 1.0 / (3.0 * k + 0.5 * (kxm + kxp + kym + kyp + kzm + kzp))
        return carry

    lax.fori_loop(0, 8, fine_weights, 0)
    w_f = (f_wx, f_wy, f_wz)

    def fine_base(i, carry):
        f_base[i + 1, own_f] = 0.25 * f_src[i] + coupled(f_v, w_f, i + 1, 8, 32, lanes, 32)
        return carry

    lax.fori_loop(0, 8, fine_base, 0)

    for copy in layer[:2]:
        copy.wait_recv()

    def blank_sides(ref):
        @pl.when(my == 0)
        def _():
            ref[0, 8:40] = jnp.zeros((32, 128), F32)

        @pl.when(my == N_Y - 1)
        def _():
            ref[9, 8:40] = jnp.zeros((32, 128), F32)

    blank_sides(s_fr)

    for ox in range(2):
        for oy in range(2):
            rows = pl.ds(8 + 16 * ox, 16)
            oz = (ox + oy) % 2
            shift = (128 - 96 - 16 * oz, 16 - 16 * oz)[oy] % 128
            beside = s_fr[9 * oy, rows]
            if shift:
                beside = roll(beside, shift)
            wanted = (lanes >= 16 * oy) & (lanes < 16 * oy + 16)
            faces[2 * ox + oy] = faces[2 * ox + oy] + jnp.where(wanted, beside, 0.0)

    def to_mates(source, target, send_sem, recv_sem):
        started = []
        for d in FAR_FIRST:
            other = lax.rem(mx + d, N_X)
            started.append(
                remote(source(other), target.at[mx], send_sem.at[d], recv_sem.at[d], (other, my))
            )
        return started

    for h in range(N_X):
        ghost_out[h] = faces[picks[h]]
    ghosts = to_mates(lambda other: ghost_out.at[other], ghost_in, sem_s1, sem_r1)
    ghost_in[mx] = ghost_out[mx]

    for copy in layer:
        copy.wait_recv()
    blank_sides(kq_fr)
    for ref in (s_fr, kq_fr):

        @pl.when(mx == 0)
        def _():
            ref[1:9, 7:8] = jnp.zeros((8, 1, 128), F32)

        @pl.when(mx == N_X - 1)
        def _():
            ref[1:9, 40:41] = jnp.zeros((8, 1, 128), F32)

    for copy in loads[6]:
        copy.wait()

    def coarse_residual(i, carry):
        j = i + 1
        s = s_fr[j, own_f]
        k = kq_fr[j, own_f]

        def flux(k_there, s_there):
            return (k + k_there) * (s - s_there)

        before, beyond = pl.ds(7, 32), pl.ds(9, 32)
        total = flux(kq_fr[j, before], s_fr[j, before]) + flux(kq_fr[j, beyond], s_fr[j, beyond])
        total = total + flux(
            y_before(kq_fr, j, own_f, lanes, 32), y_before(s_fr, j, own_f, lanes, 32)
        )
        total = total + flux(
            y_beyond(kq_fr, j, own_f, lanes, 32), y_beyond(s_fr, j, own_f, lanes, 32)
        )
        total = total + flux(
            jnp.where(z_first, 0.0, roll(k, 1)), jnp.where(z_first, 0.0, roll(s, 1))
        )
        total = total + flux(
            jnp.where(z_last, 0.0, roll(k, 127)), jnp.where(z_last, 0.0, roll(s, 127))
        )
        r_fr[i + 5, pl.ds(24, 32)] = src_c[i] - 0.5 * total
        return carry

    lax.fori_loop(0, 8, coarse_residual, 0)
    deep_r = deep_x(r_fr, 16, sem_sr, sem_rr)

    for copy in deep_k:
        copy.wait_recv()

    @pl.when(mx == 0)
    def _():
        k_fr[5:13, 7:24] = jnp.zeros((8, 17, 128), F32)

    @pl.when(mx == N_X - 1)
    def _():
        k_fr[5:13, 56:73] = jnp.zeros((8, 17, 128), F32)

    deep_k += deep_y(k_fr, 5, sem_sk, sem_rk)

    k = iota((128, 1280), 0)
    c = iota((128, 1280), 1)
    y, z = c // 32, c % 32
    inner = c < 1024
    mask = inner & (y == 0) & (k == z // 2)
    mask = mask | (inner & (y == 31) & (k == 16 + z // 2))
    mask = mask | (inner & (z == 0) & (k == 32 + y // 2))
    mask = mask | (inner & (z == 31) & (k == 48 + y // 2))
    mask = mask | ((c >= 1024) & (k == 64 + (y - 32) // 2 * 16 + z // 2))
    put(m_ghost, mask)
    k, c = iota((512, 128), 0), iota((512, 128), 1)
    put(m_down, c == k // 64 * 16 + k % 32 // 2)

    for copy in ghosts:
        copy.wait_recv()
    high_x = (own_pos >> 2) & 1
    other_x = owner_x + 2 * high_x - 1
    beyond_x = ghost_in[jnp.clip(other_x, 0, N_X - 1)]
    inside = jnp.where((other_x >= 0) & (other_x < N_X), 1.0, 0.0)
    mine = ghost_in[owner_x] + inside * beyond_x
    dup[0, pl.ds(0, 16, stride=2)] = mine
    dup[0, pl.ds(1, 16, stride=2)] = mine
    widened = mapped(dup[0], m_ghost[...])
    for q in range(4):
        for t in range(2):
            piece = widened[:, 1024 + 128 * t : 1152 + 128 * t]
            f_gx[2 * q + t, 0:1] = piece[2 * q : 2 * q + 1]
            f_gx[2 * q + t, 31:32] = piece[8 + 2 * q : 9 + 2 * q]
    for i in range(8):
        j = i + 1
        ghost = f_k[j, own_f] * (widened[:, 128 * i : 128 * i + 128] + f_gx[i])
        f_gx[i] = ghost
        f_a[j, own_f] = jnp.where(first_f, (f_base[j, own_f] + ghost) * f_inv[j, own_f], 0.0)
    for i in range(8):
        j = i + 1
        around_a = coupled(f_a, w_f, j, 8, 32, lanes, 32)
        fresh = (0.25 * f_src[i] + f_gx[i] + around_a) * f_inv[j, own_f]
        f_sm[i] = jnp.where(first_f, f_a[j, own_f], fresh)
        f_d[j, own_f] = jnp.where(first_f, 0.0, fresh - f_v[j, own_f])
    for i in range(8):
        f_res[i] = jnp.where(first_f, coupled(f_d, w_f, i + 1, 8, 32, lanes, 32), 0.0)
    stacked = []
    for b in range(2):
        parts = [
            f_res[4 * b + q, pl.ds(0, 16, stride=2)] + f_res[4 * b + q, pl.ds(1, 16, stride=2)]
            for q in range(4)
        ]
        stacked.append(jnp.concatenate(parts, axis=1))
    packed = 0.5 * mapped(jnp.concatenate(stacked, axis=0), m_down[...])
    box_out[0] = packed[:16]
    box_out[1] = packed[16:]
    gathered = to_mates(lambda other: box_out, box_in, sem_s2, sem_r2)
    box_in[mx] = box_out[...]
    for copy in deep_r:
        copy.wait_recv()
    deep_r += deep_y(r_fr, 4, sem_sr, sem_rr)

    zero_pads(wx, 8, 72)
    zero_pads(wy, 8, 72)
    zero_pads(e_a, 8, 72)
    zero_pads(e_b, 8, 72)
    for ref in (b_k, b_wx, b_wy, b_ua, b_ub):
        zero_pads(ref, 8, 40)
    for oz in range(2):
        k, c = iota((128, 256), 0), iota((128, 256), 1)
        m_exp[oz] = jnp.where((k // 16 == c // 32) & (c % 32 == 16 * oz + k % 16), 1.0, 0.0).astype(BF16)
        k, c = iota((256, 128), 1), iota((256, 128), 0)
        m_com[oz] = jnp.where((k // 16 == c // 32) & (c % 32 == 16 * oz + k % 16), 1.0, 0.0).astype(BF16)
    k, c = iota((128, 512), 0), iota((128, 512), 1)
    put(m_up, k == c // 64 * 16 + c % 32 // 2)
    k, c = iota((128, 1024), 0), iota((128, 1024), 1)
    put(m_four, k == c // 128 * 16 + c % 32 // 4)

    for copy in deep_k:
        copy.wait_recv()
    @pl.when(my == 0)
    def _():
        k_fr[0:5] = jnp.zeros((5, 80, 128), F32)

    @pl.when(my == N_Y - 1)
    def _():
        k_fr[13:18] = jnp.zeros((5, 80, 128), F32)

    window = pl.ds(8, 64)

    def coarse_weights(i, carry):
        j = i + 1
        k = k_fr[j, window]
        kxm = k_fr[j, pl.ds(7, 64)]
        kxp = k_fr[j, pl.ds(9, 64)]
        kym = y_before(k_fr, j, window, lanes, 32)
        kyp = y_beyond(k_fr, j, window, lanes, 32)
        kzm = jnp.where(z_first, 0.0, roll(k, 1))
        kzp = jnp.where(z_last, 0.0, roll(k, 127))
        wx[j, window] = 0.5 * (k + kxm)
        wy[j, window] = 0.5 * (k + kym)
        wz[j, window] = jnp.where(z_first, 0.0, 0.5 * (k + kzm))
        inverse = 1.0 / (3.0 * k + 0.5 * (kxm + kxp + kym + kyp + kzm + kzp))
        inverse = jnp.where(k > 0.0, inverse, 0.0)
        inv_a[j, window] = jnp.where(first_c, inverse, 0.0)
        inv_b[j, window] = jnp.where(first_c, 0.0, inverse)
        return carry

    lax.fori_loop(0, 16, coarse_weights, 0)
    w_c = (wx, wy, wz)

    def coarsened(ref):
        stacked = []
        for b in range(4):
            parts = [
                ref[1 + 4 * b + q, pl.ds(8, 32, stride=2)]
                + ref[1 + 4 * b + q, pl.ds(9, 32, stride=2)]
                for q in range(4)
            ]
            stacked.append(jnp.concatenate(parts, axis=1))
        return mapped(jnp.concatenate(stacked, axis=0), m_down[...])

    summed = coarsened(k_fr)
    own_b = pl.ds(8, 32)
    for b in range(4):
        b_k[1 + b, own_b] = 0.125 * summed[32 * b : 32 * b + 32]
    zb_first = lanes % 16 == 0
    zb_last = lanes % 16 == 15
    for b in range(4):
        j = b + 1
        k = b_k[j, own_b]
        kxm = b_k[j, pl.ds(7, 32)]
        kxp = b_k[j, pl.ds(9, 32)]
        kym = y_before(b_k, j, own_b, lanes, 16)
        kyp = y_beyond(b_k, j, own_b, lanes, 16)
        kzm = jnp.where(zb_first, 0.0, roll(k, 1))
        kzp = jnp.where(zb_last, 0.0, roll(k, 127))
        b_wx[j, own_b] = 0.5 * (k + kxm)
        b_wy[j, own_b] = 0.5 * (k + kym)
        b_wz[j, own_b] = jnp.where(zb_first, 0.0, 0.5 * (k + kzm))
        inverse = 1.0 / (3.0 * k + 0.5 * (kxm + kxp + kym + kyp + kzm + kzp))
        inverse = jnp.where(k > 0.0, inverse, 0.0)
        b_ia[b] = jnp.where(first_b, inverse, 0.0)
        b_ib[b] = jnp.where(first_b, 0.0, inverse)

    for copy in deep_r:
        copy.wait_recv()
    for copy in deep_r:
        copy.wait_send()

    for copy in gathered:
        copy.wait_recv()
    for ye in (1, 2):
        for sx in range(4):
            boxes[ye, sx] = box_in[jnp.maximum(found[4 * ye + sx], 0)]
    beside = [
        remote(boxes.at[1], boxes.at[3], sem_s3.at[0], sem_r3.at[0], around[2]),
        remote(boxes.at[2], boxes.at[0], sem_s3.at[1], sem_r3.at[1], around[3]),
    ]

    def compose(ye):
        for oz in range(2):
            pair = [sx for sx in range(4) if (sx + ye) % 2 == oz]
            stacked = [boxes[ye, sx, b] for sx in pair for b in range(2)]
            wide = mapped(jnp.concatenate(stacked, axis=0), m_exp[oz])
            for number, sx in enumerate(pair):
                here = jnp.where(found[4 * ye + sx] >= 0, 1.0, 0.0)
                covered = jnp.where(lanes % 32 // 16 == oz, here, 0.0) > 0.5
                rows = pl.ds(8 + 16 * sx, 16)
                for q in range(4):
                    b, t = q // 2, q % 2
                    j = 1 + 4 * ye + q
                    at = 32 * number + 16 * b
                    part = wide[at : at + 16, 128 * t : 128 * t + 128]
                    mixed = jnp.where(covered, part, r_fr[j, rows])
                    r_fr[j, rows] = mixed
                    e_a[j, rows] = mixed * inv_a[j, rows]

    compose(1)
    compose(2)
    for copy in beside:
        copy.wait_recv()
    compose(0)
    compose(3)

    def second(i, carry):
        j = i + 1
        fresh = r_fr[j, window] + coupled(e_a, w_c, j, 8, 64, lanes, 32)
        e_b[j, window] = fresh * inv_b[j, window]
        return carry

    lax.fori_loop(0, 16, second, 0, unroll=UNROLL)

    own_c = pl.ds(24, 32)
    for oz in range(2):
        pair = [(0, oz), (1, 1 - oz)]
        stacked = []
        for ox, oy in pair:
            rows = pl.ds(24 + 16 * ox, 16)
            for b in range(2):
                parts = [
                    e_a[5 + 4 * oy + 2 * b + t, rows] + e_b[5 + 4 * oy + 2 * b + t, rows]
                    for t in range(2)
                ]
                stacked.append(jnp.concatenate(parts, axis=1))
        packed = mapped(jnp.concatenate(stacked, axis=0), m_com[oz])
        for number, (ox, oy) in enumerate(pair):
            for b in range(2):
                at = 32 * number + 16 * b
                e_oct[2 * ox + oy, b] = packed[at : at + 16]
    for h in range(N_X):
        e_out[h] = e_oct[octs[h]]
    returned = to_mates(lambda other: e_out.at[other], e_in, sem_s4, sem_r4)
    e_in[mx] = e_out[mx]

    def remaining(i, carry):
        j = i + 1
        left[j, window] = jnp.where(first_c, coupled(e_b, w_c, j, 8, 64, lanes, 32), 0.0)
        return carry

    lax.fori_loop(0, 16, remaining, 0, unroll=UNROLL)
    summed = 0.5 * coarsened(left)
    for b in range(4):
        source = summed[32 * b : 32 * b + 32]
        b_fa[b] = source * b_ia[b]
        b_fb[b] = source * b_ib[b]
        b_ua[1 + b, own_b] = source * b_ia[b]
    w_b = (b_wx, b_wy, b_wz)
    for half in range(2 * SWEEPS - 1):
        into, out_of = ((b_ub, b_ua), (b_ua, b_ub))[half % 2]
        fixed, inverse = ((b_fb, b_ib), (b_fa, b_ia))[half % 2]
        for b in range(4):
            into[1 + b, own_b] = fixed[b] + inverse[b] * coupled(
                out_of, w_b, 1 + b, 8, 32, lanes, 16
            )

    for ox in range(2):
        for oy in range(2):
            rows = pl.ds(16 + 8 * ox, 8)
            u_oct[2 * ox + oy] = b_ua[2 + oy, rows] + b_ub[2 + oy, rows]
    for h in range(N_X):
        u_out[h] = u_oct[octs[h]]
    settled = to_mates(lambda other: u_out.at[other], u_in, sem_s5, sem_r5)
    u_in[mx] = u_out[mx]

    def doubled(ref, pieces):
        for b, piece in enumerate(pieces):
            ref[b, pl.ds(0, 16, stride=2)] = piece
            ref[b, pl.ds(1, 16, stride=2)] = piece
        return mapped(jnp.concatenate([ref[0], ref[1]], axis=0), m_up[...])

    wide = doubled(dup, [b_ua[2 + b, pl.ds(16, 16)] + b_ub[2 + b, pl.ds(16, 16)] for b in range(2)])
    for j in range(8):
        b, q = j // 4, j % 4
        part = wide[32 * b : 32 * b + 32, 128 * q : 128 * q + 128]
        total = e_a[5 + j, own_c] + e_b[5 + j, own_c] + part
        out[0, :, 128 * j : 128 * j + 128] = s_fr[1 + j, own_f] + total

    for copy in returned:
        copy.wait_recv()
    got = e_in.at[owner_x]
    wide = doubled(dup2, [got[0], got[1]])
    for j in range(8):
        b, q = j // 4, j % 4
        f_sm[j] = f_sm[j] + wide[32 * b : 32 * b + 32, 128 * q : 128 * q + 128]
    for copy in settled:
        copy.wait_recv()
    tile = u_in[owner_x]
    side = jnp.where(own_oz == 1, 1.0, 0.0)
    tile = jnp.where(jnp.zeros((8, 128), F32) + side > 0.5, roll(tile, 120), tile)
    for t in range(4):
        dup[0, pl.ds(t, 8, stride=4)] = tile
    wide = mapped(dup[0], m_four[...])
    for j in range(8):
        out[1, :, 128 * j : 128 * j + 128] = f_sm[j] + wide[:, 128 * j : 128 * j + 128]

    for copy in sends:
        copy.wait_send()


def scratch():
    v = pltpu.VMEM
    lists = [pltpu.SMEM((N_X * N_Y,), jnp.int32), pltpu.SMEM((3,), jnp.int32)]
    shapes = [(10, 48, 128)] * 2 + [(8, 32, 128)]
    shapes += [(8, 32, 128)] + [(10, 48, 128)] * 8 + [(8, 32, 128), (10, 48, 128)]
    shapes += [(8, 32, 128)] * 2
    shapes += [(18, 80, 128)] * 10
    shapes += [(6, 48, 128)] * 4 + [(4, 32, 128)] * 4 + [(6, 48, 128)] * 2
    shapes += [(8, 16, 128), (8, 16, 128), (N_X, 16, 128), (N_X, 16, 128)]
    shapes += [(2, 16, 128), (N_X, 2, 16, 128), (4, 4, 2, 16, 128)]
    shapes += [(4, 2, 16, 128), (N_X, 2, 16, 128), (N_X, 2, 16, 128)]
    shapes += [(4, 8, 128), (N_X, 8, 128), (N_X, 8, 128)]
    shapes += [(2, 32, 128)] * 2
    result = lists + [v(shape, F32) for shape in shapes]
    maps = [(2, 896, 128), (128, 1280), (512, 128), (128, 512), (2, 128, 256), (2, 256, 128)]
    result += [v(shape, BF16) for shape in maps + [(128, 1024)]]
    dma = pltpu.SemaphoreType.DMA
    result += [dma((8, 8))] + [dma((8,))] * 2 + [dma((12,))] * 4 + [dma((N_X,))] * 4 + [dma((2,))] * 2
    return result + [dma((N_X,))] * 4


def on_device(
    coarse_source,
    coarse_coefficient,
    coarse_start,
    fine_source,
    fine_coefficient,
    fine_start,
    fine_position,
    first_colour,
):
    vmem = pl.BlockSpec(memory_space=pltpu.VMEM)
    hbm = pl.BlockSpec(memory_space=pltpu.HBM)
    both = pl.pallas_call(
        kernel,
        out_shape=jax.ShapeDtypeStruct((2, 32, 1024), F32),
        in_specs=[hbm] * 8,
        out_specs=vmem,
        scratch_shapes=scratch(),
        compiler_params=pltpu.CompilerParams(
            collective_id=0, has_side_effects=True, vmem_limit_bytes=48 << 20
        ),
    )(
        *[
            pltpu.with_memory_space_constraint(array, pltpu.HBM)
            for array in (
                fine_position,
                first_colour,
                coarse_source,
                coarse_coefficient,
                coarse_start,
                fine_source,
                fine_coefficient,
                fine_start,
            )
        ],
    )
    return both[0], both[1:]


def solution(mesh):
    placed = (
        P("gx", "gy"),
        P("gx", "gy"),
        P("gx", "gy"),
        P(("gx", "gy"), None, None),
        P(("gx", "gy"), None, None),
        P(("gx", "gy"), None, None),
        P(),
        P(),
    )
    return jax.shard_map(
        on_device,
        mesh=mesh,
        in_specs=placed,
        out_specs=(P("gx", "gy"), P(("gx", "gy"), None, None)),
        check_vma=False,
    )
```

```python
import functools

import jax
import jax.numpy as jnp
from jax import lax
from jax.experimental import pallas as pl
from jax.experimental.pallas import tpu as pltpu
from jax.sharding import PartitionSpec as P


MESH = pl.DeviceIdType.MESH
F32 = jnp.float32
BF16 = jnp.bfloat16
SWEEPS = 4
N_X = 16
N_Y = 8
FAR_FIRST = (10, 6, 9, 11, 7, 5, 14, 2, 8, 13, 15, 3, 1, 12, 4)
UNROLL = 16


def iota(shape, dim):
    return lax.broadcasted_iota(jnp.int32, shape, dim)


def halves(values):
    high = values.astype(BF16)
    low = (values - high.astype(F32)).astype(BF16)
    return jnp.concatenate([high, low], axis=0)


def mapped(values, matrix):
    rows = values.shape[0]
    both = jnp.dot(halves(values), matrix, preferred_element_type=F32)
    return both[:rows] + both[rows:]


def roll(values, amount):
    return pltpu.roll(values, amount, axis=1)


def y_before(ref, j, rows, lanes, step):
    return roll(jnp.where(lanes >= 128 - step, ref[j - 1, rows], ref[j, rows]), step)


def y_beyond(ref, j, rows, lanes, step):
    return roll(jnp.where(lanes < step, ref[j + 1, rows], ref[j, rows]), 128 - step)


def coupled(value, weights, j, low, count, lanes, step):
    wx, wy, wz = weights
    here = pl.ds(low, count)
    before = pl.ds(low - 1, count)
    beyond = pl.ds(low + 1, count)
    mid = value[j, here]
    w_y = wy[j, here]
    w_z = wz[j, here]
    total = wx[j, here] * value[j, before] + wx[j, beyond] * value[j, beyond]
    total = total + w_y * y_before(value, j, here, lanes, step)
    ahead = jnp.where(lanes < step, wy[j + 1, here] * value[j + 1, here], w_y * mid)
    total = total + roll(ahead, 128 - step)
    return total + w_z * roll(mid, 1) + roll(w_z * mid, 127)


def zero_pads(ref, low, high):
    blocks, rows, _ = ref.shape
    ref[0] = jnp.zeros((rows, 128), F32)
    ref[blocks - 1] = jnp.zeros((rows, 128), F32)
    ref[1 : blocks - 1, :low] = jnp.zeros((blocks - 2, low, 128), F32)
    ref[1 : blocks - 1, high:] = jnp.zeros((blocks - 2, rows - high, 128), F32)


class Remote:
    def __init__(self, copy):
        self.copy = copy
        self.landed = False
        self.left = False
        copy.start()

    def wait_recv(self):
        if not self.landed:
            self.copy.wait_recv()
        self.landed = True

    def wait_send(self):
        if not self.left:
            self.copy.wait_send()
        self.left = True


class Group:
    def __init__(self, span, send_sem, recv_sem):
        self.sent = pltpu.make_async_copy(span, span, send_sem)
        self.landed = pltpu.make_async_copy(span, span, recv_sem)

    def wait_recv(self):
        self.landed.wait()

    def wait_send(self):
        self.sent.wait()


def put(ref, mask):
    ref[...] = jnp.where(mask, 1.0, 0.0).astype(BF16)


def kernel(
    pos_hbm,
    colours_hbm,
    c_source,
    c_coeff,
    c_start,
    f_source,
    f_coeff,
    f_start,
    out,
    pos,
    colours,
    s_fr,
    kq_fr,
    src_c,
    f_src,
    f_k,
    f_v,
    f_wx,
    f_wy,
    f_wz,
    f_inv,
    f_base,
    f_a,
    f_sm,
    f_d,
    f_res,
    f_gx,
    k_fr,
    r_fr,
    wx,
    wy,
    wz,
    inv_a,
    inv_b,
    e_a,
    e_b,
    left,
    b_k,
    b_wx,
    b_wy,
    b_wz,
    b_ia,
    b_ib,
    b_fa,
    b_fb,
    b_ua,
    b_ub,
    x_rows,
    faces,
    ghost_out,
    ghost_in,
    box_out,
    box_in,
    boxes,
    e_oct,
    e_out,
    e_in,
    u_oct,
    u_out,
    u_in,
    dup,
    dup2,
    m_face,
    m_ghost,
    m_down,
    m_up,
    m_exp,
    m_com,
    m_four,
    sem_l,
    sem_s0,
    sem_r0,
    sem_sk,
    sem_rk,
    sem_sr,
    sem_rr,
    sem_s1,
    sem_r1,
    sem_s2,
    sem_r2,
    sem_s3,
    sem_r3,
    sem_s4,
    sem_r4,
    sem_s5,
    sem_r5,
):
    mx = lax.axis_index("gx")
    my = lax.axis_index("gy")
    x_up, x_dn = lax.rem(mx + 1, N_X), lax.rem(mx + N_X - 1, N_X)
    y_up, y_dn = lax.rem(my + 1, N_Y), lax.rem(my + N_Y - 1, N_Y)
    around = [
        (x_dn, my),
        (x_up, my),
        (mx, y_dn),
        (mx, y_up),
    ]
    mates = [(lax.rem(mx + d, N_X), my) for d in FAR_FIRST]

    barrier = pltpu.get_barrier_semaphore()
    greeted = mates + around[2:]
    for device in greeted:
        pl.semaphore_signal(barrier, inc=1, device_id=device, device_id_type=MESH)

    loads = [
        [
            pltpu.make_async_copy(pos_hbm, pos, sem_l.at[7]),
            pltpu.make_async_copy(colours_hbm, colours, sem_l.at[8]),
        ]
    ]
    for copy in loads[0]:
        copy.start()

    def load(number, source, target, span):
        for j in range(8):
            pltpu.make_async_copy(source(j), target(j), sem_l.at[number]).start()
        loads.append([pltpu.make_async_copy(span, span, sem_l.at[number])])

    def chunk(j):
        return pl.ds(128 * j, 128)

    load(0, lambda j: c_start.at[:, chunk(j)], lambda j: s_fr.at[1 + j, pl.ds(8, 32)], s_fr.at[pl.ds(1, 8), pl.ds(8, 32)])
    load(1, lambda j: c_coeff.at[:, chunk(j)], lambda j: kq_fr.at[1 + j, pl.ds(8, 32)], kq_fr.at[pl.ds(1, 8), pl.ds(8, 32)])
    load(2, lambda j: f_coeff.at[0, :, chunk(j)], lambda j: f_k.at[1 + j, pl.ds(8, 32)], f_k.at[pl.ds(1, 8), pl.ds(8, 32)])
    load(3, lambda j: f_start.at[0, :, chunk(j)], lambda j: f_v.at[1 + j, pl.ds(8, 32)], f_v.at[pl.ds(1, 8), pl.ds(8, 32)])
    load(4, lambda j: f_source.at[0, :, chunk(j)], lambda j: f_src.at[j], f_src)
    load(5, lambda j: c_source.at[:, chunk(j)], lambda j: src_c.at[j], src_c)
    load(6, lambda j: c_coeff.at[:, chunk(j)], lambda j: k_fr.at[5 + j, pl.ds(24, 32)], k_fr.at[pl.ds(5, 8), pl.ds(24, 32)])

    for q in range(5):
        for j in (4 - q, 13 + q):
            for low, high in ((0, 8 + 4 * q), (72 - 4 * q, 80)):
                k_fr[j, low:high] = jnp.zeros((high - low, 128), F32)
                r_fr[j, low:high] = jnp.zeros((high - low, 128), F32)
    for copy in loads[0]:
        copy.wait()
    own_pos = pos[mx * N_Y + my]
    owner_x = own_pos >> 6
    own_oz = own_pos & 1

    slots = []
    for ye in range(4):
        row = (my, y_dn, y_up)[1 if ye == 0 else (2 if ye == 3 else 0)]
        for sx in range(4):
            ox, oy = (sx + 1) % 2, (ye + 1) % 2
            octant = 4 * ox + 2 * oy + (ox + oy) % 2
            column = mx + (-1, 0, 0, 1)[sx]
            slots.append((row, (column * N_Y + row) * 8 + octant))

    def look(h, found):
        held = [pos[h * N_Y + row] for row in (my, y_dn, y_up)]
        result = []
        for number, (row, wanted) in enumerate(slots):
            ye = number // 4
            at = held[1 if ye == 0 else (2 if ye == 3 else 0)]
            result.append(jnp.where(at == wanted, h, found[number]))
        return tuple(result)

    found = lax.fori_loop(0, N_X, look, tuple(jnp.int32(-1) for _ in slots))
    octs, picks = [], []
    for h in range(N_X):
        at = pos[h * N_Y + my]
        octant, away = (at >> 1) & 3, (at >> 6) - mx
        pick = jnp.where((away == 1) & (octant < 2), 4 + octant, 0)
        pick = jnp.where((away == -1) & (octant >= 2), 4 + octant, pick)
        octs.append(octant)
        picks.append(jnp.where(away == 0, octant, pick))

    lanes = iota((1, 128), 1)
    z_first = lanes % 32 == 0
    z_last = lanes % 32 == 31
    parity = (iota((8, 128), 0) + iota((8, 128), 1) // 32 + iota((8, 128), 1)) % 2
    parity_b = (iota((8, 128), 0) + iota((8, 128), 1) // 16 + iota((8, 128), 1)) % 2

    def painted(base, colour, rows):
        flags = jnp.where(base == colour, 1.0, 0.0)
        return jnp.concatenate([flags] * (rows // 8), axis=0) > 0.5

    first_f = painted(parity, colours[0], 32)
    first_c = painted(parity, colours[1], 64)
    first_b = painted(parity_b, colours[2], 32)

    zero_pads(f_v, 8, 40)
    zero_pads(f_wx, 8, 40)
    zero_pads(f_wy, 8, 40)
    zero_pads(f_a, 8, 40)
    zero_pads(f_d, 8, 40)
    x_rows[...] = jnp.zeros(x_rows.shape, F32)
    f_gx[...] = jnp.zeros(f_gx.shape, F32)

    for oz in range(2):
        k = iota((896, 128), 0)
        c = iota((896, 128), 1)
        block, lane = k // 128, k % 128
        z, yy = lane % 32, lane // 32
        mask = (block == 0) & (c < 16) & (lane == 96 + 16 * oz + c)
        mask = mask | ((block == 1) & (c >= 16) & (c < 32) & (lane == 16 * oz + c - 16))
        own = (block >= 2) & (block < 6) & (z == (16, 15)[oz])
        mask = mask | (own & (c == (48, 32)[oz] + 4 * (block - 2) + yy))
        mask = mask | (
            (block == 6) & (z >= 16 * oz) & (z < 16 * oz + 16) & (c == 64 + yy * 16 + z - 16 * oz)
        )
        m_face[oz] = jnp.where(mask, 1.0, 0.0).astype(BF16)

    for group in loads[1:3]:
        for copy in group:
            copy.wait()

    for ox in range(2):
        for oy in range(2):
            own, at = (24, 4) if ox == 0 else (23, 0)
            far, at_far = (39, 0) if ox == 0 else (8, 4)
            for q in range(4):
                j = 1 + 4 * oy + q
                x_rows[2 * ox + oy, at + q : at + q + 1] = s_fr[j, own : own + 1]
                x_rows[4 + 2 * ox + oy, at_far + q : at_far + q + 1] = s_fr[j, far : far + 1]
    blank = jnp.zeros((16, 128), F32)
    for oz in range(2):
        pair = [(0, oz), (1, 1 - oz)]
        stacked = []
        for ox, oy in pair:
            rows = pl.ds(8 + 16 * ox, 16)
            parts = [s_fr[4, rows], blank] if oy else [blank, s_fr[5, rows]]
            parts += [s_fr[1 + 4 * oy + q, rows] for q in range(4)]
            parts.append(x_rows[2 * ox + oy])
            stacked.append(jnp.concatenate(parts, axis=1))
        for ox, oy in pair:
            stacked.append(jnp.concatenate([blank] * 6 + [x_rows[4 + 2 * ox + oy]], axis=1))
        packed = mapped(jnp.concatenate(stacked, axis=0), m_face[oz])
        for number, (ox, oy) in enumerate(pair):
            faces[2 * ox + oy] = packed[16 * number : 16 * number + 16]
            faces[4 + 2 * ox + oy] = packed[32 + 16 * number : 48 + 16 * number]
    pl.semaphore_wait(barrier, len(greeted))

    sends = []

    def remote(source, target, send_sem, recv_sem, device):
        copy = Remote(
            pltpu.make_async_remote_copy(
                src_ref=source,
                dst_ref=target,
                send_sem=send_sem,
                recv_sem=recv_sem,
                device_id=device,
                device_id_type=MESH,
            )
        )
        sends.append(copy)
        return copy

    layer = []
    for number, ref in enumerate((s_fr, kq_fr)):
        rows, blocks = pl.ds(8, 32), pl.ds(1, 8)
        for side, (source, target, device) in enumerate(
            (
                (ref.at[8, rows], ref.at[0, rows], around[3]),
                (ref.at[1, rows], ref.at[9, rows], around[2]),
                (ref.at[blocks, pl.ds(39, 1)], ref.at[blocks, pl.ds(7, 1)], around[1]),
                (ref.at[blocks, pl.ds(8, 1)], ref.at[blocks, pl.ds(40, 1)], around[0]),
            )
        ):
            at = 4 * number + side
            layer.append(remote(source, target, sem_s0.at[at], sem_r0.at[at], device))

    for copy in loads[7]:
        copy.wait()

    def deep_x(ref, width, send_sem, recv_sem):
        blocks = pl.ds(5, 8)
        started = []
        for side, (source, target) in enumerate(((24, 56), (56 - width, 24 - width))):
            started.append(
                remote(
                    ref.at[blocks, pl.ds(source, width)],
                    ref.at[blocks, pl.ds(target, width)],
                    send_sem.at[side],
                    recv_sem.at[side],
                    around[side],
                )
            )
        return started

    def deep_y(ref, depth, send_sem, recv_sem):
        started = []
        for q in range(depth):
            rows = pl.ds(8 + 4 * q, 64 - 8 * q)
            for side, (source, target) in enumerate(((5 + q, 13 + q), (12 - q, 4 - q))):
                at = 2 + 2 * q + side
                started.append(
                    remote(
                        ref.at[source, rows],
                        ref.at[target, rows],
                        send_sem.at[at],
                        recv_sem.at[at],
                        around[2 + side],
                    )
                )
        return started

    deep_k = deep_x(k_fr, 17, sem_sk, sem_rk)

    for group in loads[3:6]:
        for copy in group:
            copy.wait()
    rows_f = iota((32, 128), 0)
    own_f = pl.ds(8, 32)

    def fine_weights(i, carry):
        j = i + 1
        k = f_k[j, own_f]
        y_first = (lanes < 32) & (j == 1)
        y_last = (lanes >= 96) & (j == 8)
        kxm = jnp.where(rows_f == 0, k, f_k[j, pl.ds(7, 32)])
        kxp = jnp.where(rows_f == 31, k, f_k[j, pl.ds(9, 32)])
        kym = jnp.where(y_first, k, y_before(f_k, j, own_f, lanes, 32))
        kyp = jnp.where(y_last, k, y_beyond(f_k, j, own_f, lanes, 32))
        kzm = jnp.where(z_first, k, roll(k, 1))
        kzp = jnp.where(z_last, k, roll(k, 127))
        f_wx[j, own_f] = jnp.where(rows_f == 0, 0.0, 0.5 * (k + kxm))
        f_wy[j, own_f] = jnp.where(y_first, 0.0, 0.5 * (k + kym))
        f_wz[j, own_f] = jnp.where(z_first, 0.0, 0.5 * (k + kzm))
        f_inv[j, own_f] = 1.0 / (3.0 * k + 0.5 * (kxm + kxp + kym + kyp + kzm + kzp))
        return carry

    lax.fori_loop(0, 8, fine_weights, 0)
    w_f = (f_wx, f_wy, f_wz)

    def fine_base(i, carry):
        f_base[i + 1, own_f] = 0.25 * f_src[i] + coupled(f_v, w_f, i + 1, 8, 32, lanes, 32)
        return carry

    lax.fori_loop(0, 8, fine_base, 0)

    for copy in layer[:2]:
        copy.wait_recv()

    def blank_sides(ref):
        @pl.when(my == 0)
        def _():
            ref[0, 8:40] = jnp.zeros((32, 128), F32)

        @pl.when(my == N_Y - 1)
        def _():
            ref[9, 8:40] = jnp.zeros((32, 128), F32)

    blank_sides(s_fr)

    for ox in range(2):
        for oy in range(2):
            rows = pl.ds(8 + 16 * ox, 16)
            oz = (ox + oy) % 2
            shift = (128 - 96 - 16 * oz, 16 - 16 * oz)[oy] % 128
            beside = s_fr[9 * oy, rows]
            if shift:
                beside = roll(beside, shift)
            wanted = (lanes >= 16 * oy) & (lanes < 16 * oy + 16)
            faces[2 * ox + oy] = faces[2 * ox + oy] + jnp.where(wanted, beside, 0.0)

    def to_mates(source, target, send_sem, recv_sem):
        for d in FAR_FIRST:
            other = lax.rem(mx + d, N_X)
            pltpu.make_async_remote_copy(
                src_ref=source(other),
                dst_ref=target.at[mx],
                send_sem=send_sem.at[0],
                recv_sem=recv_sem.at[0],
                device_id=(other, my),
                device_id_type=MESH,
            ).start()
        group = Group(target.at[pl.ds(0, N_X - 1)], send_sem.at[0], recv_sem.at[0])
        sends.append(group)
        return [group]

    for h in range(N_X):
        ghost_out[h] = faces[picks[h]]
    ghosts = to_mates(lambda other: ghost_out.at[other], ghost_in, sem_s1, sem_r1)
    ghost_in[mx] = ghost_out[mx]

    for copy in layer:
        copy.wait_recv()
    blank_sides(kq_fr)
    for ref in (s_fr, kq_fr):

        @pl.when(mx == 0)
        def _():
            ref[1:9, 7:8] = jnp.zeros((8, 1, 128), F32)

        @pl.when(mx == N_X - 1)
        def _():
            ref[1:9, 40:41] = jnp.zeros((8, 1, 128), F32)

    for copy in loads[6]:
        copy.wait()

    def coarse_residual(i, carry):
        j = i + 1
        s = s_fr[j, own_f]
        k = kq_fr[j, own_f]

        def flux(k_there, s_there):
            return (k + k_there) * (s - s_there)

        before, beyond = pl.ds(7, 32), pl.ds(9, 32)
        total = flux(kq_fr[j, before], s_fr[j, before]) + flux(kq_fr[j, beyond], s_fr[j, beyond])
        total = total + flux(
            y_before(kq_fr, j, own_f, lanes, 32), y_before(s_fr, j, own_f, lanes, 32)
        )
        total = total + flux(
            y_beyond(kq_fr, j, own_f, lanes, 32), y_beyond(s_fr, j, own_f, lanes, 32)
        )
        total = total + flux(
            jnp.where(z_first, 0.0, roll(k, 1)), jnp.where(z_first, 0.0, roll(s, 1))
        )
        total = total + flux(
            jnp.where(z_last, 0.0, roll(k, 127)), jnp.where(z_last, 0.0, roll(s, 127))
        )
        r_fr[i + 5, pl.ds(24, 32)] = src_c[i] - 0.5 * total
        return carry

    lax.fori_loop(0, 8, coarse_residual, 0)
    deep_r = deep_x(r_fr, 16, sem_sr, sem_rr)

    for copy in deep_k:
        copy.wait_recv()

    @pl.when(mx == 0)
    def _():
        k_fr[5:13, 7:24] = jnp.zeros((8, 17, 128), F32)

    @pl.when(mx == N_X - 1)
    def _():
        k_fr[5:13, 56:73] = jnp.zeros((8, 17, 128), F32)

    deep_k += deep_y(k_fr, 5, sem_sk, sem_rk)

    k = iota((128, 1280), 0)
    c = iota((128, 1280), 1)
    y, z = c // 32, c % 32
    inner = c < 1024
    mask = inner & (y == 0) & (k == z // 2)
    mask = mask | (inner & (y == 31) & (k == 16 + z // 2))
    mask = mask | (inner & (z == 0) & (k == 32 + y // 2))
    mask = mask | (inner & (z == 31) & (k == 48 + y // 2))
    mask = mask | ((c >= 1024) & (k == 64 + (y - 32) // 2 * 16 + z // 2))
    put(m_ghost, mask)
    k, c = iota((512, 128), 0), iota((512, 128), 1)
    put(m_down, c == k // 64 * 16 + k % 32 // 2)

    for copy in ghosts:
        copy.wait_recv()
    high_x = (own_pos >> 2) & 1
    other_x = owner_x + 2 * high_x - 1
    beyond_x = ghost_in[jnp.clip(other_x, 0, N_X - 1)]
    inside = jnp.where((other_x >= 0) & (other_x < N_X), 1.0, 0.0)
    mine = ghost_in[owner_x] + inside * beyond_x
    dup[0, pl.ds(0, 16, stride=2)] = mine
    dup[0, pl.ds(1, 16, stride=2)] = mine
    widened = mapped(dup[0], m_ghost[...])
    for q in range(4):
        for t in range(2):
            piece = widened[:, 1024 + 128 * t : 1152 + 128 * t]
            f_gx[2 * q + t, 0:1] = piece[2 * q : 2 * q + 1]
            f_gx[2 * q + t, 31:32] = piece[8 + 2 * q : 9 + 2 * q]
    for i in range(8):
        j = i + 1
        ghost = f_k[j, own_f] * (widened[:, 128 * i : 128 * i + 128] + f_gx[i])
        f_gx[i] = ghost
        f_a[j, own_f] = jnp.where(first_f, (f_base[j, own_f] + ghost) * f_inv[j, own_f], 0.0)
    for i in range(8):
        j = i + 1
        around_a = coupled(f_a, w_f, j, 8, 32, lanes, 32)
        fresh = (0.25 * f_src[i] + f_gx[i] + around_a) * f_inv[j, own_f]
        f_sm[i] = jnp.where(first_f, f_a[j, own_f], fresh)
        f_d[j, own_f] = jnp.where(first_f, 0.0, fresh - f_v[j, own_f])
    for i in range(8):
        f_res[i] = jnp.where(first_f, coupled(f_d, w_f, i + 1, 8, 32, lanes, 32), 0.0)
    stacked = []
    for b in range(2):
        parts = [
            f_res[4 * b + q, pl.ds(0, 16, stride=2)] + f_res[4 * b + q, pl.ds(1, 16, stride=2)]
            for q in range(4)
        ]
        stacked.append(jnp.concatenate(parts, axis=1))
    packed = 0.5 * mapped(jnp.concatenate(stacked, axis=0), m_down[...])
    box_out[0] = packed[:16]
    box_out[1] = packed[16:]
    gathered = to_mates(lambda other: box_out, box_in, sem_s2, sem_r2)
    box_in[mx] = box_out[...]
    for copy in deep_r:
        copy.wait_recv()
    deep_r += deep_y(r_fr, 4, sem_sr, sem_rr)

    zero_pads(wx, 8, 72)
    zero_pads(wy, 8, 72)
    zero_pads(e_a, 8, 72)
    zero_pads(e_b, 8, 72)
    for ref in (b_k, b_wx, b_wy, b_ua, b_ub):
        zero_pads(ref, 8, 40)
    for oz in range(2):
        k, c = iota((128, 256), 0), iota((128, 256), 1)
        m_exp[oz] = jnp.where((k // 16 == c // 32) & (c % 32 == 16 * oz + k % 16), 1.0, 0.0).astype(BF16)
        k, c = iota((256, 128), 1), iota((256, 128), 0)
        m_com[oz] = jnp.where((k // 16 == c // 32) & (c % 32 == 16 * oz + k % 16), 1.0, 0.0).astype(BF16)
    k, c = iota((128, 512), 0), iota((128, 512), 1)
    put(m_up, k == c // 64 * 16 + c % 32 // 2)
    k, c = iota((128, 1024), 0), iota((128, 1024), 1)
    put(m_four, k == c // 128 * 16 + c % 32 // 4)

    for copy in deep_k:
        copy.wait_recv()
    @pl.when(my == 0)
    def _():
        k_fr[0:5] = jnp.zeros((5, 80, 128), F32)

    @pl.when(my == N_Y - 1)
    def _():
        k_fr[13:18] = jnp.zeros((5, 80, 128), F32)

    window = pl.ds(8, 64)

    def coarse_weights(i, carry):
        j = i + 1
        k = k_fr[j, window]
        kxm = k_fr[j, pl.ds(7, 64)]
        kxp = k_fr[j, pl.ds(9, 64)]
        kym = y_before(k_fr, j, window, lanes, 32)
        kyp = y_beyond(k_fr, j, window, lanes, 32)
        kzm = jnp.where(z_first, 0.0, roll(k, 1))
        kzp = jnp.where(z_last, 0.0, roll(k, 127))
        wx[j, window] = 0.5 * (k + kxm)
        wy[j, window] = 0.5 * (k + kym)
        wz[j, window] = jnp.where(z_first, 0.0, 0.5 * (k + kzm))
        inverse = 1.0 / (3.0 * k + 0.5 * (kxm + kxp + kym + kyp + kzm + kzp))
        inverse = jnp.where(k > 0.0, inverse, 0.0)
        inv_a[j, window] = jnp.where(first_c, inverse, 0.0)
        inv_b[j, window] = jnp.where(first_c, 0.0, inverse)
        return carry

    lax.fori_loop(0, 16, coarse_weights, 0)
    w_c = (wx, wy, wz)

    def coarsened(ref):
        stacked = []
        for b in range(4):
            parts = [
                ref[1 + 4 * b + q, pl.ds(8, 32, stride=2)]
                + ref[1 + 4 * b + q, pl.ds(9, 32, stride=2)]
                for q in range(4)
            ]
            stacked.append(jnp.concatenate(parts, axis=1))
        return mapped(jnp.concatenate(stacked, axis=0), m_down[...])

    summed = coarsened(k_fr)
    own_b = pl.ds(8, 32)
    for b in range(4):
        b_k[1 + b, own_b] = 0.125 * summed[32 * b : 32 * b + 32]
    zb_first = lanes % 16 == 0
    zb_last = lanes % 16 == 15
    for b in range(4):
        j = b + 1
        k = b_k[j, own_b]
        kxm = b_k[j, pl.ds(7, 32)]
        kxp = b_k[j, pl.ds(9, 32)]
        kym = y_before(b_k, j, own_b, lanes, 16)
        kyp = y_beyond(b_k, j, own_b, lanes, 16)
        kzm = jnp.where(zb_first, 0.0, roll(k, 1))
        kzp = jnp.where(zb_last, 0.0, roll(k, 127))
        b_wx[j, own_b] = 0.5 * (k + kxm)
        b_wy[j, own_b] = 0.5 * (k + kym)
        b_wz[j, own_b] = jnp.where(zb_first, 0.0, 0.5 * (k + kzm))
        inverse = 1.0 / (3.0 * k + 0.5 * (kxm + kxp + kym + kyp + kzm + kzp))
        inverse = jnp.where(k > 0.0, inverse, 0.0)
        b_ia[b] = jnp.where(first_b, inverse, 0.0)
        b_ib[b] = jnp.where(first_b, 0.0, inverse)

    for copy in deep_r:
        copy.wait_recv()
    for copy in deep_r:
        copy.wait_send()

    for copy in gathered:
        copy.wait_recv()
    for ye in (1, 2):
        for sx in range(4):
            boxes[ye, sx] = box_in[jnp.maximum(found[4 * ye + sx], 0)]
    beside = [
        remote(boxes.at[1], boxes.at[3], sem_s3.at[0], sem_r3.at[0], around[2]),
        remote(boxes.at[2], boxes.at[0], sem_s3.at[1], sem_r3.at[1], around[3]),
    ]

    def compose(ye):
        for oz in range(2):
            pair = [sx for sx in range(4) if (sx + ye) % 2 == oz]
            stacked = [boxes[ye, sx, b] for sx in pair for b in range(2)]
            wide = mapped(jnp.concatenate(stacked, axis=0), m_exp[oz])
            for number, sx in enumerate(pair):
                here = jnp.where(found[4 * ye + sx] >= 0, 1.0, 0.0)
                covered = jnp.where(lanes % 32 // 16 == oz, here, 0.0) > 0.5
                rows = pl.ds(8 + 16 * sx, 16)
                for q in range(4):
                    b, t = q // 2, q % 2
                    j = 1 + 4 * ye + q
                    at = 32 * number + 16 * b
                    part = wide[at : at + 16, 128 * t : 128 * t + 128]
                    mixed = jnp.where(covered, part, r_fr[j, rows])
                    r_fr[j, rows] = mixed
                    e_a[j, rows] = mixed * inv_a[j, rows]

    compose(1)
    compose(2)
    for copy in beside:
        copy.wait_recv()
    compose(0)
    compose(3)

    def second(i, carry):
        j = i + 1
        fresh = r_fr[j, window] + coupled(e_a, w_c, j, 8, 64, lanes, 32)
        e_b[j, window] = fresh * inv_b[j, window]
        return carry

    lax.fori_loop(0, 16, second, 0, unroll=UNROLL)

    own_c = pl.ds(24, 32)
    for oz in range(2):
        pair = [(0, oz), (1, 1 - oz)]
        stacked = []
        for ox, oy in pair:
            rows = pl.ds(24 + 16 * ox, 16)
            for b in range(2):
                parts = [
                    e_a[5 + 4 * oy + 2 * b + t, rows] + e_b[5 + 4 * oy + 2 * b + t, rows]
                    for t in range(2)
                ]
                stacked.append(jnp.concatenate(parts, axis=1))
        packed = mapped(jnp.concatenate(stacked, axis=0), m_com[oz])
        for number, (ox, oy) in enumerate(pair):
            for b in range(2):
                at = 32 * number + 16 * b
                e_oct[2 * ox + oy, b] = packed[at : at + 16]
    for h in range(N_X):
        e_out[h] = e_oct[octs[h]]
    returned = to_mates(lambda other: e_out.at[other], e_in, sem_s4, sem_r4)
    e_in[mx] = e_out[mx]

    def remaining(i, carry):
        j = i + 1
        left[j, window] = jnp.where(first_c, coupled(e_b, w_c, j, 8, 64, lanes, 32), 0.0)
        return carry

    lax.fori_loop(0, 16, remaining, 0, unroll=UNROLL)
    summed = 0.5 * coarsened(left)
    for b in range(4):
        source = summed[32 * b : 32 * b + 32]
        b_fa[b] = source * b_ia[b]
        b_fb[b] = source * b_ib[b]
        b_ua[1 + b, own_b] = source * b_ia[b]
    w_b = (b_wx, b_wy, b_wz)
    for half in range(2 * SWEEPS - 1):
        into, out_of = ((b_ub, b_ua), (b_ua, b_ub))[half % 2]
        fixed, inverse = ((b_fb, b_ib), (b_fa, b_ia))[half % 2]
        for b in range(4):
            into[1 + b, own_b] = fixed[b] + inverse[b] * coupled(
                out_of, w_b, 1 + b, 8, 32, lanes, 16
            )

    for ox in range(2):
        for oy in range(2):
            rows = pl.ds(16 + 8 * ox, 8)
            u_oct[2 * ox + oy] = b_ua[2 + oy, rows] + b_ub[2 + oy, rows]
    for h in range(N_X):
        u_out[h] = u_oct[octs[h]]
    settled = to_mates(lambda other: u_out.at[other], u_in, sem_s5, sem_r5)
    u_in[mx] = u_out[mx]

    def doubled(ref, pieces):
        for b, piece in enumerate(pieces):
            ref[b, pl.ds(0, 16, stride=2)] = piece
            ref[b, pl.ds(1, 16, stride=2)] = piece
        return mapped(jnp.concatenate([ref[0], ref[1]], axis=0), m_up[...])

    wide = doubled(dup, [b_ua[2 + b, pl.ds(16, 16)] + b_ub[2 + b, pl.ds(16, 16)] for b in range(2)])
    for j in range(8):
        b, q = j // 4, j % 4
        part = wide[32 * b : 32 * b + 32, 128 * q : 128 * q + 128]
        total = e_a[5 + j, own_c] + e_b[5 + j, own_c] + part
        out[0, :, 128 * j : 128 * j + 128] = s_fr[1 + j, own_f] + total

    for copy in returned:
        copy.wait_recv()
    got = e_in.at[owner_x]
    wide = doubled(dup2, [got[0], got[1]])
    for j in range(8):
        b, q = j // 4, j % 4
        f_sm[j] = f_sm[j] + wide[32 * b : 32 * b + 32, 128 * q : 128 * q + 128]
    for copy in sends:
        copy.wait_send()
    for copy in settled:
        copy.wait_recv()
    tile = u_in[owner_x]
    side = jnp.where(own_oz == 1, 1.0, 0.0)
    tile = jnp.where(jnp.zeros((8, 128), F32) + side > 0.5, roll(tile, 120), tile)
    for t in range(4):
        dup[0, pl.ds(t, 8, stride=4)] = tile
    wide = mapped(dup[0], m_four[...])
    for j in range(8):
        out[1, :, 128 * j : 128 * j + 128] = f_sm[j] + wide[:, 128 * j : 128 * j + 128]


def scratch():
    v = pltpu.VMEM
    lists = [pltpu.SMEM((N_X * N_Y,), jnp.int32), pltpu.SMEM((3,), jnp.int32)]
    shapes = [(10, 48, 128)] * 2 + [(8, 32, 128)]
    shapes += [(8, 32, 128)] + [(10, 48, 128)] * 8 + [(8, 32, 128), (10, 48, 128)]
    shapes += [(8, 32, 128)] * 2
    shapes += [(18, 80, 128)] * 10
    shapes += [(6, 48, 128)] * 4 + [(4, 32, 128)] * 4 + [(6, 48, 128)] * 2
    shapes += [(8, 16, 128), (8, 16, 128), (N_X, 16, 128), (N_X, 16, 128)]
    shapes += [(2, 16, 128), (N_X, 2, 16, 128), (4, 4, 2, 16, 128)]
    shapes += [(4, 2, 16, 128), (N_X, 2, 16, 128), (N_X, 2, 16, 128)]
    shapes += [(4, 8, 128), (N_X, 8, 128), (N_X, 8, 128)]
    shapes += [(2, 32, 128)] * 2
    result = lists + [v(shape, F32) for shape in shapes]
    maps = [(2, 896, 128), (128, 1280), (512, 128), (128, 512), (2, 128, 256), (2, 256, 128)]
    result += [v(shape, BF16) for shape in maps + [(128, 1024)]]
    dma = pltpu.SemaphoreType.DMA
    result += [dma((9,))] + [dma((8,))] * 2 + [dma((12,))] * 4 + [dma((1,))] * 4 + [dma((2,))] * 2
    return result + [dma((1,))] * 4


def on_device(
    coarse_source,
    coarse_coefficient,
    coarse_start,
    fine_source,
    fine_coefficient,
    fine_start,
    fine_position,
    first_colour,
):
    vmem = pl.BlockSpec(memory_space=pltpu.VMEM)
    hbm = pl.BlockSpec(memory_space=pltpu.HBM)
    both = pl.pallas_call(
        kernel,
        out_shape=jax.ShapeDtypeStruct((2, 32, 1024), F32),
        in_specs=[hbm] * 8,
        out_specs=vmem,
        scratch_shapes=scratch(),
        compiler_params=pltpu.CompilerParams(
            collective_id=0, has_side_effects=True, vmem_limit_bytes=48 << 20
        ),
    )(
        *[
            pltpu.with_memory_space_constraint(array, pltpu.HBM)
            for array in (
                fine_position,
                first_colour,
                coarse_source,
                coarse_coefficient,
                coarse_start,
                fine_source,
                fine_coefficient,
                fine_start,
            )
        ],
    )
    return both[0], both[1:]


def solution(mesh):
    placed = (
        P("gx", "gy"),
        P("gx", "gy"),
        P("gx", "gy"),
        P(("gx", "gy"), None, None),
        P(("gx", "gy"), None, None),
        P(("gx", "gy"), None, None),
        P(),
        P(),
    )
    return jax.shard_map(
        on_device,
        mesh=mesh,
        in_specs=placed,
        out_specs=(P("gx", "gy"), P(("gx", "gy"), None, None)),
        check_vma=False,
    )
```

```python
import functools

import jax
import jax.numpy as jnp
from jax import lax
from jax.experimental import pallas as pl
from jax.experimental.pallas import tpu as pltpu
from jax.sharding import PartitionSpec as P


MESH = pl.DeviceIdType.MESH
F32 = jnp.float32
BF16 = jnp.bfloat16
SWEEPS = 4
N_X = 16
N_Y = 8
FAR_FIRST = (10, 6, 9, 11, 7, 5, 14, 2, 8, 13, 15, 3, 1, 12, 4)
UNROLL = 16


def iota(shape, dim):
    return lax.broadcasted_iota(jnp.int32, shape, dim)


def halves(values):
    high = values.astype(BF16)
    low = (values - high.astype(F32)).astype(BF16)
    return jnp.concatenate([high, low], axis=0)


def mapped(values, matrix):
    rows = values.shape[0]
    both = jnp.dot(halves(values), matrix, preferred_element_type=F32)
    return both[:rows] + both[rows:]


def roll(values, amount):
    return pltpu.roll(values, amount, axis=1)


def y_before(ref, j, rows, lanes, step):
    return roll(jnp.where(lanes >= 128 - step, ref[j - 1, rows], ref[j, rows]), step)


def y_beyond(ref, j, rows, lanes, step):
    return roll(jnp.where(lanes < step, ref[j + 1, rows], ref[j, rows]), 128 - step)


def coupled(value, weights, j, low, count, lanes, step):
    wx, wy, wz = weights
    here = pl.ds(low, count)
    before = pl.ds(low - 1, count)
    beyond = pl.ds(low + 1, count)
    mid = value[j, here]
    w_y = wy[j, here]
    w_z = wz[j, here]
    total = wx[j, here] * value[j, before] + wx[j, beyond] * value[j, beyond]
    total = total + w_y * y_before(value, j, here, lanes, step)
    ahead = jnp.where(lanes < step, wy[j + 1, here] * value[j + 1, here], w_y * mid)
    total = total + roll(ahead, 128 - step)
    return total + w_z * roll(mid, 1) + roll(w_z * mid, 127)


def zero_pads(ref, low, high):
    blocks, rows, _ = ref.shape
    ref[0] = jnp.zeros((rows, 128), F32)
    ref[blocks - 1] = jnp.zeros((rows, 128), F32)
    ref[1 : blocks - 1, :low] = jnp.zeros((blocks - 2, low, 128), F32)
    ref[1 : blocks - 1, high:] = jnp.zeros((blocks - 2, rows - high, 128), F32)


class Remote:
    def __init__(self, copy):
        self.copy = copy
        self.landed = False
        self.left = False
        copy.start()

    def wait_recv(self):
        if not self.landed:
            self.copy.wait_recv()
        self.landed = True

    def wait_send(self):
        if not self.left:
            self.copy.wait_send()
        self.left = True


class Group:
    def __init__(self, span, send_sem, recv_sem):
        self.sent = pltpu.make_async_copy(span, span, send_sem)
        self.landed = pltpu.make_async_copy(span, span, recv_sem)
        self.left = False

    def wait_recv(self):
        self.landed.wait()

    def wait_send(self):
        if not self.left:
            self.sent.wait()
        self.left = True


def put(ref, mask):
    ref[...] = jnp.where(mask, 1.0, 0.0).astype(BF16)


def kernel(
    pos_hbm,
    colours_hbm,
    c_source,
    c_coeff,
    c_start,
    f_source,
    f_coeff,
    f_start,
    out,
    pos,
    colours,
    s_fr,
    kq_fr,
    src_c,
    f_src,
    f_k,
    f_v,
    f_wx,
    f_wy,
    f_wz,
    f_inv,
    f_base,
    f_a,
    f_sm,
    f_d,
    f_res,
    f_gx,
    k_fr,
    r_fr,
    wx,
    wy,
    wz,
    inv_a,
    inv_b,
    e_a,
    e_b,
    left,
    b_k,
    b_wx,
    b_wy,
    b_wz,
    b_ia,
    b_ib,
    b_fa,
    b_fb,
    b_ua,
    b_ub,
    x_rows,
    faces,
    ghost_out,
    ghost_in,
    box_out,
    box_in,
    boxes,
    e_oct,
    e_out,
    e_in,
    u_oct,
    u_out,
    u_in,
    dup,
    dup2,
    m_face,
    m_ghost,
    m_down,
    m_up,
    m_exp,
    m_com,
    m_four,
    sem_l,
    sem_s0,
    sem_r0,
    sem_sk,
    sem_rk,
    sem_sr,
    sem_rr,
    sem_s1,
    sem_r1,
    sem_s2,
    sem_r2,
    sem_s3,
    sem_r3,
    sem_s4,
    sem_r4,
    sem_s5,
    sem_r5,
):
    mx = lax.axis_index("gx")
    my = lax.axis_index("gy")
    x_up, x_dn = lax.rem(mx + 1, N_X), lax.rem(mx + N_X - 1, N_X)
    y_up, y_dn = lax.rem(my + 1, N_Y), lax.rem(my + N_Y - 1, N_Y)
    around = [
        (x_dn, my),
        (x_up, my),
        (mx, y_dn),
        (mx, y_up),
    ]
    mates = [(lax.rem(mx + d, N_X), my) for d in FAR_FIRST]

    barrier = pltpu.get_barrier_semaphore()
    greeted = mates + around[2:]
    for device in greeted:
        pl.semaphore_signal(barrier, inc=1, device_id=device, device_id_type=MESH)

    loads = [
        [
            pltpu.make_async_copy(pos_hbm, pos, sem_l.at[7]),
            pltpu.make_async_copy(colours_hbm, colours, sem_l.at[8]),
        ]
    ]
    for copy in loads[0]:
        copy.start()

    def load(number, source, target, span):
        for j in range(8):
            pltpu.make_async_copy(source(j), target(j), sem_l.at[number]).start()
        loads.append([pltpu.make_async_copy(span, span, sem_l.at[number])])

    def chunk(j):
        return pl.ds(128 * j, 128)

    load(0, lambda j: c_start.at[:, chunk(j)], lambda j: s_fr.at[1 + j, pl.ds(8, 32)], s_fr.at[pl.ds(1, 8), pl.ds(8, 32)])
    load(1, lambda j: c_coeff.at[:, chunk(j)], lambda j: kq_fr.at[1 + j, pl.ds(8, 32)], kq_fr.at[pl.ds(1, 8), pl.ds(8, 32)])
    load(2, lambda j: f_coeff.at[0, :, chunk(j)], lambda j: f_k.at[1 + j, pl.ds(8, 32)], f_k.at[pl.ds(1, 8), pl.ds(8, 32)])
    load(3, lambda j: f_start.at[0, :, chunk(j)], lambda j: f_v.at[1 + j, pl.ds(8, 32)], f_v.at[pl.ds(1, 8), pl.ds(8, 32)])
    load(4, lambda j: f_source.at[0, :, chunk(j)], lambda j: f_src.at[j], f_src)
    load(5, lambda j: c_source.at[:, chunk(j)], lambda j: src_c.at[j], src_c)
    load(6, lambda j: c_coeff.at[:, chunk(j)], lambda j: k_fr.at[5 + j, pl.ds(24, 32)], k_fr.at[pl.ds(5, 8), pl.ds(24, 32)])

    for q in range(5):
        for j in (4 - q, 13 + q):
            for low, high in ((0, 8 + 4 * q), (72 - 4 * q, 80)):
                k_fr[j, low:high] = jnp.zeros((high - low, 128), F32)
                r_fr[j, low:high] = jnp.zeros((high - low, 128), F32)
    for copy in loads[0]:
        copy.wait()
    own_pos = pos[mx * N_Y + my]
    owner_x = own_pos >> 6
    own_oz = own_pos & 1

    slots = []
    for ye in range(4):
        row = (my, y_dn, y_up)[1 if ye == 0 else (2 if ye == 3 else 0)]
        for sx in range(4):
            ox, oy = (sx + 1) % 2, (ye + 1) % 2
            octant = 4 * ox + 2 * oy + (ox + oy) % 2
            column = mx + (-1, 0, 0, 1)[sx]
            slots.append((row, (column * N_Y + row) * 8 + octant))

    def look(h, found):
        held = [pos[h * N_Y + row] for row in (my, y_dn, y_up)]
        result = []
        for number, (row, wanted) in enumerate(slots):
            ye = number // 4
            at = held[1 if ye == 0 else (2 if ye == 3 else 0)]
            result.append(jnp.where(at == wanted, h, found[number]))
        return tuple(result)

    found = lax.fori_loop(0, N_X, look, tuple(jnp.int32(-1) for _ in slots))
    octs, picks = [], []
    for h in range(N_X):
        at = pos[h * N_Y + my]
        octant, away = (at >> 1) & 3, (at >> 6) - mx
        pick = jnp.where((away == 1) & (octant < 2), 4 + octant, 0)
        pick = jnp.where((away == -1) & (octant >= 2), 4 + octant, pick)
        octs.append(octant)
        picks.append(jnp.where(away == 0, octant, pick))

    lanes = iota((1, 128), 1)
    z_first = lanes % 32 == 0
    z_last = lanes % 32 == 31
    parity = (iota((8, 128), 0) + iota((8, 128), 1) // 32 + iota((8, 128), 1)) % 2
    parity_b = (iota((8, 128), 0) + iota((8, 128), 1) // 16 + iota((8, 128), 1)) % 2

    def painted(base, colour, rows):
        flags = jnp.where(base == colour, 1.0, 0.0)
        return jnp.concatenate([flags] * (rows // 8), axis=0) > 0.5

    first_f = painted(parity, colours[0], 32)
    first_c = painted(parity, colours[1], 64)
    first_b = painted(parity_b, colours[2], 32)

    zero_pads(f_v, 8, 40)
    zero_pads(f_wx, 8, 40)
    zero_pads(f_wy, 8, 40)
    zero_pads(f_a, 8, 40)
    zero_pads(f_d, 8, 40)
    x_rows[...] = jnp.zeros(x_rows.shape, F32)
    f_gx[...] = jnp.zeros(f_gx.shape, F32)

    for oz in range(2):
        k = iota((896, 128), 0)
        c = iota((896, 128), 1)
        block, lane = k // 128, k % 128
        z, yy = lane % 32, lane // 32
        mask = (block == 0) & (c < 16) & (lane == 96 + 16 * oz + c)
        mask = mask | ((block == 1) & (c >= 16) & (c < 32) & (lane == 16 * oz + c - 16))
        own = (block >= 2) & (block < 6) & (z == (16, 15)[oz])
        mask = mask | (own & (c == (48, 32)[oz] + 4 * (block - 2) + yy))
        mask = mask | (
            (block == 6) & (z >= 16 * oz) & (z < 16 * oz + 16) & (c == 64 + yy * 16 + z - 16 * oz)
        )
        m_face[oz] = jnp.where(mask, 1.0, 0.0).astype(BF16)

    for group in loads[1:3]:
        for copy in group:
            copy.wait()

    for ox in range(2):
        for oy in range(2):
            own, at = (24, 4) if ox == 0 else (23, 0)
            far, at_far = (39, 0) if ox == 0 else (8, 4)
            for q in range(4):
                j = 1 + 4 * oy + q
                x_rows[2 * ox + oy, at + q : at + q + 1] = s_fr[j, own : own + 1]
                x_rows[4 + 2 * ox + oy, at_far + q : at_far + q + 1] = s_fr[j, far : far + 1]
    blank = jnp.zeros((16, 128), F32)
    for oz in range(2):
        pair = [(0, oz), (1, 1 - oz)]
        stacked = []
        for ox, oy in pair:
            rows = pl.ds(8 + 16 * ox, 16)
            parts = [s_fr[4, rows], blank] if oy else [blank, s_fr[5, rows]]
            parts += [s_fr[1 + 4 * oy + q, rows] for q in range(4)]
            parts.append(x_rows[2 * ox + oy])
            stacked.append(jnp.concatenate(parts, axis=1))
        for ox, oy in pair:
            stacked.append(jnp.concatenate([blank] * 6 + [x_rows[4 + 2 * ox + oy]], axis=1))
        packed = mapped(jnp.concatenate(stacked, axis=0), m_face[oz])
        for number, (ox, oy) in enumerate(pair):
            faces[2 * ox + oy] = packed[16 * number : 16 * number + 16]
            faces[4 + 2 * ox + oy] = packed[32 + 16 * number : 48 + 16 * number]
    pl.semaphore_wait(barrier, len(greeted))

    sends = []

    def remote(source, target, send_sem, recv_sem, device):
        copy = Remote(
            pltpu.make_async_remote_copy(
                src_ref=source,
                dst_ref=target,
                send_sem=send_sem,
                recv_sem=recv_sem,
                device_id=device,
                device_id_type=MESH,
            )
        )
        sends.append(copy)
        return copy

    layer = []
    for number, ref in enumerate((s_fr, kq_fr)):
        rows, blocks = pl.ds(8, 32), pl.ds(1, 8)
        for side, (source, target, device) in enumerate(
            (
                (ref.at[8, rows], ref.at[0, rows], around[3]),
                (ref.at[1, rows], ref.at[9, rows], around[2]),
                (ref.at[blocks, pl.ds(39, 1)], ref.at[blocks, pl.ds(7, 1)], around[1]),
                (ref.at[blocks, pl.ds(8, 1)], ref.at[blocks, pl.ds(40, 1)], around[0]),
            )
        ):
            at = 4 * number + side
            layer.append(remote(source, target, sem_s0.at[at], sem_r0.at[at], device))

    for copy in loads[7]:
        copy.wait()

    def deep_x(ref, width, send_sem, recv_sem):
        blocks = pl.ds(5, 8)
        started = []
        for side, (source, target) in enumerate(((24, 56), (56 - width, 24 - width))):
            started.append(
                remote(
                    ref.at[blocks, pl.ds(source, width)],
                    ref.at[blocks, pl.ds(target, width)],
                    send_sem.at[side],
                    recv_sem.at[side],
                    around[side],
                )
            )
        return started

    def deep_y(ref, depth, send_sem, recv_sem):
        for q in range(depth):
            rows = pl.ds(8 + 4 * q, 64 - 8 * q)
            for side, (source, target) in enumerate(((5 + q, 13 + q), (12 - q, 4 - q))):
                pltpu.make_async_remote_copy(
                    src_ref=ref.at[source, rows],
                    dst_ref=ref.at[target, rows],
                    send_sem=send_sem.at[2],
                    recv_sem=recv_sem.at[2],
                    device_id=around[2 + side],
                    device_id_type=MESH,
                ).start()
        total = 2 * sum(64 - 8 * q for q in range(depth))
        span = ref.at[pl.ds(1, 8), pl.ds(8, total // 8)]
        group = Group(span, send_sem.at[2], recv_sem.at[2])
        sends.append(group)
        return [group]

    deep_k = deep_x(k_fr, 17, sem_sk, sem_rk)

    for group in loads[3:6]:
        for copy in group:
            copy.wait()
    rows_f = iota((32, 128), 0)
    own_f = pl.ds(8, 32)

    def fine_weights(i, carry):
        j = i + 1
        k = f_k[j, own_f]
        y_first = (lanes < 32) & (j == 1)
        y_last = (lanes >= 96) & (j == 8)
        kxm = jnp.where(rows_f == 0, k, f_k[j, pl.ds(7, 32)])
        kxp = jnp.where(rows_f == 31, k, f_k[j, pl.ds(9, 32)])
        kym = jnp.where(y_first, k, y_before(f_k, j, own_f, lanes, 32))
        kyp = jnp.where(y_last, k, y_beyond(f_k, j, own_f, lanes, 32))
        kzm = jnp.where(z_first, k, roll(k, 1))
        kzp = jnp.where(z_last, k, roll(k, 127))
        f_wx[j, own_f] = jnp.where(rows_f == 0, 0.0, 0.5 * (k + kxm))
        f_wy[j, own_f] = jnp.where(y_first, 0.0, 0.5 * (k + kym))
        f_wz[j, own_f] = jnp.where(z_first, 0.0, 0.5 * (k + kzm))
        f_inv[j, own_f] = 1.0 / (3.0 * k + 0.5 * (kxm + kxp + kym + kyp + kzm + kzp))
        return carry

    lax.fori_loop(0, 8, fine_weights, 0)
    w_f = (f_wx, f_wy, f_wz)

    def fine_base(i, carry):
        f_base[i + 1, own_f] = 0.25 * f_src[i] + coupled(f_v, w_f, i + 1, 8, 32, lanes, 32)
        return carry

    lax.fori_loop(0, 8, fine_base, 0)

    for copy in layer[:2]:
        copy.wait_recv()

    def blank_sides(ref):
        @pl.when(my == 0)
        def _():
            ref[0, 8:40] = jnp.zeros((32, 128), F32)

        @pl.when(my == N_Y - 1)
        def _():
            ref[9, 8:40] = jnp.zeros((32, 128), F32)

    blank_sides(s_fr)

    for ox in range(2):
        for oy in range(2):
            rows = pl.ds(8 + 16 * ox, 16)
            oz = (ox + oy) % 2
            shift = (128 - 96 - 16 * oz, 16 - 16 * oz)[oy] % 128
            beside = s_fr[9 * oy, rows]
            if shift:
                beside = roll(beside, shift)
            wanted = (lanes >= 16 * oy) & (lanes < 16 * oy + 16)
            faces[2 * ox + oy] = faces[2 * ox + oy] + jnp.where(wanted, beside, 0.0)

    def to_mates(source, target, send_sem, recv_sem):
        for d in FAR_FIRST:
            other = lax.rem(mx + d, N_X)
            pltpu.make_async_remote_copy(
                src_ref=source(other),
                dst_ref=target.at[mx],
                send_sem=send_sem.at[0],
                recv_sem=recv_sem.at[0],
                device_id=(other, my),
                device_id_type=MESH,
            ).start()
        group = Group(target.at[pl.ds(0, N_X - 1)], send_sem.at[0], recv_sem.at[0])
        sends.append(group)
        return [group]

    for h in range(N_X):
        ghost_out[h] = faces[picks[h]]
    ghosts = to_mates(lambda other: ghost_out.at[other], ghost_in, sem_s1, sem_r1)
    ghost_in[mx] = ghost_out[mx]

    for copy in layer:
        copy.wait_recv()
    blank_sides(kq_fr)
    for ref in (s_fr, kq_fr):

        @pl.when(mx == 0)
        def _():
            ref[1:9, 7:8] = jnp.zeros((8, 1, 128), F32)

        @pl.when(mx == N_X - 1)
        def _():
            ref[1:9, 40:41] = jnp.zeros((8, 1, 128), F32)

    for copy in loads[6]:
        copy.wait()

    def coarse_residual(i, carry):
        j = i + 1
        s = s_fr[j, own_f]
        k = kq_fr[j, own_f]

        def flux(k_there, s_there):
            return (k + k_there) * (s - s_there)

        before, beyond = pl.ds(7, 32), pl.ds(9, 32)
        total = flux(kq_fr[j, before], s_fr[j, before]) + flux(kq_fr[j, beyond], s_fr[j, beyond])
        total = total + flux(
            y_before(kq_fr, j, own_f, lanes, 32), y_before(s_fr, j, own_f, lanes, 32)
        )
        total = total + flux(
            y_beyond(kq_fr, j, own_f, lanes, 32), y_beyond(s_fr, j, own_f, lanes, 32)
        )
        total = total + flux(
            jnp.where(z_first, 0.0, roll(k, 1)), jnp.where(z_first, 0.0, roll(s, 1))
        )
        total = total + flux(
            jnp.where(z_last, 0.0, roll(k, 127)), jnp.where(z_last, 0.0, roll(s, 127))
        )
        r_fr[i + 5, pl.ds(24, 32)] = src_c[i] - 0.5 * total
        return carry

    lax.fori_loop(0, 8, coarse_residual, 0)
    deep_r = deep_x(r_fr, 16, sem_sr, sem_rr)

    for copy in deep_k:
        copy.wait_recv()

    @pl.when(mx == 0)
    def _():
        k_fr[5:13, 7:24] = jnp.zeros((8, 17, 128), F32)

    @pl.when(mx == N_X - 1)
    def _():
        k_fr[5:13, 56:73] = jnp.zeros((8, 17, 128), F32)

    deep_k = deep_y(k_fr, 5, sem_sk, sem_rk)

    k = iota((128, 1280), 0)
    c = iota((128, 1280), 1)
    y, z = c // 32, c % 32
    inner = c < 1024
    mask = inner & (y == 0) & (k == z // 2)
    mask = mask | (inner & (y == 31) & (k == 16 + z // 2))
    mask = mask | (inner & (z == 0) & (k == 32 + y // 2))
    mask = mask | (inner & (z == 31) & (k == 48 + y // 2))
    mask = mask | ((c >= 1024) & (k == 64 + (y - 32) // 2 * 16 + z // 2))
    put(m_ghost, mask)
    k, c = iota((512, 128), 0), iota((512, 128), 1)
    put(m_down, c == k // 64 * 16 + k % 32 // 2)

    for copy in ghosts:
        copy.wait_recv()
    high_x = (own_pos >> 2) & 1
    other_x = owner_x + 2 * high_x - 1
    beyond_x = ghost_in[jnp.clip(other_x, 0, N_X - 1)]
    inside = jnp.where((other_x >= 0) & (other_x < N_X), 1.0, 0.0)
    mine = ghost_in[owner_x] + inside * beyond_x
    dup[0, pl.ds(0, 16, stride=2)] = mine
    dup[0, pl.ds(1, 16, stride=2)] = mine
    widened = mapped(dup[0], m_ghost[...])
    for q in range(4):
        for t in range(2):
            piece = widened[:, 1024 + 128 * t : 1152 + 128 * t]
            f_gx[2 * q + t, 0:1] = piece[2 * q : 2 * q + 1]
            f_gx[2 * q + t, 31:32] = piece[8 + 2 * q : 9 + 2 * q]
    for i in range(8):
        j = i + 1
        ghost = f_k[j, own_f] * (widened[:, 128 * i : 128 * i + 128] + f_gx[i])
        f_gx[i] = ghost
        f_a[j, own_f] = jnp.where(first_f, (f_base[j, own_f] + ghost) * f_inv[j, own_f], 0.0)
    for i in range(8):
        j = i + 1
        around_a = coupled(f_a, w_f, j, 8, 32, lanes, 32)
        fresh = (0.25 * f_src[i] + f_gx[i] + around_a) * f_inv[j, own_f]
        f_sm[i] = jnp.where(first_f, f_a[j, own_f], fresh)
        f_d[j, own_f] = jnp.where(first_f, 0.0, fresh - f_v[j, own_f])
    for i in range(8):
        f_res[i] = jnp.where(first_f, coupled(f_d, w_f, i + 1, 8, 32, lanes, 32), 0.0)
    stacked = []
    for b in range(2):
        parts = [
            f_res[4 * b + q, pl.ds(0, 16, stride=2)] + f_res[4 * b + q, pl.ds(1, 16, stride=2)]
            for q in range(4)
        ]
        stacked.append(jnp.concatenate(parts, axis=1))
    packed = 0.5 * mapped(jnp.concatenate(stacked, axis=0), m_down[...])
    box_out[0] = packed[:16]
    box_out[1] = packed[16:]
    gathered = to_mates(lambda other: box_out, box_in, sem_s2, sem_r2)
    box_in[mx] = box_out[...]
    for copy in deep_r:
        copy.wait_recv()
    for copy in deep_r:
        copy.wait_send()
    deep_r = deep_y(r_fr, 4, sem_sr, sem_rr)

    zero_pads(wx, 8, 72)
    zero_pads(wy, 8, 72)
    zero_pads(e_a, 8, 72)
    zero_pads(e_b, 8, 72)
    for ref in (b_k, b_wx, b_wy, b_ua, b_ub):
        zero_pads(ref, 8, 40)
    for oz in range(2):
        k, c = iota((128, 256), 0), iota((128, 256), 1)
        m_exp[oz] = jnp.where((k // 16 == c // 32) & (c % 32 == 16 * oz + k % 16), 1.0, 0.0).astype(BF16)
        k, c = iota((256, 128), 1), iota((256, 128), 0)
        m_com[oz] = jnp.where((k // 16 == c // 32) & (c % 32 == 16 * oz + k % 16), 1.0, 0.0).astype(BF16)
    k, c = iota((128, 512), 0), iota((128, 512), 1)
    put(m_up, k == c // 64 * 16 + c % 32 // 2)
    k, c = iota((128, 1024), 0), iota((128, 1024), 1)
    put(m_four, k == c // 128 * 16 + c % 32 // 4)

    for copy in deep_k:
        copy.wait_recv()
    @pl.when(my == 0)
    def _():
        k_fr[0:5] = jnp.zeros((5, 80, 128), F32)

    @pl.when(my == N_Y - 1)
    def _():
        k_fr[13:18] = jnp.zeros((5, 80, 128), F32)

    window = pl.ds(8, 64)

    def coarse_weights(i, carry):
        j = i + 1
        k = k_fr[j, window]
        kxm = k_fr[j, pl.ds(7, 64)]
        kxp = k_fr[j, pl.ds(9, 64)]
        kym = y_before(k_fr, j, window, lanes, 32)
        kyp = y_beyond(k_fr, j, window, lanes, 32)
        kzm = jnp.where(z_first, 0.0, roll(k, 1))
        kzp = jnp.where(z_last, 0.0, roll(k, 127))
        wx[j, window] = 0.5 * (k + kxm)
        wy[j, window] = 0.5 * (k + kym)
        wz[j, window] = jnp.where(z_first, 0.0, 0.5 * (k + kzm))
        inverse = 1.0 / (3.0 * k + 0.5 * (kxm + kxp + kym + kyp + kzm + kzp))
        inverse = jnp.where(k > 0.0, inverse, 0.0)
        inv_a[j, window] = jnp.where(first_c, inverse, 0.0)
        inv_b[j, window] = jnp.where(first_c, 0.0, inverse)
        return carry

    lax.fori_loop(0, 16, coarse_weights, 0)
    w_c = (wx, wy, wz)

    def coarsened(ref):
        stacked = []
        for b in range(4):
            parts = [
                ref[1 + 4 * b + q, pl.ds(8, 32, stride=2)]
                + ref[1 + 4 * b + q, pl.ds(9, 32, stride=2)]
                for q in range(4)
            ]
            stacked.append(jnp.concatenate(parts, axis=1))
        return mapped(jnp.concatenate(stacked, axis=0), m_down[...])

    summed = coarsened(k_fr)
    own_b = pl.ds(8, 32)
    for b in range(4):
        b_k[1 + b, own_b] = 0.125 * summed[32 * b : 32 * b + 32]
    zb_first = lanes % 16 == 0
    zb_last = lanes % 16 == 15
    for b in range(4):
        j = b + 1
        k = b_k[j, own_b]
        kxm = b_k[j, pl.ds(7, 32)]
        kxp = b_k[j, pl.ds(9, 32)]
        kym = y_before(b_k, j, own_b, lanes, 16)
        kyp = y_beyond(b_k, j, own_b, lanes, 16)
        kzm = jnp.where(zb_first, 0.0, roll(k, 1))
        kzp = jnp.where(zb_last, 0.0, roll(k, 127))
        b_wx[j, own_b] = 0.5 * (k + kxm)
        b_wy[j, own_b] = 0.5 * (k + kym)
        b_wz[j, own_b] = jnp.where(zb_first, 0.0, 0.5 * (k + kzm))
        inverse = 1.0 / (3.0 * k + 0.5 * (kxm + kxp + kym + kyp + kzm + kzp))
        inverse = jnp.where(k > 0.0, inverse, 0.0)
        b_ia[b] = jnp.where(first_b, inverse, 0.0)
        b_ib[b] = jnp.where(first_b, 0.0, inverse)

    for copy in deep_r:
        copy.wait_recv()
    for copy in deep_r:
        copy.wait_send()

    for copy in gathered:
        copy.wait_recv()
    for ye in (1, 2):
        for sx in range(4):
            boxes[ye, sx] = box_in[jnp.maximum(found[4 * ye + sx], 0)]
    beside = [
        remote(boxes.at[1], boxes.at[3], sem_s3.at[0], sem_r3.at[0], around[2]),
        remote(boxes.at[2], boxes.at[0], sem_s3.at[1], sem_r3.at[1], around[3]),
    ]

    def compose(ye):
        for oz in range(2):
            pair = [sx for sx in range(4) if (sx + ye) % 2 == oz]
            stacked = [boxes[ye, sx, b] for sx in pair for b in range(2)]
            wide = mapped(jnp.concatenate(stacked, axis=0), m_exp[oz])
            for number, sx in enumerate(pair):
                here = jnp.where(found[4 * ye + sx] >= 0, 1.0, 0.0)
                covered = jnp.where(lanes % 32 // 16 == oz, here, 0.0) > 0.5
                rows = pl.ds(8 + 16 * sx, 16)
                for q in range(4):
                    b, t = q // 2, q % 2
                    j = 1 + 4 * ye + q
                    at = 32 * number + 16 * b
                    part = wide[at : at + 16, 128 * t : 128 * t + 128]
                    mixed = jnp.where(covered, part, r_fr[j, rows])
                    r_fr[j, rows] = mixed
                    e_a[j, rows] = mixed * inv_a[j, rows]

    compose(1)
    compose(2)
    for copy in beside:
        copy.wait_recv()
    compose(0)
    compose(3)

    def second(i, carry):
        j = i + 1
        fresh = r_fr[j, window] + coupled(e_a, w_c, j, 8, 64, lanes, 32)
        e_b[j, window] = fresh * inv_b[j, window]
        return carry

    lax.fori_loop(0, 16, second, 0, unroll=UNROLL)

    own_c = pl.ds(24, 32)
    for oz in range(2):
        pair = [(0, oz), (1, 1 - oz)]
        stacked = []
        for ox, oy in pair:
            rows = pl.ds(24 + 16 * ox, 16)
            for b in range(2):
                parts = [
                    e_a[5 + 4 * oy + 2 * b + t, rows] + e_b[5 + 4 * oy + 2 * b + t, rows]
                    for t in range(2)
                ]
                stacked.append(jnp.concatenate(parts, axis=1))
        packed = mapped(jnp.concatenate(stacked, axis=0), m_com[oz])
        for number, (ox, oy) in enumerate(pair):
            for b in range(2):
                at = 32 * number + 16 * b
                e_oct[2 * ox + oy, b] = packed[at : at + 16]
    for h in range(N_X):
        e_out[h] = e_oct[octs[h]]
    returned = to_mates(lambda other: e_out.at[other], e_in, sem_s4, sem_r4)
    e_in[mx] = e_out[mx]

    def remaining(i, carry):
        j = i + 1
        left[j, window] = jnp.where(first_c, coupled(e_b, w_c, j, 8, 64, lanes, 32), 0.0)
        return carry

    lax.fori_loop(0, 16, remaining, 0, unroll=UNROLL)
    summed = 0.5 * coarsened(left)
    for b in range(4):
        source = summed[32 * b : 32 * b + 32]
        b_fa[b] = source * b_ia[b]
        b_fb[b] = source * b_ib[b]
        b_ua[1 + b, own_b] = source * b_ia[b]
    w_b = (b_wx, b_wy, b_wz)
    for half in range(2 * SWEEPS - 1):
        into, out_of = ((b_ub, b_ua), (b_ua, b_ub))[half % 2]
        fixed, inverse = ((b_fb, b_ib), (b_fa, b_ia))[half % 2]
        for b in range(4):
            into[1 + b, own_b] = fixed[b] + inverse[b] * coupled(
                out_of, w_b, 1 + b, 8, 32, lanes, 16
            )

    for ox in range(2):
        for oy in range(2):
            rows = pl.ds(16 + 8 * ox, 8)
            u_oct[2 * ox + oy] = b_ua[2 + oy, rows] + b_ub[2 + oy, rows]
    for h in range(N_X):
        u_out[h] = u_oct[octs[h]]
    settled = to_mates(lambda other: u_out.at[other], u_in, sem_s5, sem_r5)
    u_in[mx] = u_out[mx]

    def doubled(ref, pieces):
        for b, piece in enumerate(pieces):
            ref[b, pl.ds(0, 16, stride=2)] = piece
            ref[b, pl.ds(1, 16, stride=2)] = piece
        return mapped(jnp.concatenate([ref[0], ref[1]], axis=0), m_up[...])

    wide = doubled(dup, [b_ua[2 + b, pl.ds(16, 16)] + b_ub[2 + b, pl.ds(16, 16)] for b in range(2)])
    for j in range(8):
        b, q = j // 4, j % 4
        part = wide[32 * b : 32 * b + 32, 128 * q : 128 * q + 128]
        total = e_a[5 + j, own_c] + e_b[5 + j, own_c] + part
        out[0, :, 128 * j : 128 * j + 128] = s_fr[1 + j, own_f] + total

    for copy in returned:
        copy.wait_recv()
    got = e_in.at[owner_x]
    wide = doubled(dup2, [got[0], got[1]])
    for j in range(8):
        b, q = j // 4, j % 4
        f_sm[j] = f_sm[j] + wide[32 * b : 32 * b + 32, 128 * q : 128 * q + 128]
    for copy in sends:
        copy.wait_send()
    for copy in settled:
        copy.wait_recv()
    tile = u_in[owner_x]
    side = jnp.where(own_oz == 1, 1.0, 0.0)
    tile = jnp.where(jnp.zeros((8, 128), F32) + side > 0.5, roll(tile, 120), tile)
    for t in range(4):
        dup[0, pl.ds(t, 8, stride=4)] = tile
    wide = mapped(dup[0], m_four[...])
    for j in range(8):
        out[1, :, 128 * j : 128 * j + 128] = f_sm[j] + wide[:, 128 * j : 128 * j + 128]


def scratch():
    v = pltpu.VMEM
    lists = [pltpu.SMEM((N_X * N_Y,), jnp.int32), pltpu.SMEM((3,), jnp.int32)]
    shapes = [(10, 48, 128)] * 2 + [(8, 32, 128)]
    shapes += [(8, 32, 128)] + [(10, 48, 128)] * 8 + [(8, 32, 128), (10, 48, 128)]
    shapes += [(8, 32, 128)] * 2
    shapes += [(18, 80, 128)] * 10
    shapes += [(6, 48, 128)] * 4 + [(4, 32, 128)] * 4 + [(6, 48, 128)] * 2
    shapes += [(8, 16, 128), (8, 16, 128), (N_X, 16, 128), (N_X, 16, 128)]
    shapes += [(2, 16, 128), (N_X, 2, 16, 128), (4, 4, 2, 16, 128)]
    shapes += [(4, 2, 16, 128), (N_X, 2, 16, 128), (N_X, 2, 16, 128)]
    shapes += [(4, 8, 128), (N_X, 8, 128), (N_X, 8, 128)]
    shapes += [(2, 32, 128)] * 2
    result = lists + [v(shape, F32) for shape in shapes]
    maps = [(2, 896, 128), (128, 1280), (512, 128), (128, 512), (2, 128, 256), (2, 256, 128)]
    result += [v(shape, BF16) for shape in maps + [(128, 1024)]]
    dma = pltpu.SemaphoreType.DMA
    result += [dma((9,))] + [dma((8,))] * 2 + [dma((3,))] * 4 + [dma((1,))] * 4 + [dma((2,))] * 2
    return result + [dma((1,))] * 4


def on_device(
    coarse_source,
    coarse_coefficient,
    coarse_start,
    fine_source,
    fine_coefficient,
    fine_start,
    fine_position,
    first_colour,
):
    vmem = pl.BlockSpec(memory_space=pltpu.VMEM)
    hbm = pl.BlockSpec(memory_space=pltpu.HBM)
    both = pl.pallas_call(
        kernel,
        out_shape=jax.ShapeDtypeStruct((2, 32, 1024), F32),
        in_specs=[hbm] * 8,
        out_specs=vmem,
        scratch_shapes=scratch(),
        compiler_params=pltpu.CompilerParams(
            collective_id=0, has_side_effects=True, vmem_limit_bytes=48 << 20
        ),
    )(
        *[
            pltpu.with_memory_space_constraint(array, pltpu.HBM)
            for array in (
                fine_position,
                first_colour,
                coarse_source,
                coarse_coefficient,
                coarse_start,
                fine_source,
                fine_coefficient,
                fine_start,
            )
        ],
    )
    return both[0], both[1:]


def solution(mesh):
    placed = (
        P("gx", "gy"),
        P("gx", "gy"),
        P("gx", "gy"),
        P(("gx", "gy"), None, None),
        P(("gx", "gy"), None, None),
        P(("gx", "gy"), None, None),
        P(),
        P(),
    )
    return jax.shard_map(
        on_device,
        mesh=mesh,
        in_specs=placed,
        out_specs=(P("gx", "gy"), P(("gx", "gy"), None, None)),
        check_vma=False,
    )
```

```python
import functools

import jax
import jax.numpy as jnp
from jax import lax
from jax.experimental import pallas as pl
from jax.experimental.pallas import tpu as pltpu
from jax.sharding import PartitionSpec as P


MESH = pl.DeviceIdType.MESH
F32 = jnp.float32
BF16 = jnp.bfloat16
SWEEPS = 4
N_X = 16
N_Y = 8
FAR_FIRST = (10, 6, 9, 11, 7, 5, 14, 2, 8, 13, 15, 3, 1, 12, 4)
UNROLL = 16


def iota(shape, dim):
    return lax.broadcasted_iota(jnp.int32, shape, dim)


def halves(values):
    high = values.astype(BF16)
    low = (values - high.astype(F32)).astype(BF16)
    return jnp.concatenate([high, low], axis=0)


def mapped(values, matrix):
    rows = values.shape[0]
    both = jnp.dot(halves(values), matrix, preferred_element_type=F32)
    return both[:rows] + both[rows:]


def roll(values, amount):
    return pltpu.roll(values, amount, axis=1)


def y_before(ref, j, rows, lanes, step):
    return roll(jnp.where(lanes >= 128 - step, ref[j - 1, rows], ref[j, rows]), step)


def y_beyond(ref, j, rows, lanes, step):
    return roll(jnp.where(lanes < step, ref[j + 1, rows], ref[j, rows]), 128 - step)


def coupled(value, weights, j, low, count, lanes, step):
    wx, wy, wz = weights
    here = pl.ds(low, count)
    before = pl.ds(low - 1, count)
    beyond = pl.ds(low + 1, count)
    mid = value[j, here]
    w_y = wy[j, here]
    w_z = wz[j, here]
    total = wx[j, here] * value[j, before] + wx[j, beyond] * value[j, beyond]
    total = total + w_y * y_before(value, j, here, lanes, step)
    ahead = jnp.where(lanes < step, wy[j + 1, here] * value[j + 1, here], w_y * mid)
    total = total + roll(ahead, 128 - step)
    return total + w_z * roll(mid, 1) + roll(w_z * mid, 127)


def zero_pads(ref, low, high):
    blocks, rows, _ = ref.shape
    ref[0] = jnp.zeros((rows, 128), F32)
    ref[blocks - 1] = jnp.zeros((rows, 128), F32)
    ref[1 : blocks - 1, :low] = jnp.zeros((blocks - 2, low, 128), F32)
    ref[1 : blocks - 1, high:] = jnp.zeros((blocks - 2, rows - high, 128), F32)


class Remote:
    def __init__(self, copy):
        self.copy = copy
        self.landed = False
        self.left = False
        copy.start()

    def wait_recv(self):
        if not self.landed:
            self.copy.wait_recv()
        self.landed = True

    def wait_send(self):
        if not self.left:
            self.copy.wait_send()
        self.left = True


class Group:
    def __init__(self, span, send_sem, recv_sem):
        self.sent = pltpu.make_async_copy(span, span, send_sem)
        self.landed = pltpu.make_async_copy(span, span, recv_sem)
        self.left = False

    def wait_recv(self):
        self.landed.wait()

    def wait_send(self):
        if not self.left:
            self.sent.wait()
        self.left = True


def put(ref, mask):
    ref[...] = jnp.where(mask, 1.0, 0.0).astype(BF16)


def kernel(
    pos_hbm,
    colours_hbm,
    c_source,
    c_coeff,
    c_start,
    f_source,
    f_coeff,
    f_start,
    out,
    pos,
    colours,
    s_fr,
    kq_fr,
    src_c,
    f_src,
    f_k,
    f_v,
    f_wx,
    f_wy,
    f_wz,
    f_inv,
    f_base,
    f_a,
    f_sm,
    f_d,
    f_res,
    f_gx,
    k_fr,
    r_fr,
    wx,
    wy,
    wz,
    inv_a,
    inv_b,
    e_a,
    e_b,
    left,
    b_k,
    b_wx,
    b_wy,
    b_wz,
    b_ia,
    b_ib,
    b_fa,
    b_fb,
    b_ua,
    b_ub,
    x_rows,
    faces,
    ghost_out,
    ghost_in,
    box_out,
    box_in,
    boxes,
    e_oct,
    e_out,
    e_in,
    u_oct,
    u_out,
    u_in,
    dup,
    dup2,
    m_face,
    m_ghost,
    m_down,
    m_up,
    m_exp,
    m_com,
    m_four,
    sem_l,
    sem_s0,
    sem_r0,
    sem_sk,
    sem_rk,
    sem_sr,
    sem_rr,
    sem_s1,
    sem_r1,
    sem_s2,
    sem_r2,
    sem_s3,
    sem_r3,
    sem_s4,
    sem_r4,
    sem_s5,
    sem_r5,
):
    mx = lax.axis_index("gx")
    my = lax.axis_index("gy")
    x_up, x_dn = lax.rem(mx + 1, N_X), lax.rem(mx + N_X - 1, N_X)
    y_up, y_dn = lax.rem(my + 1, N_Y), lax.rem(my + N_Y - 1, N_Y)
    around = [
        (x_dn, my),
        (x_up, my),
        (mx, y_dn),
        (mx, y_up),
    ]
    mates = [(lax.rem(mx + d, N_X), my) for d in FAR_FIRST]

    barrier = pltpu.get_barrier_semaphore()
    greeted = mates + around[2:]
    for device in greeted:
        pl.semaphore_signal(barrier, inc=1, device_id=device, device_id_type=MESH)

    loads = [
        [
            pltpu.make_async_copy(pos_hbm, pos, sem_l.at[7]),
            pltpu.make_async_copy(colours_hbm, colours, sem_l.at[8]),
        ]
    ]
    for copy in loads[0]:
        copy.start()

    def load(number, source, target, span):
        for j in range(8):
            pltpu.make_async_copy(source(j), target(j), sem_l.at[number]).start()
        loads.append([pltpu.make_async_copy(span, span, sem_l.at[number])])

    def chunk(j):
        return pl.ds(128 * j, 128)

    load(0, lambda j: c_start.at[:, chunk(j)], lambda j: s_fr.at[1 + j, pl.ds(8, 32)], s_fr.at[pl.ds(1, 8), pl.ds(8, 32)])
    load(1, lambda j: c_coeff.at[:, chunk(j)], lambda j: kq_fr.at[1 + j, pl.ds(8, 32)], kq_fr.at[pl.ds(1, 8), pl.ds(8, 32)])
    load(2, lambda j: f_coeff.at[0, :, chunk(j)], lambda j: f_k.at[1 + j, pl.ds(8, 32)], f_k.at[pl.ds(1, 8), pl.ds(8, 32)])
    load(3, lambda j: f_start.at[0, :, chunk(j)], lambda j: f_v.at[1 + j, pl.ds(8, 32)], f_v.at[pl.ds(1, 8), pl.ds(8, 32)])
    load(4, lambda j: f_source.at[0, :, chunk(j)], lambda j: f_src.at[j], f_src)
    load(5, lambda j: c_source.at[:, chunk(j)], lambda j: src_c.at[j], src_c)
    load(6, lambda j: c_coeff.at[:, chunk(j)], lambda j: k_fr.at[5 + j, pl.ds(24, 32)], k_fr.at[pl.ds(5, 8), pl.ds(24, 32)])

    for q in range(5):
        for j in (4 - q, 13 + q):
            for low, high in ((0, 8 + 4 * q), (72 - 4 * q, 80)):
                k_fr[j, low:high] = jnp.zeros((high - low, 128), F32)
                r_fr[j, low:high] = jnp.zeros((high - low, 128), F32)
    for copy in loads[0]:
        copy.wait()
    own_pos = pos[mx * N_Y + my]
    owner_x = own_pos >> 6
    own_oz = own_pos & 1

    slots = []
    for ye in range(4):
        row = (my, y_dn, y_up)[1 if ye == 0 else (2 if ye == 3 else 0)]
        for sx in range(4):
            ox, oy = (sx + 1) % 2, (ye + 1) % 2
            octant = 4 * ox + 2 * oy + (ox + oy) % 2
            column = mx + (-1, 0, 0, 1)[sx]
            slots.append((row, (column * N_Y + row) * 8 + octant))

    def look(h, found):
        held = [pos[h * N_Y + row] for row in (my, y_dn, y_up)]
        result = []
        for number, (row, wanted) in enumerate(slots):
            ye = number // 4
            at = held[1 if ye == 0 else (2 if ye == 3 else 0)]
            result.append(jnp.where(at == wanted, h, found[number]))
        return tuple(result)

    found = lax.fori_loop(0, N_X, look, tuple(jnp.int32(-1) for _ in slots))
    octs, picks = [], []
    for h in range(N_X):
        at = pos[h * N_Y + my]
        octant, away = (at >> 1) & 3, (at >> 6) - mx
        pick = jnp.where((away == 1) & (octant < 2), 4 + octant, 0)
        pick = jnp.where((away == -1) & (octant >= 2), 4 + octant, pick)
        octs.append(octant)
        picks.append(jnp.where(away == 0, octant, pick))

    lanes = iota((1, 128), 1)
    z_first = lanes % 32 == 0
    z_last = lanes % 32 == 31
    parity = (iota((8, 128), 0) + iota((8, 128), 1) // 32 + iota((8, 128), 1)) % 2
    parity_b = (iota((8, 128), 0) + iota((8, 128), 1) // 16 + iota((8, 128), 1)) % 2

    def painted(base, colour, rows):
        flags = jnp.where(base == colour, 1.0, 0.0)
        return jnp.concatenate([flags] * (rows // 8), axis=0) > 0.5

    first_f = painted(parity, colours[0], 32)
    first_c = painted(parity, colours[1], 64)
    first_b = painted(parity_b, colours[2], 32)

    zero_pads(f_v, 8, 40)
    zero_pads(f_wx, 8, 40)
    zero_pads(f_wy, 8, 40)
    zero_pads(f_a, 8, 40)
    zero_pads(f_d, 8, 40)
    x_rows[...] = jnp.zeros(x_rows.shape, F32)
    f_gx[...] = jnp.zeros(f_gx.shape, F32)

    for oz in range(2):
        k = iota((896, 128), 0)
        c = iota((896, 128), 1)
        block, lane = k // 128, k % 128
        z, yy = lane % 32, lane // 32
        mask = (block == 0) & (c < 16) & (lane == 96 + 16 * oz + c)
        mask = mask | ((block == 1) & (c >= 16) & (c < 32) & (lane == 16 * oz + c - 16))
        own = (block >= 2) & (block < 6) & (z == (16, 15)[oz])
        mask = mask | (own & (c == (48, 32)[oz] + 4 * (block - 2) + yy))
        mask = mask | (
            (block == 6) & (z >= 16 * oz) & (z < 16 * oz + 16) & (c == 64 + yy * 16 + z - 16 * oz)
        )
        m_face[oz] = jnp.where(mask, 1.0, 0.0).astype(BF16)

    for group in loads[1:3]:
        for copy in group:
            copy.wait()

    for ox in range(2):
        for oy in range(2):
            own, at = (24, 4) if ox == 0 else (23, 0)
            far, at_far = (39, 0) if ox == 0 else (8, 4)
            for q in range(4):
                j = 1 + 4 * oy + q
                x_rows[2 * ox + oy, at + q : at + q + 1] = s_fr[j, own : own + 1]
                x_rows[4 + 2 * ox + oy, at_far + q : at_far + q + 1] = s_fr[j, far : far + 1]
    blank = jnp.zeros((16, 128), F32)
    for oz in range(2):
        pair = [(0, oz), (1, 1 - oz)]
        stacked = []
        for ox, oy in pair:
            rows = pl.ds(8 + 16 * ox, 16)
            parts = [s_fr[4, rows], blank] if oy else [blank, s_fr[5, rows]]
            parts += [s_fr[1 + 4 * oy + q, rows] for q in range(4)]
            parts.append(x_rows[2 * ox + oy])
            stacked.append(jnp.concatenate(parts, axis=1))
        for ox, oy in pair:
            stacked.append(jnp.concatenate([blank] * 6 + [x_rows[4 + 2 * ox + oy]], axis=1))
        packed = mapped(jnp.concatenate(stacked, axis=0), m_face[oz])
        for number, (ox, oy) in enumerate(pair):
            faces[2 * ox + oy] = packed[16 * number : 16 * number + 16]
            faces[4 + 2 * ox + oy] = packed[32 + 16 * number : 48 + 16 * number]
    pl.semaphore_wait(barrier, len(greeted))

    sends = []

    def remote(source, target, send_sem, recv_sem, device):
        copy = Remote(
            pltpu.make_async_remote_copy(
                src_ref=source,
                dst_ref=target,
                send_sem=send_sem,
                recv_sem=recv_sem,
                device_id=device,
                device_id_type=MESH,
            )
        )
        sends.append(copy)
        return copy

    layer = []
    for number, ref in enumerate((s_fr, kq_fr)):
        rows, blocks = pl.ds(8, 32), pl.ds(1, 8)
        for side, (source, target, device) in enumerate(
            (
                (ref.at[8, rows], ref.at[0, rows], around[3]),
                (ref.at[1, rows], ref.at[9, rows], around[2]),
                (ref.at[blocks, pl.ds(39, 1)], ref.at[blocks, pl.ds(7, 1)], around[1]),
                (ref.at[blocks, pl.ds(8, 1)], ref.at[blocks, pl.ds(40, 1)], around[0]),
            )
        ):
            at = 4 * number + side
            layer.append(remote(source, target, sem_s0.at[at], sem_r0.at[at], device))

    for copy in loads[7]:
        copy.wait()

    def deep_x(ref, width, send_sem, recv_sem):
        blocks = pl.ds(5, 8)
        for side, (source, target) in enumerate(((24, 56), (56 - width, 24 - width))):
            pltpu.make_async_remote_copy(
                src_ref=ref.at[blocks, pl.ds(source, width)],
                dst_ref=ref.at[blocks, pl.ds(target, width)],
                send_sem=send_sem.at[0],
                recv_sem=recv_sem.at[0],
                device_id=around[side],
                device_id_type=MESH,
            ).start()
        span = ref.at[blocks, pl.ds(8, 2 * width)]
        group = Group(span, send_sem.at[0], recv_sem.at[0])
        sends.append(group)
        return [group]

    def deep_y(ref, depth, send_sem, recv_sem):
        for q in range(depth):
            rows = pl.ds(8 + 4 * q, 64 - 8 * q)
            for side, (source, target) in enumerate(((5 + q, 13 + q), (12 - q, 4 - q))):
                pltpu.make_async_remote_copy(
                    src_ref=ref.at[source, rows],
                    dst_ref=ref.at[target, rows],
                    send_sem=send_sem.at[2],
                    recv_sem=recv_sem.at[2],
                    device_id=around[2 + side],
                    device_id_type=MESH,
                ).start()
        total = 2 * sum(64 - 8 * q for q in range(depth))
        span = ref.at[pl.ds(1, 8), pl.ds(8, total // 8)]
        group = Group(span, send_sem.at[2], recv_sem.at[2])
        sends.append(group)
        return [group]

    deep_k = deep_x(k_fr, 17, sem_sk, sem_rk)

    for group in loads[3:6]:
        for copy in group:
            copy.wait()
    rows_f = iota((32, 128), 0)
    own_f = pl.ds(8, 32)

    def fine_weights(i, carry):
        j = i + 1
        k = f_k[j, own_f]
        y_first = (lanes < 32) & (j == 1)
        y_last = (lanes >= 96) & (j == 8)
        kxm = jnp.where(rows_f == 0, k, f_k[j, pl.ds(7, 32)])
        kxp = jnp.where(rows_f == 31, k, f_k[j, pl.ds(9, 32)])
        kym = jnp.where(y_first, k, y_before(f_k, j, own_f, lanes, 32))
        kyp = jnp.where(y_last, k, y_beyond(f_k, j, own_f, lanes, 32))
        kzm = jnp.where(z_first, k, roll(k, 1))
        kzp = jnp.where(z_last, k, roll(k, 127))
        f_wx[j, own_f] = jnp.where(rows_f == 0, 0.0, 0.5 * (k + kxm))
        f_wy[j, own_f] = jnp.where(y_first, 0.0, 0.5 * (k + kym))
        f_wz[j, own_f] = jnp.where(z_first, 0.0, 0.5 * (k + kzm))
        f_inv[j, own_f] = 1.0 / (3.0 * k + 0.5 * (kxm + kxp + kym + kyp + kzm + kzp))
        return carry

    lax.fori_loop(0, 8, fine_weights, 0)
    w_f = (f_wx, f_wy, f_wz)

    def fine_base(i, carry):
        f_base[i + 1, own_f] = 0.25 * f_src[i] + coupled(f_v, w_f, i + 1, 8, 32, lanes, 32)
        return carry

    lax.fori_loop(0, 8, fine_base, 0)

    for copy in layer[:2]:
        copy.wait_recv()

    def blank_sides(ref):
        @pl.when(my == 0)
        def _():
            ref[0, 8:40] = jnp.zeros((32, 128), F32)

        @pl.when(my == N_Y - 1)
        def _():
            ref[9, 8:40] = jnp.zeros((32, 128), F32)

    blank_sides(s_fr)

    for ox in range(2):
        for oy in range(2):
            rows = pl.ds(8 + 16 * ox, 16)
            oz = (ox + oy) % 2
            shift = (128 - 96 - 16 * oz, 16 - 16 * oz)[oy] % 128
            beside = s_fr[9 * oy, rows]
            if shift:
                beside = roll(beside, shift)
            wanted = (lanes >= 16 * oy) & (lanes < 16 * oy + 16)
            faces[2 * ox + oy] = faces[2 * ox + oy] + jnp.where(wanted, beside, 0.0)

    def to_mates(source, target, send_sem, recv_sem):
        for d in FAR_FIRST:
            other = lax.rem(mx + d, N_X)
            pltpu.make_async_remote_copy(
                src_ref=source(other),
                dst_ref=target.at[mx],
                send_sem=send_sem.at[0],
                recv_sem=recv_sem.at[0],
                device_id=(other, my),
                device_id_type=MESH,
            ).start()
        group = Group(target.at[pl.ds(0, N_X - 1)], send_sem.at[0], recv_sem.at[0])
        sends.append(group)
        return [group]

    for h in range(N_X):
        ghost_out[h] = faces[picks[h]]
    ghosts = to_mates(lambda other: ghost_out.at[other], ghost_in, sem_s1, sem_r1)
    ghost_in[mx] = ghost_out[mx]

    for copy in layer:
        copy.wait_recv()
    blank_sides(kq_fr)
    for ref in (s_fr, kq_fr):

        @pl.when(mx == 0)
        def _():
            ref[1:9, 7:8] = jnp.zeros((8, 1, 128), F32)

        @pl.when(mx == N_X - 1)
        def _():
            ref[1:9, 40:41] = jnp.zeros((8, 1, 128), F32)

    for copy in loads[6]:
        copy.wait()

    def coarse_residual(i, carry):
        j = i + 1
        s = s_fr[j, own_f]
        k = kq_fr[j, own_f]

        def flux(k_there, s_there):
            return (k + k_there) * (s - s_there)

        before, beyond = pl.ds(7, 32), pl.ds(9, 32)
        total = flux(kq_fr[j, before], s_fr[j, before]) + flux(kq_fr[j, beyond], s_fr[j, beyond])
        total = total + flux(
            y_before(kq_fr, j, own_f, lanes, 32), y_before(s_fr, j, own_f, lanes, 32)
        )
        total = total + flux(
            y_beyond(kq_fr, j, own_f, lanes, 32), y_beyond(s_fr, j, own_f, lanes, 32)
        )
        total = total + flux(
            jnp.where(z_first, 0.0, roll(k, 1)), jnp.where(z_first, 0.0, roll(s, 1))
        )
        total = total + flux(
            jnp.where(z_last, 0.0, roll(k, 127)), jnp.where(z_last, 0.0, roll(s, 127))
        )
        r_fr[i + 5, pl.ds(24, 32)] = src_c[i] - 0.5 * total
        return carry

    lax.fori_loop(0, 8, coarse_residual, 0)
    deep_r = deep_x(r_fr, 16, sem_sr, sem_rr)

    for copy in deep_k:
        copy.wait_recv()

    @pl.when(mx == 0)
    def _():
        k_fr[5:13, 7:24] = jnp.zeros((8, 17, 128), F32)

    @pl.when(mx == N_X - 1)
    def _():
        k_fr[5:13, 56:73] = jnp.zeros((8, 17, 128), F32)

    deep_k = deep_y(k_fr, 5, sem_sk, sem_rk)

    k = iota((128, 1280), 0)
    c = iota((128, 1280), 1)
    y, z = c // 32, c % 32
    inner = c < 1024
    mask = inner & (y == 0) & (k == z // 2)
    mask = mask | (inner & (y == 31) & (k == 16 + z // 2))
    mask = mask | (inner & (z == 0) & (k == 32 + y // 2))
    mask = mask | (inner & (z == 31) & (k == 48 + y // 2))
    mask = mask | ((c >= 1024) & (k == 64 + (y - 32) // 2 * 16 + z // 2))
    put(m_ghost, mask)
    k, c = iota((512, 128), 0), iota((512, 128), 1)
    put(m_down, c == k // 64 * 16 + k % 32 // 2)

    for copy in ghosts:
        copy.wait_recv()
    high_x = (own_pos >> 2) & 1
    other_x = owner_x + 2 * high_x - 1
    beyond_x = ghost_in[jnp.clip(other_x, 0, N_X - 1)]
    inside = jnp.where((other_x >= 0) & (other_x < N_X), 1.0, 0.0)
    mine = ghost_in[owner_x] + inside * beyond_x
    dup[0, pl.ds(0, 16, stride=2)] = mine
    dup[0, pl.ds(1, 16, stride=2)] = mine
    widened = mapped(dup[0], m_ghost[...])
    for q in range(4):
        for t in range(2):
            piece = widened[:, 1024 + 128 * t : 1152 + 128 * t]
            f_gx[2 * q + t, 0:1] = piece[2 * q : 2 * q + 1]
            f_gx[2 * q + t, 31:32] = piece[8 + 2 * q : 9 + 2 * q]
    for i in range(8):
        j = i + 1
        ghost = f_k[j, own_f] * (widened[:, 128 * i : 128 * i + 128] + f_gx[i])
        f_gx[i] = ghost
        f_a[j, own_f] = jnp.where(first_f, (f_base[j, own_f] + ghost) * f_inv[j, own_f], 0.0)
    for i in range(8):
        j = i + 1
        around_a = coupled(f_a, w_f, j, 8, 32, lanes, 32)
        fresh = (0.25 * f_src[i] + f_gx[i] + around_a) * f_inv[j, own_f]
        f_sm[i] = jnp.where(first_f, f_a[j, own_f], fresh)
        f_d[j, own_f] = jnp.where(first_f, 0.0, fresh - f_v[j, own_f])
    for i in range(8):
        f_res[i] = jnp.where(first_f, coupled(f_d, w_f, i + 1, 8, 32, lanes, 32), 0.0)
    stacked = []
    for b in range(2):
        parts = [
            f_res[4 * b + q, pl.ds(0, 16, stride=2)] + f_res[4 * b + q, pl.ds(1, 16, stride=2)]
            for q in range(4)
        ]
        stacked.append(jnp.concatenate(parts, axis=1))
    packed = 0.5 * mapped(jnp.concatenate(stacked, axis=0), m_down[...])
    box_out[0] = packed[:16]
    box_out[1] = packed[16:]
    gathered = to_mates(lambda other: box_out, box_in, sem_s2, sem_r2)
    box_in[mx] = box_out[...]
    for copy in deep_r:
        copy.wait_recv()
    for copy in deep_r:
        copy.wait_send()
    deep_r = deep_y(r_fr, 4, sem_sr, sem_rr)

    zero_pads(wx, 8, 72)
    zero_pads(wy, 8, 72)
    zero_pads(e_a, 8, 72)
    zero_pads(e_b, 8, 72)
    for ref in (b_k, b_wx, b_wy, b_ua, b_ub):
        zero_pads(ref, 8, 40)
    for oz in range(2):
        k, c = iota((128, 256), 0), iota((128, 256), 1)
        m_exp[oz] = jnp.where((k // 16 == c // 32) & (c % 32 == 16 * oz + k % 16), 1.0, 0.0).astype(BF16)
        k, c = iota((256, 128), 1), iota((256, 128), 0)
        m_com[oz] = jnp.where((k // 16 == c // 32) & (c % 32 == 16 * oz + k % 16), 1.0, 0.0).astype(BF16)
    k, c = iota((128, 512), 0), iota((128, 512), 1)
    put(m_up, k == c // 64 * 16 + c % 32 // 2)
    k, c = iota((128, 1024), 0), iota((128, 1024), 1)
    put(m_four, k == c // 128 * 16 + c % 32 // 4)

    for copy in deep_k:
        copy.wait_recv()
    @pl.when(my == 0)
    def _():
        k_fr[0:5] = jnp.zeros((5, 80, 128), F32)

    @pl.when(my == N_Y - 1)
    def _():
        k_fr[13:18] = jnp.zeros((5, 80, 128), F32)

    window = pl.ds(8, 64)

    def coarse_weights(i, carry):
        j = i + 1
        k = k_fr[j, window]
        kxm = k_fr[j, pl.ds(7, 64)]
        kxp = k_fr[j, pl.ds(9, 64)]
        kym = y_before(k_fr, j, window, lanes, 32)
        kyp = y_beyond(k_fr, j, window, lanes, 32)
        kzm = jnp.where(z_first, 0.0, roll(k, 1))
        kzp = jnp.where(z_last, 0.0, roll(k, 127))
        wx[j, window] = 0.5 * (k + kxm)
        wy[j, window] = 0.5 * (k + kym)
        wz[j, window] = jnp.where(z_first, 0.0, 0.5 * (k + kzm))
        inverse = 1.0 / (3.0 * k + 0.5 * (kxm + kxp + kym + kyp + kzm + kzp))
        inverse = jnp.where(k > 0.0, inverse, 0.0)
        inv_a[j, window] = jnp.where(first_c, inverse, 0.0)
        inv_b[j, window] = jnp.where(first_c, 0.0, inverse)
        return carry

    lax.fori_loop(0, 16, coarse_weights, 0)
    w_c = (wx, wy, wz)

    def coarsened(ref):
        stacked = []
        for b in range(4):
            parts = [
                ref[1 + 4 * b + q, pl.ds(8, 32, stride=2)]
                + ref[1 + 4 * b + q, pl.ds(9, 32, stride=2)]
                for q in range(4)
            ]
            stacked.append(jnp.concatenate(parts, axis=1))
        return mapped(jnp.concatenate(stacked, axis=0), m_down[...])

    summed = coarsened(k_fr)
    own_b = pl.ds(8, 32)
    for b in range(4):
        b_k[1 + b, own_b] = 0.125 * summed[32 * b : 32 * b + 32]
    zb_first = lanes % 16 == 0
    zb_last = lanes % 16 == 15
    for b in range(4):
        j = b + 1
        k = b_k[j, own_b]
        kxm = b_k[j, pl.ds(7, 32)]
        kxp = b_k[j, pl.ds(9, 32)]
        kym = y_before(b_k, j, own_b, lanes, 16)
        kyp = y_beyond(b_k, j, own_b, lanes, 16)
        kzm = jnp.where(zb_first, 0.0, roll(k, 1))
        kzp = jnp.where(zb_last, 0.0, roll(k, 127))
        b_wx[j, own_b] = 0.5 * (k + kxm)
        b_wy[j, own_b] = 0.5 * (k + kym)
        b_wz[j, own_b] = jnp.where(zb_first, 0.0, 0.5 * (k + kzm))
        inverse = 1.0 / (3.0 * k + 0.5 * (kxm + kxp + kym + kyp + kzm + kzp))
        inverse = jnp.where(k > 0.0, inverse, 0.0)
        b_ia[b] = jnp.where(first_b, inverse, 0.0)
        b_ib[b] = jnp.where(first_b, 0.0, inverse)

    for copy in deep_r:
        copy.wait_recv()
    for copy in deep_r:
        copy.wait_send()

    for copy in gathered:
        copy.wait_recv()
    for ye in (1, 2):
        for sx in range(4):
            boxes[ye, sx] = box_in[jnp.maximum(found[4 * ye + sx], 0)]
    for source, target, device in ((1, 3, around[2]), (2, 0, around[3])):
        pltpu.make_async_remote_copy(
            src_ref=boxes.at[source],
            dst_ref=boxes.at[target],
            send_sem=sem_s3.at[0],
            recv_sem=sem_r3.at[0],
            device_id=device,
            device_id_type=MESH,
        ).start()
    beside = [Group(boxes.at[pl.ds(0, 2)], sem_s3.at[0], sem_r3.at[0])]
    sends += beside

    def compose(ye):
        for oz in range(2):
            pair = [sx for sx in range(4) if (sx + ye) % 2 == oz]
            stacked = [boxes[ye, sx, b] for sx in pair for b in range(2)]
            wide = mapped(jnp.concatenate(stacked, axis=0), m_exp[oz])
            for number, sx in enumerate(pair):
                here = jnp.where(found[4 * ye + sx] >= 0, 1.0, 0.0)
                covered = jnp.where(lanes % 32 // 16 == oz, here, 0.0) > 0.5
                rows = pl.ds(8 + 16 * sx, 16)
                for q in range(4):
                    b, t = q // 2, q % 2
                    j = 1 + 4 * ye + q
                    at = 32 * number + 16 * b
                    part = wide[at : at + 16, 128 * t : 128 * t + 128]
                    mixed = jnp.where(covered, part, r_fr[j, rows])
                    r_fr[j, rows] = mixed
                    e_a[j, rows] = mixed * inv_a[j, rows]

    compose(1)
    compose(2)
    for copy in beside:
        copy.wait_recv()
    compose(0)
    compose(3)

    def second(i, carry):
        j = i + 1
        fresh = r_fr[j, window] + coupled(e_a, w_c, j, 8, 64, lanes, 32)
        e_b[j, window] = fresh * inv_b[j, window]
        return carry

    lax.fori_loop(0, 16, second, 0, unroll=UNROLL)

    own_c = pl.ds(24, 32)
    for oz in range(2):
        pair = [(0, oz), (1, 1 - oz)]
        stacked = []
        for ox, oy in pair:
            rows = pl.ds(24 + 16 * ox, 16)
            for b in range(2):
                parts = [
                    e_a[5 + 4 * oy + 2 * b + t, rows] + e_b[5 + 4 * oy + 2 * b + t, rows]
                    for t in range(2)
                ]
                stacked.append(jnp.concatenate(parts, axis=1))
        packed = mapped(jnp.concatenate(stacked, axis=0), m_com[oz])
        for number, (ox, oy) in enumerate(pair):
            for b in range(2):
                at = 32 * number + 16 * b
                e_oct[2 * ox + oy, b] = packed[at : at + 16]
    for h in range(N_X):
        e_out[h] = e_oct[octs[h]]
    returned = to_mates(lambda other: e_out.at[other], e_in, sem_s4, sem_r4)
    e_in[mx] = e_out[mx]

    def remaining(i, carry):
        j = i + 1
        left[j, window] = jnp.where(first_c, coupled(e_b, w_c, j, 8, 64, lanes, 32), 0.0)
        return carry

    lax.fori_loop(0, 16, remaining, 0, unroll=UNROLL)
    summed = 0.5 * coarsened(left)
    for b in range(4):
        source = summed[32 * b : 32 * b + 32]
        b_fa[b] = source * b_ia[b]
        b_fb[b] = source * b_ib[b]
        b_ua[1 + b, own_b] = source * b_ia[b]
    w_b = (b_wx, b_wy, b_wz)
    for half in range(2 * SWEEPS - 1):
        into, out_of = ((b_ub, b_ua), (b_ua, b_ub))[half % 2]
        fixed, inverse = ((b_fb, b_ib), (b_fa, b_ia))[half % 2]
        for b in range(4):
            into[1 + b, own_b] = fixed[b] + inverse[b] * coupled(
                out_of, w_b, 1 + b, 8, 32, lanes, 16
            )

    for ox in range(2):
        for oy in range(2):
            rows = pl.ds(16 + 8 * ox, 8)
            u_oct[2 * ox + oy] = b_ua[2 + oy, rows] + b_ub[2 + oy, rows]
    for h in range(N_X):
        u_out[h] = u_oct[octs[h]]
    settled = to_mates(lambda other: u_out.at[other], u_in, sem_s5, sem_r5)
    u_in[mx] = u_out[mx]

    def doubled(ref, pieces):
        for b, piece in enumerate(pieces):
            ref[b, pl.ds(0, 16, stride=2)] = piece
            ref[b, pl.ds(1, 16, stride=2)] = piece
        return mapped(jnp.concatenate([ref[0], ref[1]], axis=0), m_up[...])

    wide = doubled(dup, [b_ua[2 + b, pl.ds(16, 16)] + b_ub[2 + b, pl.ds(16, 16)] for b in range(2)])
    for j in range(8):
        b, q = j // 4, j % 4
        part = wide[32 * b : 32 * b + 32, 128 * q : 128 * q + 128]
        total = e_a[5 + j, own_c] + e_b[5 + j, own_c] + part
        out[0, :, 128 * j : 128 * j + 128] = s_fr[1 + j, own_f] + total

    for copy in returned:
        copy.wait_recv()
    got = e_in.at[owner_x]
    wide = doubled(dup2, [got[0], got[1]])
    for j in range(8):
        b, q = j // 4, j % 4
        f_sm[j] = f_sm[j] + wide[32 * b : 32 * b + 32, 128 * q : 128 * q + 128]
    for copy in sends:
        copy.wait_send()
    for copy in settled:
        copy.wait_recv()
    tile = u_in[owner_x]
    side = jnp.where(own_oz == 1, 1.0, 0.0)
    tile = jnp.where(jnp.zeros((8, 128), F32) + side > 0.5, roll(tile, 120), tile)
    for t in range(4):
        dup[0, pl.ds(t, 8, stride=4)] = tile
    wide = mapped(dup[0], m_four[...])
    for j in range(8):
        out[1, :, 128 * j : 128 * j + 128] = f_sm[j] + wide[:, 128 * j : 128 * j + 128]


def scratch():
    v = pltpu.VMEM
    lists = [pltpu.SMEM((N_X * N_Y,), jnp.int32), pltpu.SMEM((3,), jnp.int32)]
    shapes = [(10, 48, 128)] * 2 + [(8, 32, 128)]
    shapes += [(8, 32, 128)] + [(10, 48, 128)] * 8 + [(8, 32, 128), (10, 48, 128)]
    shapes += [(8, 32, 128)] * 2
    shapes += [(18, 80, 128)] * 10
    shapes += [(6, 48, 128)] * 4 + [(4, 32, 128)] * 4 + [(6, 48, 128)] * 2
    shapes += [(8, 16, 128), (8, 16, 128), (N_X, 16, 128), (N_X, 16, 128)]
    shapes += [(2, 16, 128), (N_X, 2, 16, 128), (4, 4, 2, 16, 128)]
    shapes += [(4, 2, 16, 128), (N_X, 2, 16, 128), (N_X, 2, 16, 128)]
    shapes += [(4, 8, 128), (N_X, 8, 128), (N_X, 8, 128)]
    shapes += [(2, 32, 128)] * 2
    result = lists + [v(shape, F32) for shape in shapes]
    maps = [(2, 896, 128), (128, 1280), (512, 128), (128, 512), (2, 128, 256), (2, 256, 128)]
    result += [v(shape, BF16) for shape in maps + [(128, 1024)]]
    dma = pltpu.SemaphoreType.DMA
    result += [dma((9,))] + [dma((8,))] * 2 + [dma((3,))] * 4 + [dma((1,))] * 4 + [dma((2,))] * 2
    return result + [dma((1,))] * 4


def on_device(
    coarse_source,
    coarse_coefficient,
    coarse_start,
    fine_source,
    fine_coefficient,
    fine_start,
    fine_position,
    first_colour,
):
    vmem = pl.BlockSpec(memory_space=pltpu.VMEM)
    hbm = pl.BlockSpec(memory_space=pltpu.HBM)
    both = pl.pallas_call(
        kernel,
        out_shape=jax.ShapeDtypeStruct((2, 32, 1024), F32),
        in_specs=[hbm] * 8,
        out_specs=vmem,
        scratch_shapes=scratch(),
        compiler_params=pltpu.CompilerParams(
            collective_id=0, has_side_effects=True, vmem_limit_bytes=48 << 20
        ),
    )(
        *[
            pltpu.with_memory_space_constraint(array, pltpu.HBM)
            for array in (
                fine_position,
                first_colour,
                coarse_source,
                coarse_coefficient,
                coarse_start,
                fine_source,
                fine_coefficient,
                fine_start,
            )
        ],
    )
    return both[0], both[1:]


def solution(mesh):
    placed = (
        P("gx", "gy"),
        P("gx", "gy"),
        P("gx", "gy"),
        P(("gx", "gy"), None, None),
        P(("gx", "gy"), None, None),
        P(("gx", "gy"), None, None),
        P(),
        P(),
    )
    return jax.shard_map(
        on_device,
        mesh=mesh,
        in_specs=placed,
        out_specs=(P("gx", "gy"), P(("gx", "gy"), None, None)),
        check_vma=False,
    )
```
